32 devices in a mesh: fsdp: 8 (over z, y), tp: 4 (over x, core).
Axes of the slice: x: 2, y: 2, z: 4, core: 2. Of those that a mesh axis runs over, the one named last changes fastest.
Arguments:
- tokens: bfloat16 [8192, 2048], P(('fsdp', 'tp')), may hold values from -6 to 6
- cotangent: bfloat16 [8192, 2048], P(('fsdp', 'tp')), may hold values from -6 to 6
- segments: int32 [8192], P('fsdp'), may hold values from 0 to 2, as said below
- routes: int32 [8192, 8], P('fsdp'), may hold values from 0 to 15, all different within a row; in each aligned block of 1024 rows (0 to 1023, 1024 to 2047, ...) at most 576 rows name the same one
- gate_logits: float32 [8192, 8], P('fsdp'), may hold values from -3 to 3
- attention_gain: float32 [2048], replicated, may hold values from 0.5 to 1.5
- feedforward_gain: float32 [2048], replicated, may hold values from 0.5 to 1.5
- query_gain: float32 [128], replicated, may hold values from 0.5 to 1.5
- key_gain: float32 [128], replicated, may hold values from 0.5 to 1.5
- query_weight: bfloat16 [2048, 4096], P('fsdp', 'tp'), may hold values from -0.125 to 0.125
- key_weight: bfloat16 [2048, 512], P('fsdp', 'tp'), may hold values from -0.125 to 0.125
- value_weight: bfloat16 [2048, 512], P('fsdp', 'tp'), may hold values from -0.125 to 0.125
- out_weight: bfloat16 [2048, 4096], P('fsdp', 'tp'), may hold values from -1 to 1
- gate_weight: bfloat16 [2048, 16, 768], P('fsdp', None, 'tp'), may hold values from -0.125 to 0.125
- up_weight: bfloat16 [2048, 16, 768], P('fsdp', None, 'tp'), may hold values from -0.125 to 0.125
- down_weight: bfloat16 [2048, 16, 768], P('fsdp', None, 'tp'), may hold values from -0.875 to 0.875
Outputs:
- output: bfloat16 [8192, 2048], P(('fsdp', 'tp'))
- tokens_grad: float32 [8192, 2048], P(('fsdp', 'tp'))
- attention_gain_grad: float32 [2048], replicated
- feedforward_gain_grad: float32 [2048], replicated
- query_gain_grad: float32 [128], replicated
- key_gain_grad: float32 [128], replicated
- query_weight_grad: float32 [2048, 4096], P('fsdp', 'tp')
- key_weight_grad: float32 [2048, 512], P('fsdp', 'tp')
- value_weight_grad: float32 [2048, 512], P('fsdp', 'tp')
- out_weight_grad: float32 [2048, 4096], P('fsdp', 'tp')
- gate_weight_grad: float32 [2048, 16, 768], P('fsdp', None, 'tp')
- up_weight_grad: float32 [2048, 16, 768], P('fsdp', None, 'tp')
- down_weight_grad: float32 [2048, 16, 768], P('fsdp', None, 'tp')
The draws below stay inside these ranges and needn't reach their ends.
Inputs may be any that keep to these rules, and one draw needn't show every extreme that they name: `segments`: in each block of 1024 positions the ids never fall: id 0 covers fewer than 128 first positions, id 1 more than three quarters of the block, id 2 the remaining positions; each id is present in every block. `routes`: each row names 8 different experts. In each aligned block of 1024 rows (one block of tokens) no expert is named by more than 576 rows, a bound that some block reaches.
All inputs are finite; a program needn't handle non-finite values.
Results may differ from the reference program's by a relative error of at most 0.019.
Values may be sent and summed in bfloat16 or wider, within the bound.
No kernel may reach another device: no remote copies, remote signals or barrier semaphores. Data moves between devices by JAX's collectives and lax.ppermute only.
A program may use at most 192 MiB of HBM per device.

```python
import math
import jax
import jax.numpy as jnp
import numpy as np
from jax import lax

D = 2048
HQ = 32
HK = 4
HD = 128
FF = 768
TOPK = 8
EXPERTS = 16
SEQ = 1024
CAP = 576
TOKENS = 8192


def draw_segments(key, part):
    key = jax.random.fold_in(key, 11)
    early_key, late_key = jax.random.split(key)
    block_count = TOKENS // SEQ
    early_cut = jax.random.randint(early_key, (block_count, 1), 1, max(SEQ // 8, 2), dtype=jnp.int32)
    late_cut = jax.random.randint(late_key, (block_count, 1), SEQ - SEQ // 8 + 1, SEQ, dtype=jnp.int32)
    positions = jnp.arange(SEQ, dtype=jnp.int32)[None, :]
    doc_ids = (positions >= early_cut).astype(jnp.int32) + (positions >= late_cut).astype(jnp.int32)
    return doc_ids.reshape(TOKENS)


def steps_of(key, dims, cuts, least, largest):
    loudness = 1.0
    for axis_at, blocks in cuts:
        heights = jax.random.uniform(jax.random.fold_in(jax.random.fold_in(key, 6), axis_at), (blocks,), jnp.float32, least / len(cuts), largest / len(cuts))
        loudness = loudness * jnp.repeat(jnp.exp(heights), dims[axis_at] // blocks).reshape((-1,) + (1,) * (len(dims) - 1 - axis_at))
    return loudness


def assign_block(own_key, own, number, rows, number_of, top, bound, lean):
    order = jax.random.permutation(own_key, number_of)
    heavy_load, usual = portions_of(number_of, rows * top, bound, lean, True), portions_of(number_of, rows * top, bound, lean, False)
    places = jnp.arange(number_of)

    def named(lengths, offset_by):
        used = int((lengths > 0).sum())
        fixed = max(1, used // 4)
        moved = fixed + (places - fixed + offset_by * (used - fixed)) % max(1, number_of - fixed)
        return jnp.zeros((number_of,), jnp.int32).at[order[jnp.where(places < fixed, places, moved)]].set(jnp.asarray(lengths, jnp.int32))

    lengths = jnp.where(number % 4 == 0, named(heavy_load, number // 4), named(usual, number - number // 4 - 1))
    mixed = jax.random.permutation(jax.random.fold_in(own, 3), number_of)
    source_of, sink = mixed[0:number_of // 2 * 2:2], mixed[1:number_of // 2 * 2:2]
    room = jnp.minimum(lengths[source_of] - 1, bound - lengths[sink]) // 2
    room = jnp.where((source_of == order[0]) | (sink == order[0]) | (lengths[sink] == 0), 0, jnp.maximum(room, 0))
    moved = jax.random.randint(jax.random.fold_in(own, 4), (number_of // 2,), 0, 1 << 20) % (room + 1)
    lengths = lengths.at[source_of].add(-moved).at[sink].add(moved)
    items = jnp.searchsorted(jnp.cumsum(lengths), jnp.arange(rows * top), side="right").astype(jnp.int32)
    listing = items.reshape(top, rows).T
    listing = listing[jax.random.permutation(jax.random.fold_in(own, 1), rows)]
    offset_by = jax.random.randint(jax.random.fold_in(own, 2), (rows, 1), 0, top)
    return jnp.take_along_axis(listing, (jnp.arange(top)[None, :] + offset_by) % top, axis=1)


def portions_of(count, total, bound, slope, full):
    weights = [(1 << 20) // math.isqrt(rank ** slope) + 1 for rank in range(1, count + 1)]
    largest = bound if full else min(bound, max(-(-total // count), total * weights[0] // sum(weights)))
    least = 1 if total - largest >= count - 1 else 0
    counts, rest = [largest] + [least] * (count - 1), total - largest - least * (count - 1)
    while rest > 0:
        free = [i for i in range(1, count) if counts[i] < largest] or [i for i in range(1, count) if counts[i] < bound]
        whole, left = sum([weights[i] for i in free]), rest
        for i in free:
            extra = min(bound - counts[i], max(1, left * weights[i] // whole), rest)
            counts[i] = counts[i] + extra
            rest = rest - extra
    return np.array(counts)


def noise(own_key, shape, deviation, reach, shards=(), kind=jnp.bfloat16):
    level = steps_of(own_key, shape, shards, -0.22, 0.18) if shards else 1.0
    entries = jax.random.normal(own_key, shape, jnp.float32) * deviation * level
    return jnp.minimum(jnp.maximum(entries, -reach), reach).astype(kind)


def setup_inputs(seed: int = 0) -> dict:
    key_of = jax.random.split(jax.random.key(seed), 17)
    tokens = noise(key_of[0], (TOKENS, D), 1.0, 6.0, ((0, 32),))
    cotangent = noise(key_of[1], (TOKENS, D), 1.0, 6.0, ((0, 32),))
    segments = draw_segments(jax.random.fold_in(key_of[16], 71), 0)
    routes_keys = jax.random.split(jax.random.fold_in(key_of[3], 1), TOKENS // SEQ)
    routes_turns = jax.random.permutation(jax.random.fold_in(key_of[3], 3), TOKENS // SEQ)
    routes = jax.vmap(lambda own, number: assign_block(jax.random.fold_in(key_of[3], 2), own, number, SEQ, EXPERTS, TOPK, CAP, 1))(routes_keys, routes_turns).reshape((TOKENS, TOPK))
    gate_logits = noise(key_of[4], (TOKENS, TOPK), 0.5, 3.0, ((0, 8),), jnp.float32)
    attention_gain = jnp.clip(1.0 + 0.1 * jax.random.normal(key_of[5], (D,), jnp.float32), 0.5, 1.5)
    feedforward_gain = jnp.clip(1.0 + 0.1 * jax.random.normal(key_of[6], (D,), jnp.float32), 0.5, 1.5)
    query_gain = jnp.clip(1.0 + 0.1 * jax.random.normal(key_of[7], (HD,), jnp.float32), 0.5, 1.5)
    key_gain = jnp.clip(1.0 + 0.1 * jax.random.normal(key_of[8], (HD,), jnp.float32), 0.5, 1.5)
    query_weight = noise(key_of[9], (D, HQ * HD), D ** -0.5, 0.125, ((0, 8), (1, 4)))
    key_weight = noise(key_of[10], (D, HK * HD), D ** -0.5, 0.125, ((0, 8), (1, 4)))
    value_weight = noise(key_of[11], (D, HK * HD), D ** -0.5, 0.125, ((0, 8), (1, 4)))
    out_weight = noise(key_of[12], (D, HQ * HD), (HQ * HD // 128) ** -0.5, 1.0, ((0, 8), (1, 4)))
    gate_weight = noise(key_of[13], (D, EXPERTS, FF), D ** -0.5, 0.125, ((0, 8), (2, 4)))
    up_weight = noise(key_of[14], (D, EXPERTS, FF), D ** -0.5, 0.125, ((0, 8), (2, 4)))
    down_weight = noise(key_of[15], (D, EXPERTS, FF), (FF // 16) ** -0.5, 0.875, ((0, 8), (2, 4)))
    return {"tokens": tokens, "cotangent": cotangent, "segments": segments, "routes": routes, "gate_logits": gate_logits, "attention_gain": attention_gain, "feedforward_gain": feedforward_gain, "query_gain": query_gain, "key_gain": key_gain, "query_weight": query_weight, "key_weight": key_weight, "value_weight": value_weight, "out_weight": out_weight, "gate_weight": gate_weight, "up_weight": up_weight, "down_weight": down_weight}


@jax.custom_vjp
def low(v):
    return lax.optimization_barrier(v.astype(jnp.bfloat16)).astype(jnp.float32)

@jax.custom_vjp
def low_back(v):
    return v

def low_keep(v):
    return (low(v), None)

def low_pass(kept, grad):
    return (grad,)

def back_keep(v):
    return (v, None)

def back_low(kept, grad):
    return (low(grad),)
low.defvjp(low_keep, low_pass)
low_back.defvjp(back_keep, back_low)
eps_norm = 1e-06
rope_base = 1000000.0
highest = lax.Precision.HIGHEST

def product(left_side, right_side):
    return jnp.dot(left_side, right_side, precision=highest)

def norm_rows(values, scale_gain):
    inverse = lax.rsqrt(lax.optimization_barrier(jnp.mean(values * values, axis=-1, keepdims=True)) + eps_norm)
    return values * inverse * scale_gain

def rope_tables(row_count, head_size):
    positions = jnp.arange(row_count, dtype=jnp.float32)
    frequencies = rope_base ** (-jnp.arange(0, head_size, 2, dtype=jnp.float32) / head_size)
    angles = positions[:, None] * frequencies[None, :]
    angles = jnp.concatenate([angles, angles], axis=-1)
    return (jnp.cos(angles), jnp.sin(angles))

def rotate(values, cosine, sine_table):
    half_size = values.shape[-1] // 2
    turned = jnp.concatenate([-values[..., half_size:], values[..., :half_size]], axis=-1)
    return values * cosine[:, None, :] + turned * sine_table[:, None, :]

def attention(queries, key_heads, value_heads, segment_ids):
    block_rows = min(512, SEQ)
    block_count = SEQ // block_rows
    group_size = HQ // HK
    grouped = queries.reshape(block_count, block_rows, HK, group_size, HD)
    positions = jnp.arange(SEQ, dtype=jnp.int32)
    query_places = positions.reshape(block_count, block_rows)
    query_ids = segment_ids.reshape(block_count, block_rows)

    def one_block(block_item):
        query_block, query_place, query_id = block_item
        scores = jnp.einsum('qagd,kad->agqk', query_block, key_heads, precision=highest) * HD ** (-0.5)
        scores = low_back(scores)
        allowed = (positions[None, :] <= query_place[:, None]) & (segment_ids[None, :] == query_id[:, None])
        scores = jnp.where(allowed[None, None], scores, -jnp.inf)
        row_max = lax.optimization_barrier(jnp.max(scores, axis=-1, keepdims=True))
        weights = jnp.exp(scores - row_max)
        weights = low(weights / lax.optimization_barrier(jnp.sum(weights, axis=-1, keepdims=True)))
        return jnp.einsum('agqk,kad->qagd', weights, value_heads, precision=highest)
    result = lax.map(jax.checkpoint(one_block), (grouped, query_places, query_ids))
    return result.reshape(SEQ, HQ * HD)

def experts(normed, route_rows, gate_probs, gate_weight, up_weight, down_weight):
    pair_count = SEQ * TOPK
    routes_flat = route_rows.reshape(pair_count).astype(jnp.int32)
    members = (routes_flat[:, None] == jnp.arange(EXPERTS, dtype=jnp.int32)[None, :]).astype(jnp.int32)
    slot_of = lax.optimization_barrier(jnp.sum((jnp.cumsum(members, axis=0, dtype=jnp.int32) - 1) * members, axis=1, dtype=jnp.int32))
    place_of = (routes_flat * CAP + slot_of).astype(jnp.int32)
    owners = (jnp.arange(pair_count, dtype=jnp.int32) // TOPK).astype(jnp.int32)
    slot_table = jnp.full((EXPERTS * CAP,), SEQ, jnp.int32).at[place_of].set(owners)
    shares = jnp.zeros((EXPERTS * CAP,), jnp.float32).at[place_of].set(gate_probs.reshape(pair_count))
    padded = jnp.concatenate([normed, jnp.zeros((1, D), jnp.float32)], axis=0)
    taken_rows = padded[slot_table].reshape(EXPERTS, CAP, D)
    gate_pre = low_back(jnp.einsum('ecd,def->ecf', taken_rows, gate_weight, precision=highest))
    up_pre = low_back(jnp.einsum('ecd,def->ecf', taken_rows, up_weight, precision=highest))
    hidden = low(jax.nn.silu(gate_pre) * up_pre)
    result = low_back(jnp.einsum('ecf,def->ecd', hidden, down_weight, precision=highest))
    weighted = result.reshape(EXPERTS * CAP, D) * shares[:, None]
    summed = jnp.zeros((SEQ + 1, D), jnp.float32).at[slot_table].add(weighted)
    return summed[:SEQ]

def layer_block(weights, token_rows, route_rows, logit_rows, segment_ids):
    attention_gain, feedforward_gain, query_gain, key_gain, query_weight, key_weight, value_weight, out_weight, gate_weight, up_weight, down_weight = weights
    cosine, sine_table = rope_tables(SEQ, HD)
    first_norm = low(norm_rows(token_rows, attention_gain))
    queries = low_back(product(first_norm, query_weight)).reshape(SEQ, HQ, HD)
    key_heads = low_back(product(first_norm, key_weight)).reshape(SEQ, HK, HD)
    value_heads = low(low_back(product(first_norm, value_weight))).reshape(SEQ, HK, HD)
    queries = low(rotate(norm_rows(queries, query_gain), cosine, sine_table))
    key_heads = low(rotate(norm_rows(key_heads, key_gain), cosine, sine_table))
    heads = low(low_back(attention(queries, key_heads, value_heads, segment_ids)))
    middle = token_rows + low_back(product(heads, out_weight.T))
    second_norm = low(norm_rows(middle, feedforward_gain))
    gate_probs = jax.nn.softmax(logit_rows, axis=-1)
    moe = low_back(experts(second_norm, route_rows, gate_probs, gate_weight, up_weight, down_weight))
    return middle + moe

def reference(tokens, cotangent, segments, routes, gate_logits, attention_gain, feedforward_gain, query_gain, key_gain, query_weight, key_weight, value_weight, out_weight, gate_weight, up_weight, down_weight):
    block_count = TOKENS // SEQ
    weights = (attention_gain.astype(jnp.float32), feedforward_gain.astype(jnp.float32), query_gain.astype(jnp.float32), key_gain.astype(jnp.float32), query_weight.astype(jnp.float32), key_weight.astype(jnp.float32), value_weight.astype(jnp.float32), out_weight.astype(jnp.float32), gate_weight.astype(jnp.float32), up_weight.astype(jnp.float32), down_weight.astype(jnp.float32))
    blocks = (routes.reshape(block_count, SEQ, TOPK), gate_logits.astype(jnp.float32).reshape(block_count, SEQ, TOPK), segments.reshape(block_count, SEQ))

    def whole_layer(token_rows, layer_weights):

        def block_step(running, block_item):
            rows_in, route_rows, logit_rows, segment_ids = block_item
            return (running, jax.checkpoint(layer_block)(layer_weights, rows_in, route_rows, logit_rows, segment_ids))
        items = (token_rows.reshape(block_count, SEQ, D),) + blocks
        running, outputs = lax.scan(block_step, jnp.zeros((), jnp.float32), items)
        return outputs.reshape(TOKENS, D)
    output, pullback = jax.vjp(whole_layer, tokens.astype(jnp.float32), weights)
    tokens_grad, weight_grads = pullback(cotangent.astype(jnp.float32))
    return (output.astype(jnp.bfloat16), tokens_grad, weight_grads[0], weight_grads[1], weight_grads[2], weight_grads[3], weight_grads[4], weight_grads[5], weight_grads[6], weight_grads[7], weight_grads[8], weight_grads[9], weight_grads[10])
```

```python
from functools import partial

import jax
import jax.numpy as jnp
from jax import lax
from jax.sharding import PartitionSpec as P

SEQ = 1024
PARTS = 4


eps_norm = 1e-06
rope_base = 1000000.0


def matmul(left_side, right_side):
    return jnp.dot(left_side, right_side, preferred_element_type=jnp.float32)


def times_transposed(left_side, right_side):
    return lax.dot_general(
        left_side, right_side, (((1,), (1,)), ((), ())), preferred_element_type=jnp.float32
    )


def inner_rows(left_side, right_side):
    return lax.dot_general(
        left_side, right_side, (((0,), (0,)), ((), ())), preferred_element_type=jnp.float32
    )


def norm_rows(values, scale_gain):
    inverse = lax.rsqrt(jnp.mean(values * values, axis=-1, keepdims=True) + eps_norm)
    return (values * inverse * scale_gain, inverse)


def norm_back(values, inverse, scale_gain, incoming):
    normed = values * inverse
    scaled_grad = incoming * scale_gain
    gain_grad = jnp.sum(incoming * normed, axis=tuple(range(values.ndim - 1)))
    result = inverse * (
        scaled_grad - normed * jnp.mean(scaled_grad * normed, axis=-1, keepdims=True)
    )
    return (result, gain_grad)


def rope_tables(row_count, head_size):
    positions = jnp.arange(row_count, dtype=jnp.float32)
    frequencies = rope_base ** (-jnp.arange(0, head_size, 2, dtype=jnp.float32) / head_size)
    angles = positions[:, None] * frequencies[None, :]
    angles = jnp.concatenate([angles, angles], axis=-1)
    return (jnp.cos(angles), jnp.sin(angles))


def rotate(values, cosine, sine_table):
    half_size = values.shape[-1] // 2
    turned = jnp.concatenate([-values[..., half_size:], values[..., :half_size]], axis=-1)
    return values * cosine[:, None, :] + turned * sine_table[:, None, :]


def rotate_back(incoming, cosine, sine_table):
    half_size = incoming.shape[-1] // 2
    shifted = incoming * sine_table[:, None, :]
    turned = jnp.concatenate([shifted[..., half_size:], -shifted[..., :half_size]], axis=-1)
    return incoming * cosine[:, None, :] + turned


def block_mask(segment_ids, offset, finish):
    positions = jnp.arange(finish, dtype=jnp.int32)
    earlier = positions[None, :] <= positions[offset:finish, None]
    same_doc = segment_ids[None, :finish] == segment_ids[offset:finish, None]
    return earlier & same_doc


def attend(queries, key_heads, value_heads, segment_ids, group_size):
    seq_rows, head_count, head_size = queries.shape
    block_rows = min(512, seq_rows)
    scaling = head_size ** (-0.5)
    head_ids = jnp.arange(head_count, dtype=jnp.int32)
    outputs = []
    logsums = []
    for offset in range(0, seq_rows, block_rows):
        finish = offset + block_rows
        allowed = block_mask(segment_ids, offset, finish)

        def one_head(head_index):
            query_block = lax.dynamic_index_in_dim(queries[offset:finish], head_index, 1, False)
            key_block = lax.dynamic_index_in_dim(
                key_heads[:finish], head_index // group_size, 1, False
            )
            value_block = lax.dynamic_index_in_dim(
                value_heads[:finish], head_index // group_size, 1, False
            )
            scores = jnp.where(
                allowed, times_transposed(query_block, key_block) * scaling, -jnp.inf
            )
            row_max = jnp.max(scores, axis=-1, keepdims=True)
            weights = jnp.exp(scores - row_max)
            row_total = jnp.sum(weights, axis=-1, keepdims=True)
            probs_low = (weights / row_total).astype(jnp.bfloat16)
            return (matmul(probs_low, value_block), (row_max + jnp.log(row_total))[:, 0])

        result, row_logsum = lax.map(one_head, head_ids)
        outputs.append(jnp.moveaxis(result, 0, 1))
        logsums.append(row_logsum)
    return (jnp.concatenate(outputs, axis=0), jnp.concatenate(logsums, axis=1))


def attend_back(queries, key_heads, value_heads, segment_ids, logsums, head_grads, group_size):
    seq_rows, head_count, head_size = queries.shape
    block_rows = min(512, seq_rows)
    scaling = head_size ** (-0.5)
    head_ids = jnp.arange(head_count, dtype=jnp.int32)
    key_acc = jnp.zeros(key_heads.shape, jnp.float32)
    value_acc = jnp.zeros(value_heads.shape, jnp.float32)
    query_parts = []
    for offset in range(0, seq_rows, block_rows):
        finish = offset + block_rows
        allowed = block_mask(segment_ids, offset, finish)

        def head_step(running, head_index):
            key_sum, value_sum = running
            kv_index = head_index // group_size
            query_block = lax.dynamic_index_in_dim(queries[offset:finish], head_index, 1, False)
            key_block = lax.dynamic_index_in_dim(key_heads[:finish], kv_index, 1, False)
            value_block = lax.dynamic_index_in_dim(value_heads[:finish], kv_index, 1, False)
            grad_block = lax.dynamic_index_in_dim(head_grads[offset:finish], head_index, 1, False)
            row_logsum = lax.dynamic_index_in_dim(logsums[:, offset:finish], head_index, 0, False)
            scores = jnp.where(
                allowed, times_transposed(query_block, key_block) * scaling, -jnp.inf
            )
            probs = jnp.exp(scores - row_logsum[:, None])
            prob_grads = times_transposed(grad_block, value_block)
            score_grads = (
                probs * (prob_grads - jnp.sum(probs * prob_grads, axis=-1, keepdims=True))
            ).astype(jnp.bfloat16)
            query_grad = matmul(score_grads, key_block) * scaling
            key_sum = key_sum.at[:finish, kv_index].add(
                inner_rows(score_grads, query_block) * scaling
            )
            value_sum = value_sum.at[:finish, kv_index].add(
                inner_rows(probs.astype(jnp.bfloat16), grad_block)
            )
            return ((key_sum, value_sum), query_grad)

        (key_acc, value_acc), query_piece = lax.scan(head_step, (key_acc, value_acc), head_ids)
        query_parts.append(jnp.moveaxis(query_piece, 0, 1))
    return (jnp.concatenate(query_parts, axis=0), key_acc, value_acc)


def joined(own, other, bit):
    first_half = jnp.where(bit == 0, own, other)
    last_half = jnp.where(bit == 0, other, own)
    return jnp.concatenate([first_half, last_half], axis=0)


def halves(values, bit):
    rows = values.shape[0] // 2
    kept = lax.dynamic_slice_in_dim(values, bit * rows, rows, 0)
    sent = lax.dynamic_slice_in_dim(values, (1 - bit) * rows, rows, 0)
    return (kept, sent)


def make_moves(fsdp_size, tp_size):
    swap_core = [(i, i ^ 1) for i in range(tp_size)]
    swap_chip = [(i, (i + 2) % tp_size) for i in range(tp_size)]
    swap_pair = [(i, i ^ 1) for i in range(fsdp_size)]
    columns = [list(range(b, fsdp_size, 2)) for b in range(2)]

    def tp_gather(own):
        place = lax.axis_index("tp")
        rows, width = own.shape
        both = joined(own, lax.ppermute(own, "tp", swap_chip), place // 2)
        others = lax.ppermute(both, "tp", swap_core)
        both = both.reshape(2, 1, rows, width)
        others = others.reshape(2, 1, rows, width)
        first_core = jnp.where(place % 2 == 0, both, others)
        last_core = jnp.where(place % 2 == 0, others, both)
        return jnp.concatenate([first_core, last_core], axis=1).reshape(4 * rows, width)

    def tp_scatter(full):
        place = lax.axis_index("tp")
        rows, width = full.shape[0] // 4, full.shape[1]
        split = full.reshape(2, 2, rows, width)
        kept = lax.dynamic_index_in_dim(split, place % 2, 1, False)
        sent = lax.dynamic_index_in_dim(split, 1 - place % 2, 1, False).astype(jnp.bfloat16)
        pair = kept.astype(jnp.float32) + lax.ppermute(sent, "tp", swap_core).astype(jnp.float32)
        kept, sent = halves(pair, place // 2)
        received = lax.ppermute(sent.astype(jnp.bfloat16), "tp", swap_chip)
        return (kept + received.astype(jnp.float32)).reshape(rows, width)

    def pair_swap(values):
        return lax.ppermute(values, "fsdp", swap_pair)

    def column_gather(own):
        return lax.all_gather(own, "fsdp", axis=0, tiled=True, axis_index_groups=columns)

    def column_scatter(full):
        return lax.psum_scatter(
            full, "fsdp", scatter_dimension=0, tiled=True, axis_index_groups=columns
        )

    return (tp_gather, tp_scatter, pair_swap, column_gather, column_scatter)


def per_device(
    fsdp_size,
    tp_size,
    tokens,
    cotangent,
    segments,
    routes,
    gate_logits,
    attention_gain,
    feedforward_gain,
    query_gain,
    key_gain,
    query_weight,
    key_weight,
    value_weight,
    out_weight,
    gate_weight,
    up_weight,
    down_weight,
):
    tp_gather, tp_scatter, pair_swap, column_gather, column_scatter = make_moves(
        fsdp_size, tp_size
    )
    pair_bit = lax.axis_index("fsdp") % 2
    head_size = query_gain.shape[0]
    kv_count = key_weight.shape[1] // head_size
    query_count = query_weight.shape[1] // head_size
    group_size = query_count // kv_count
    model_width = tokens.shape[1]
    own_rows = tokens.shape[0]
    weight_rows, expert_count, expert_width = gate_weight.shape
    half_experts = expert_count // 2
    half_width = half_experts * expert_width
    part_width = half_width // PARTS
    rows_all = segments.shape[0]
    block_count = rows_all // SEQ
    cosine_block, sine_block = rope_tables(SEQ, head_size)
    cosine = jnp.tile(cosine_block, (block_count, 1))
    sine_table = jnp.tile(sine_block, (block_count, 1))
    token_rows = tokens.astype(jnp.float32)
    first_norm, first_inverse = norm_rows(token_rows, attention_gain)
    first_full = tp_gather(first_norm.astype(jnp.bfloat16))
    query_key_value = lax.all_gather(
        jnp.concatenate([query_weight, key_weight, value_weight], axis=1),
        "fsdp",
        axis=0,
        tiled=True,
    )
    full_out = lax.all_gather(out_weight, "fsdp", axis=0, tiled=True)
    query_width = query_count * head_size
    key_width = kv_count * head_size

    def flat(weight):
        return weight.reshape(weight_rows, 2, PARTS, part_width)

    flats = (flat(gate_weight), flat(up_weight), flat(down_weight))

    def fetch(part):
        def side(bit):
            return jnp.concatenate(
                [lax.dynamic_index_in_dim(w[:, :, part], bit, 1, False) for w in flats], axis=1
            )

        return column_gather(joined(side(pair_bit), pair_swap(side(1 - pair_bit)), pair_bit))

    expert_weights = [fetch(part) for part in range(PARTS)]

    projected = matmul(first_full, query_key_value)
    query_raw = projected[:, :query_width].reshape(rows_all, query_count, head_size)
    key_raw = projected[:, query_width : query_width + key_width].reshape(
        rows_all, kv_count, head_size
    )
    value_low = (
        projected[:, query_width + key_width :]
        .astype(jnp.bfloat16)
        .reshape(rows_all, kv_count, head_size)
    )
    query_normed, query_inverse = norm_rows(query_raw, query_gain)
    key_normed, key_inverse = norm_rows(key_raw, key_gain)
    query_low = rotate(query_normed, cosine, sine_table).astype(jnp.bfloat16)
    key_low = rotate(key_normed, cosine, sine_table).astype(jnp.bfloat16)
    piece_out, piece_logsum = attend(query_low, key_low, value_low, segments, group_size)
    heads_low = piece_out.reshape(rows_all, query_width).astype(jnp.bfloat16)
    attn_local = tp_scatter(times_transposed(heads_low, full_out))
    middle = token_rows + attn_local
    second_norm, second_inverse = norm_rows(middle, feedforward_gain)

    def group_gather(own):
        return tp_gather(joined(own, pair_swap(own), pair_bit))

    def group_scatter(full):
        kept, sent = halves(tp_scatter(full), pair_bit)
        return kept + pair_swap(sent.astype(jnp.bfloat16)).astype(jnp.float32)

    grad_group = group_gather(cotangent)
    second_group = group_gather(second_norm.astype(jnp.bfloat16))
    gate_probs = jax.nn.softmax(gate_logits, axis=-1)
    expert_ids = jnp.arange(expert_count, dtype=jnp.int32)
    share_own = jnp.sum(
        jnp.where(routes[:, :, None] == expert_ids[None, None, :], gate_probs[:, :, None], 0.0),
        axis=1,
    )
    share_other = pair_swap(share_own)
    share_own = share_own.reshape(tp_size, 1, own_rows, expert_count)
    share_other = share_other.reshape(tp_size, 1, own_rows, expert_count)
    share_group = jnp.concatenate(
        [
            jnp.where(pair_bit == 0, share_own, share_other),
            jnp.where(pair_bit == 0, share_other, share_own),
        ],
        axis=1,
    ).reshape(2 * rows_all, expert_count)
    share_half = lax.dynamic_slice_in_dim(share_group, pair_bit * half_experts, half_experts, 1)

    moe_sum = None
    second_sum = None
    owned_parts = []
    for part in range(PARTS):
        weights = expert_weights[part]
        weight_in = weights[:, : 2 * part_width]
        weight_down = weights[:, 2 * part_width :]
        step = half_experts // PARTS
        share = jnp.repeat(share_half[:, part * step : (part + 1) * step], expert_width, axis=1)
        both_pre = matmul(second_group, weight_in)
        gate_pre, up_pre = both_pre[:, :part_width], both_pre[:, part_width:]
        sigmoid_gate = jax.nn.sigmoid(gate_pre)
        silu_gate = gate_pre * sigmoid_gate
        hidden = (silu_gate * up_pre * share).astype(jnp.bfloat16)
        hidden_grad = matmul(grad_group, weight_down) * share
        up_grad = (hidden_grad * silu_gate).astype(jnp.bfloat16)
        gate_grad = (
            hidden_grad * up_pre * sigmoid_gate * (1.0 + gate_pre * (1.0 - sigmoid_gate))
        ).astype(jnp.bfloat16)
        both_grad = jnp.concatenate([gate_grad, up_grad], axis=1)
        moe_part = times_transposed(hidden, weight_down)
        second_part = times_transposed(both_grad, weight_in)
        moe_sum = moe_part if moe_sum is None else moe_sum + moe_part
        second_sum = second_part if second_sum is None else second_sum + second_part
        weight_term = jnp.concatenate(
            [
                inner_rows(second_group, both_grad).astype(jnp.bfloat16),
                inner_rows(grad_group, hidden).astype(jnp.bfloat16),
            ],
            axis=1,
        )
        kept, sent = halves(column_scatter(weight_term), pair_bit)
        owned_parts.append((kept, pair_swap(sent)))

    def owned(index):
        place = slice(index * part_width, (index + 1) * part_width)
        mine = jnp.concatenate([kept[:, place] for kept, sent in owned_parts], axis=1)
        theirs = jnp.concatenate([sent[:, place] for kept, sent in owned_parts], axis=1)
        return (
            jnp.concatenate(
                [
                    jnp.where(pair_bit == 0, mine, theirs),
                    jnp.where(pair_bit == 0, theirs, mine),
                ],
                axis=1,
            )
            .astype(jnp.float32)
            .reshape(weight_rows, expert_count, expert_width)
        )

    second_grad = group_scatter(second_sum)
    output = (middle + group_scatter(moe_sum)).astype(jnp.bfloat16)
    middle_back, feedforward_gain_grad = norm_back(
        middle, second_inverse, feedforward_gain, second_grad
    )
    middle_grad = cotangent.astype(jnp.float32) + middle_back
    attn_grad_full = tp_gather(middle_grad.astype(jnp.bfloat16))
    heads_grad = (
        matmul(attn_grad_full, full_out)
        .astype(jnp.bfloat16)
        .reshape(rows_all, query_count, head_size)
    )
    out_weight_grad = inner_rows(attn_grad_full, heads_low)
    piece_query, piece_key, piece_value = attend_back(
        query_low, key_low, value_low, segments, piece_logsum, heads_grad, group_size
    )
    value_low_grad = piece_value.astype(jnp.bfloat16).reshape(rows_all, key_width)
    query_back, query_gain_grad = norm_back(
        query_raw, query_inverse, query_gain, rotate_back(piece_query, cosine, sine_table)
    )
    key_back, key_gain_grad = norm_back(
        key_raw, key_inverse, key_gain, rotate_back(piece_key, cosine, sine_table)
    )
    projected_grad = jnp.concatenate(
        [
            query_back.astype(jnp.bfloat16).reshape(rows_all, query_width),
            key_back.astype(jnp.bfloat16).reshape(rows_all, key_width),
            value_low_grad,
        ],
        axis=1,
    )
    first_grad = tp_scatter(times_transposed(projected_grad, query_key_value))
    out_owned = lax.psum_scatter(
        out_weight_grad.astype(jnp.bfloat16), "fsdp", scatter_dimension=0, tiled=True
    ).astype(jnp.float32)
    projected_owned = lax.psum_scatter(
        inner_rows(first_full, projected_grad).astype(jnp.bfloat16),
        "fsdp",
        scatter_dimension=0,
        tiled=True,
    ).astype(jnp.float32)
    rows_back, attention_gain_grad = norm_back(
        token_rows, first_inverse, attention_gain, first_grad
    )
    tokens_grad = middle_grad + rows_back
    gain_sums = lax.psum(
        (attention_gain_grad, feedforward_gain_grad, query_gain_grad, key_gain_grad), ("fsdp", "tp")
    )
    return (
        output,
        tokens_grad,
        gain_sums[0],
        gain_sums[1],
        gain_sums[2],
        gain_sums[3],
        projected_owned[:, :query_width],
        projected_owned[:, query_width : query_width + key_width],
        projected_owned[:, query_width + key_width :],
        out_owned,
        owned(0),
        owned(1),
        owned(2),
    )


def solution(mesh):
    placed = (
        P(("fsdp", "tp"), None),
        P(("fsdp", "tp"), None),
        P("fsdp"),
        P("fsdp", None),
        P("fsdp", None),
        P(),
        P(),
        P(),
        P(),
        P("fsdp", "tp"),
        P("fsdp", "tp"),
        P("fsdp", "tp"),
        P("fsdp", "tp"),
        P("fsdp", None, "tp"),
        P("fsdp", None, "tp"),
        P("fsdp", None, "tp"),
    )
    return jax.shard_map(
        partial(per_device, mesh.shape["fsdp"], mesh.shape["tp"]),
        mesh=mesh,
        in_specs=placed,
        out_specs=(
            P(("fsdp", "tp"), None),
            P(("fsdp", "tp"), None),
            P(),
            P(),
            P(),
            P(),
            P("fsdp", "tp"),
            P("fsdp", "tp"),
            P("fsdp", "tp"),
            P("fsdp", "tp"),
            P("fsdp", None, "tp"),
            P("fsdp", None, "tp"),
            P("fsdp", None, "tp"),
        ),
        check_vma=False,
    )
```

```python
from functools import partial

import jax
import jax.numpy as jnp
from jax import lax
from jax.experimental import pallas as pl
from jax.experimental.pallas import tpu as pltpu
from jax.sharding import PartitionSpec as P

SEQ = 1024
TILE = 256
PARTS = 4
VMEM_BYTES = 48 * 1024 * 1024


eps_norm = 1e-06
rope_base = 1000000.0


def matmul(left_side, right_side):
    return jnp.dot(left_side, right_side, preferred_element_type=jnp.float32)


def times_transposed(left_side, right_side):
    return lax.dot_general(
        left_side, right_side, (((1,), (1,)), ((), ())), preferred_element_type=jnp.float32
    )


def inner_rows(left_side, right_side):
    return lax.dot_general(
        left_side, right_side, (((0,), (0,)), ((), ())), preferred_element_type=jnp.float32
    )


def norm_rows(values, scale_gain):
    inverse = lax.rsqrt(jnp.mean(values * values, axis=-1, keepdims=True) + eps_norm)
    return (values * inverse * scale_gain, inverse)


def norm_back(values, inverse, scale_gain, incoming):
    normed = values * inverse
    scaled_grad = incoming * scale_gain
    gain_grad = jnp.sum(incoming * normed, axis=tuple(range(values.ndim - 1)))
    result = inverse * (
        scaled_grad - normed * jnp.mean(scaled_grad * normed, axis=-1, keepdims=True)
    )
    return (result, gain_grad)


def rope_tables(row_count, head_size):
    positions = jnp.arange(row_count, dtype=jnp.float32)
    frequencies = rope_base ** (-jnp.arange(0, head_size, 2, dtype=jnp.float32) / head_size)
    angles = positions[:, None] * frequencies[None, :]
    angles = jnp.concatenate([angles, angles], axis=-1)
    return (jnp.cos(angles), jnp.sin(angles))


def head_norm(values):
    inverse = lax.rsqrt(jnp.mean(values * values, axis=-1, keepdims=True) + eps_norm)
    return (values * inverse, inverse)


def turn(values, cosine, signed_sine):
    half_size = values.shape[-1] // 2
    return values * cosine + pltpu.roll(values, half_size, 1) * signed_sine


def turn_back(incoming, cosine, signed_sine):
    half_size = incoming.shape[-1] // 2
    return incoming * cosine + pltpu.roll(incoming * signed_sine, half_size, 1)


def masked_probs(query_tile, key_rows, row_ids, column_ids, offset, scaling):
    scores = times_transposed(query_tile, key_rows) * scaling
    row_place = lax.broadcasted_iota(jnp.int32, scores.shape, 0) + offset
    column_place = lax.broadcasted_iota(jnp.int32, scores.shape, 1)
    allowed = (column_place <= row_place) & (row_ids == column_ids)
    scores = jnp.where(allowed, scores, -jnp.inf)
    weights = jnp.exp(scores - jnp.max(scores, axis=-1, keepdims=True))
    return weights * (1.0 / jnp.sum(weights, axis=-1, keepdims=True))


def attend_kernel(
    group_size,
    query_ref,
    key_ref,
    value_ref,
    cosine_ref,
    sine_ref,
    row_ids_ref,
    column_ids_ref,
    query_gain_ref,
    key_gain_ref,
    heads_ref,
    key_low,
    value_low,
):
    head_size = query_ref.shape[1]
    scaling = head_size ** (-0.5)

    @pl.when(lax.rem(pl.program_id(1), group_size) == 0)
    def prepare():
        normed, unused = head_norm(key_ref[...])
        key_low[...] = turn(normed * key_gain_ref[...], cosine_ref[...], sine_ref[...]).astype(
            jnp.bfloat16
        )
        value_low[...] = value_ref[...].astype(jnp.bfloat16)

    for offset in range(0, SEQ, TILE):
        finish = offset + TILE
        rows = pl.ds(offset, TILE)
        normed, unused = head_norm(query_ref[rows, :])
        query_tile = turn(
            normed * query_gain_ref[...], cosine_ref[rows, :], sine_ref[rows, :]
        ).astype(jnp.bfloat16)
        probs = masked_probs(
            query_tile,
            key_low[:finish, :],
            row_ids_ref[rows, :],
            column_ids_ref[:, :finish],
            offset,
            scaling,
        )
        heads_ref[rows, :] = matmul(probs.astype(jnp.bfloat16), value_low[:finish, :]).astype(
            jnp.bfloat16
        )


def attend_back_kernel(
    query_count,
    kv_count,
    query_ref,
    key_ref,
    value_ref,
    grad_ref,
    cosine_ref,
    sine_ref,
    row_ids_ref,
    column_ids_ref,
    query_gain_ref,
    key_gain_ref,
    projected_ref,
    query_gain_grad_ref,
    key_gain_grad_ref,
    key_low,
    value_low,
    key_sum,
    value_sum,
):
    head_size = query_ref.shape[1]
    scaling = head_size ** (-0.5)
    group_size = query_count // kv_count
    head = pl.program_id(1)
    place = lax.rem(head, group_size)

    @pl.when((pl.program_id(0) == 0) & (head == 0))
    def clear():
        query_gain_grad_ref[...] = jnp.zeros_like(query_gain_grad_ref)
        key_gain_grad_ref[...] = jnp.zeros_like(key_gain_grad_ref)

    @pl.when(place == 0)
    def prepare():
        normed, unused = head_norm(key_ref[...])
        key_low[...] = turn(normed * key_gain_ref[...], cosine_ref[...], sine_ref[...]).astype(
            jnp.bfloat16
        )
        value_low[...] = value_ref[...].astype(jnp.bfloat16)
        key_sum[...] = jnp.zeros_like(key_sum)
        value_sum[...] = jnp.zeros_like(value_sum)

    def through_norm(turned_grad, cosine, signed_sine, normed, inverse, gain):
        incoming = turn_back(turned_grad, cosine, signed_sine)
        scaled_grad = incoming * gain
        result = inverse * (
            scaled_grad - normed * jnp.mean(scaled_grad * normed, axis=-1, keepdims=True)
        )
        return (result, jnp.sum(incoming * normed, axis=0, keepdims=True))

    columns = pl.ds(pl.multiple_of(head * head_size, head_size), head_size)
    for offset in range(0, SEQ, TILE):
        finish = offset + TILE
        rows = pl.ds(offset, TILE)
        cosine, signed_sine = cosine_ref[rows, :], sine_ref[rows, :]
        normed, inverse = head_norm(query_ref[rows, :])
        query_tile = turn(normed * query_gain_ref[...], cosine, signed_sine).astype(jnp.bfloat16)
        grad_tile = grad_ref[rows, :]
        key_rows = key_low[:finish, :]
        probs = masked_probs(
            query_tile,
            key_rows,
            row_ids_ref[rows, :],
            column_ids_ref[:, :finish],
            offset,
            scaling,
        )
        prob_grad = times_transposed(grad_tile, value_low[:finish, :])
        score_grad = (
            probs * (prob_grad - jnp.sum(probs * prob_grad, axis=-1, keepdims=True))
        ).astype(jnp.bfloat16)
        value_sum[:finish, :] += inner_rows(probs.astype(jnp.bfloat16), grad_tile)
        key_sum[:finish, :] += inner_rows(score_grad, query_tile)
        result, gain_grad = through_norm(
            matmul(score_grad, key_rows) * scaling,
            cosine,
            signed_sine,
            normed,
            inverse,
            query_gain_ref[...],
        )
        projected_ref[rows, columns] = result.astype(jnp.bfloat16)
        query_gain_grad_ref[...] += gain_grad

    @pl.when(place == group_size - 1)
    def finish_group():
        group = lax.div(head, group_size)
        normed, inverse = head_norm(key_ref[...])
        result, gain_grad = through_norm(
            key_sum[...] * scaling,
            cosine_ref[...],
            sine_ref[...],
            normed,
            inverse,
            key_gain_ref[...],
        )
        key_columns = pl.ds(
            pl.multiple_of((query_count + group) * head_size, head_size), head_size
        )
        value_columns = pl.ds(
            pl.multiple_of((query_count + kv_count + group) * head_size, head_size), head_size
        )
        projected_ref[:, key_columns] = result.astype(jnp.bfloat16)
        projected_ref[:, value_columns] = value_sum[...].astype(jnp.bfloat16)
        key_gain_grad_ref[...] += gain_grad


def attention_specs(query_count, kv_count, head_size):
    group_size = query_count // kv_count
    block = (SEQ, head_size)
    fixed = lambda shape: pl.BlockSpec(shape, lambda s, h: (0, 0))
    operands = [
        pl.BlockSpec(block, lambda s, h: (s, h)),
        pl.BlockSpec(block, lambda s, h: (s, query_count + h // group_size)),
        pl.BlockSpec(block, lambda s, h: (s, query_count + kv_count + h // group_size)),
    ]
    tables = [
        fixed(block),
        fixed(block),
        pl.BlockSpec((SEQ, 1), lambda s, h: (s, 0)),
        pl.BlockSpec((1, SEQ), lambda s, h: (0, s)),
        fixed((1, head_size)),
        fixed((1, head_size)),
    ]
    return (operands, tables)


def attend(projected, tables, query_count, kv_count, head_size):
    rows = projected.shape[0]
    operands, table_specs = attention_specs(query_count, kv_count, head_size)
    pairs = rows * SEQ * query_count * 5 // 8
    return pl.pallas_call(
        partial(attend_kernel, query_count // kv_count),
        grid=(rows // SEQ, query_count),
        in_specs=operands + table_specs,
        out_specs=pl.BlockSpec((SEQ, head_size), lambda s, h: (s, h)),
        out_shape=jax.ShapeDtypeStruct((rows, query_count * head_size), jnp.bfloat16),
        scratch_shapes=[
            pltpu.VMEM((SEQ, head_size), jnp.bfloat16),
            pltpu.VMEM((SEQ, head_size), jnp.bfloat16),
        ],
        compiler_params=pltpu.CompilerParams(vmem_limit_bytes=VMEM_BYTES),
        cost_estimate=pl.CostEstimate(
            flops=4 * pairs * head_size,
            bytes_accessed=6 * rows * query_count * head_size,
            transcendentals=pairs,
        ),
        name="attend",
    )(projected, projected, projected, *tables)


def attend_back(projected, heads_grad, tables, query_count, kv_count, head_size):
    rows = projected.shape[0]
    width = projected.shape[1]
    operands, table_specs = attention_specs(query_count, kv_count, head_size)
    pairs = rows * SEQ * query_count * 5 // 8
    return pl.pallas_call(
        partial(attend_back_kernel, query_count, kv_count),
        grid=(rows // SEQ, query_count),
        in_specs=operands + [pl.BlockSpec((SEQ, head_size), lambda s, h: (s, h))] + table_specs,
        out_specs=[
            pl.BlockSpec((SEQ, width), lambda s, h: (s, 0)),
            pl.BlockSpec((1, head_size), lambda s, h: (0, 0)),
            pl.BlockSpec((1, head_size), lambda s, h: (0, 0)),
        ],
        out_shape=[
            jax.ShapeDtypeStruct((rows, width), jnp.bfloat16),
            jax.ShapeDtypeStruct((1, head_size), jnp.float32),
            jax.ShapeDtypeStruct((1, head_size), jnp.float32),
        ],
        scratch_shapes=[
            pltpu.VMEM((SEQ, head_size), jnp.bfloat16),
            pltpu.VMEM((SEQ, head_size), jnp.bfloat16),
            pltpu.VMEM((SEQ, head_size), jnp.float32),
            pltpu.VMEM((SEQ, head_size), jnp.float32),
        ],
        compiler_params=pltpu.CompilerParams(vmem_limit_bytes=VMEM_BYTES),
        cost_estimate=pl.CostEstimate(
            flops=10 * pairs * head_size,
            bytes_accessed=10 * rows * query_count * head_size,
            transcendentals=pairs,
        ),
        name="attend_back",
    )(projected, projected, projected, heads_grad, *tables)


def joined(own, other, bit):
    first_half = jnp.where(bit == 0, own, other)
    last_half = jnp.where(bit == 0, other, own)
    return jnp.concatenate([first_half, last_half], axis=0)


def halves(values, bit):
    rows = values.shape[0] // 2
    kept = lax.dynamic_slice_in_dim(values, bit * rows, rows, 0)
    sent = lax.dynamic_slice_in_dim(values, (1 - bit) * rows, rows, 0)
    return (kept, sent)


def make_moves(fsdp_size, tp_size):
    swap_core = [(i, i ^ 1) for i in range(tp_size)]
    swap_chip = [(i, (i + 2) % tp_size) for i in range(tp_size)]
    swap_pair = [(i, i ^ 1) for i in range(fsdp_size)]
    columns = [list(range(b, fsdp_size, 2)) for b in range(2)]

    def to_core(values):
        return lax.ppermute(values, "tp", swap_core)

    def to_chip(values):
        return lax.ppermute(values, "tp", swap_chip)

    def to_pair(values):
        return lax.ppermute(values, "fsdp", swap_pair)

    def tp_gather(own):
        place = lax.axis_index("tp")
        rows, width = own.shape
        both = joined(own, to_chip(own), place // 2)
        others = to_core(both)
        both = both.reshape(2, 1, rows, width)
        others = others.reshape(2, 1, rows, width)
        first_core = jnp.where(place % 2 == 0, both, others)
        last_core = jnp.where(place % 2 == 0, others, both)
        return jnp.concatenate([first_core, last_core], axis=1).reshape(4 * rows, width)

    def tp_scatter(full):
        place = lax.axis_index("tp")
        rows, width = full.shape[0] // 4, full.shape[1]
        split = full.reshape(2, 2, rows, width)
        kept = lax.dynamic_index_in_dim(split, place % 2, 1, False)
        sent = lax.dynamic_index_in_dim(split, 1 - place % 2, 1, False).astype(jnp.bfloat16)
        pair = kept.astype(jnp.float32) + to_core(sent).astype(jnp.float32)
        kept, sent = halves(pair, place // 2)
        received = to_chip(sent.astype(jnp.bfloat16))
        return (kept + received.astype(jnp.float32)).reshape(rows, width)

    def plane_gather(own):
        cut = own.shape[0] // 2
        across = to_chip(own)
        beside = to_pair(own)
        mine = jnp.concatenate(
            [own, across, beside, to_chip(beside[:cut]), to_pair(across[cut:])], axis=0
        )
        return jnp.concatenate([mine, to_core(mine)], axis=0)

    def plane_scatter(full):
        rows = full.shape[0] // 8
        cut = rows // 2
        low = jnp.bfloat16
        wide = jnp.float32
        mine = full[: 4 * rows] + to_core(full[4 * rows :].astype(low)).astype(wide)
        own, across, beside, far = [mine[i * rows : (i + 1) * rows] for i in range(4)]
        from_chip = to_chip(far[:cut].astype(low)).astype(wide)
        from_pair = to_pair(far[cut:].astype(low)).astype(wide)
        across = jnp.concatenate([across[:cut], across[cut:] + from_pair], axis=0)
        beside = jnp.concatenate([beside[:cut] + from_chip, beside[cut:]], axis=0)
        return own + to_chip(across.astype(low)).astype(wide) + to_pair(
            beside.astype(low)
        ).astype(wide)

    def plane_share(share):
        place = lax.axis_index("tp")
        rows, count = share.shape[0] // 4, share.shape[1]
        split = share.reshape(2, 2, rows, count)
        split = jnp.where(place // 2 == 0, split, split[::-1])
        split = jnp.where(place % 2 == 0, split, split[:, ::-1]).swapaxes(0, 1)
        return jnp.stack([split, to_pair(split)], axis=1).reshape(8 * rows, count)

    def column_gather(own):
        return lax.all_gather(own, "fsdp", axis=0, tiled=True, axis_index_groups=columns)

    def column_scatter(full):
        return lax.psum_scatter(
            full, "fsdp", scatter_dimension=0, tiled=True, axis_index_groups=columns
        )

    def weight_gather(own):
        pair_bit = lax.axis_index("fsdp") % 2
        rows, width = own.shape
        mine = column_gather(own)
        theirs = to_pair(mine)
        mine = mine.reshape(fsdp_size // 2, 1, rows, width)
        theirs = theirs.reshape(fsdp_size // 2, 1, rows, width)
        return jnp.concatenate(
            [jnp.where(pair_bit == 0, mine, theirs), jnp.where(pair_bit == 0, theirs, mine)],
            axis=1,
        ).reshape(fsdp_size * rows, width)

    def weight_scatter(full):
        pair_bit = lax.axis_index("fsdp") % 2
        rows, width = full.shape[0] // fsdp_size, full.shape[1]
        split = full.reshape(fsdp_size // 2, 2, rows, width)
        kept = lax.dynamic_index_in_dim(split, pair_bit, 1, False)
        sent = lax.dynamic_index_in_dim(split, 1 - pair_bit, 1, False).astype(jnp.bfloat16)
        summed = kept.astype(jnp.float32) + to_pair(sent).astype(jnp.float32)
        return column_scatter(
            summed.astype(jnp.bfloat16).reshape(fsdp_size // 2 * rows, width)
        ).astype(jnp.float32)

    def sum_all(values):
        for step in range(tp_size.bit_length() - 1):
            swap = [(i, i ^ (1 << step)) for i in range(tp_size)]
            values = values + lax.ppermute(values, "tp", swap)
        for step in range(fsdp_size.bit_length() - 1):
            swap = [(i, i ^ (1 << step)) for i in range(fsdp_size)]
            values = values + lax.ppermute(values, "fsdp", swap)
        return values

    return (
        to_pair,
        tp_gather,
        tp_scatter,
        plane_gather,
        plane_scatter,
        plane_share,
        column_gather,
        column_scatter,
        weight_gather,
        weight_scatter,
        sum_all,
    )


def per_device(
    fsdp_size,
    tp_size,
    tokens,
    cotangent,
    segments,
    routes,
    gate_logits,
    attention_gain,
    feedforward_gain,
    query_gain,
    key_gain,
    query_weight,
    key_weight,
    value_weight,
    out_weight,
    gate_weight,
    up_weight,
    down_weight,
):
    (
        to_pair,
        tp_gather,
        tp_scatter,
        plane_gather,
        plane_scatter,
        plane_share,
        column_gather,
        column_scatter,
        weight_gather,
        weight_scatter,
        sum_all,
    ) = make_moves(fsdp_size, tp_size)
    pair_bit = lax.axis_index("fsdp") % 2
    head_size = query_gain.shape[0]
    kv_count = key_weight.shape[1] // head_size
    query_count = query_weight.shape[1] // head_size
    weight_rows, expert_count, expert_width = gate_weight.shape
    half_experts = expert_count // 2
    half_width = half_experts * expert_width
    part_width = half_width // PARTS
    rows_all = segments.shape[0]
    cosine, sine_table = rope_tables(SEQ, head_size)
    turn_sign = jnp.where(jnp.arange(head_size) < head_size // 2, -1.0, 1.0)
    tables = (
        cosine,
        sine_table * turn_sign,
        segments.reshape(rows_all, 1),
        segments.reshape(1, rows_all),
        query_gain.reshape(1, head_size),
        key_gain.reshape(1, head_size),
    )
    token_rows = tokens.astype(jnp.float32)
    first_norm, first_inverse = norm_rows(token_rows, attention_gain)
    first_full = tp_gather(first_norm.astype(jnp.bfloat16))
    query_key_value = weight_gather(
        jnp.concatenate([query_weight, key_weight, value_weight], axis=1)
    )
    full_out = weight_gather(out_weight)
    model_width = tokens.shape[1]
    query_width = query_count * head_size
    key_width = kv_count * head_size

    def flat(weight):
        return weight.reshape(weight_rows, 2, PARTS, part_width)

    flats = (flat(gate_weight), flat(up_weight), flat(down_weight))

    def fetch(part):
        def side(bit):
            return jnp.concatenate(
                [lax.dynamic_index_in_dim(w[:, :, part], bit, 1, False) for w in flats], axis=1
            )

        return column_gather(joined(side(pair_bit), to_pair(side(1 - pair_bit)), pair_bit))

    expert_weights = [fetch(part) for part in range(PARTS)]

    grad_group = plane_gather(cotangent)
    projected = matmul(first_full, query_key_value)
    heads_low = attend(projected, tables, query_count, kv_count, head_size)
    heads_low, grad_group = lax.optimization_barrier((heads_low, grad_group))
    attn_local = tp_scatter(times_transposed(heads_low, full_out))
    middle = token_rows + attn_local
    second_norm, second_inverse = norm_rows(middle, feedforward_gain)

    second_group = plane_gather(second_norm.astype(jnp.bfloat16))
    gate_probs = jax.nn.softmax(gate_logits, axis=-1)
    expert_ids = jnp.arange(expert_count, dtype=jnp.int32)
    share_own = jnp.sum(
        jnp.where(routes[:, :, None] == expert_ids[None, None, :], gate_probs[:, :, None], 0.0),
        axis=1,
    )
    share_group = plane_share(share_own)
    share_half = lax.dynamic_slice_in_dim(share_group, pair_bit * half_experts, half_experts, 1)

    owned_parts = []
    for part in range(PARTS):
        weights = expert_weights[part]
        weight_in = weights[:, : 2 * part_width]
        weight_down = weights[:, 2 * part_width :]
        step = half_experts // PARTS
        share = jnp.repeat(share_half[:, part * step : (part + 1) * step], expert_width, axis=1)
        both_pre = matmul(second_group, weight_in)
        gate_pre, up_pre = both_pre[:, :part_width], both_pre[:, part_width:]
        sigmoid_gate = jax.nn.sigmoid(gate_pre)
        silu_gate = gate_pre * sigmoid_gate
        hidden = (silu_gate * up_pre * share).astype(jnp.bfloat16)
        hidden_grad = matmul(grad_group, weight_down) * share
        up_grad = (hidden_grad * silu_gate).astype(jnp.bfloat16)
        gate_grad = (
            hidden_grad * up_pre * sigmoid_gate * (1.0 + gate_pre * (1.0 - sigmoid_gate))
        ).astype(jnp.bfloat16)
        both_grad = jnp.concatenate([gate_grad, up_grad], axis=1)
        moe_part = times_transposed(hidden, weight_down)
        second_part = times_transposed(both_grad, weight_in)
        moe_sum = moe_part if part == 0 else moe_sum + moe_part
        second_sum = second_part if part == 0 else second_sum + second_part
        moe_sum, second_sum = lax.optimization_barrier((moe_sum, second_sum))
        weight_term = jnp.concatenate(
            [
                inner_rows(second_group, both_grad).astype(jnp.bfloat16),
                inner_rows(grad_group, hidden).astype(jnp.bfloat16),
            ],
            axis=1,
        )
        kept, sent = halves(column_scatter(weight_term), pair_bit)
        owned_parts.append((kept, to_pair(sent)))

    def owned(index):
        place = slice(index * part_width, (index + 1) * part_width)
        mine = jnp.concatenate([kept[:, place] for kept, sent in owned_parts], axis=1)
        theirs = jnp.concatenate([sent[:, place] for kept, sent in owned_parts], axis=1)
        return (
            jnp.concatenate(
                [
                    jnp.where(pair_bit == 0, mine, theirs),
                    jnp.where(pair_bit == 0, theirs, mine),
                ],
                axis=1,
            )
            .astype(jnp.float32)
            .reshape(weight_rows, expert_count, expert_width)
        )

    second_grad = plane_scatter(second_sum)
    moe_sum, second_grad = lax.optimization_barrier((moe_sum, second_grad))
    output = (middle + plane_scatter(moe_sum)).astype(jnp.bfloat16)
    middle_back, feedforward_gain_grad = norm_back(
        middle, second_inverse, feedforward_gain, second_grad
    )
    middle_grad = cotangent.astype(jnp.float32) + middle_back
    attn_grad_full = tp_gather(middle_grad.astype(jnp.bfloat16))
    heads_grad = matmul(attn_grad_full, full_out).astype(jnp.bfloat16)
    out_owned = weight_scatter(inner_rows(attn_grad_full, heads_low))
    projected_grad, query_gain_grad, key_gain_grad = attend_back(
        projected, heads_grad, tables, query_count, kv_count, head_size
    )
    projected_owned = weight_scatter(inner_rows(first_full, projected_grad))
    first_grad = tp_scatter(times_transposed(projected_grad, query_key_value))
    rows_back, attention_gain_grad = norm_back(
        token_rows, first_inverse, attention_gain, first_grad
    )
    tokens_grad = middle_grad + rows_back
    gain_sums = sum_all(
        jnp.concatenate(
            [
                attention_gain_grad,
                feedforward_gain_grad,
                query_gain_grad.reshape(head_size),
                key_gain_grad.reshape(head_size),
            ]
        )
    )
    gain_sums = jnp.split(
        gain_sums,
        [model_width, 2 * model_width, 2 * model_width + head_size],
    )
    return (
        output,
        tokens_grad,
        gain_sums[0],
        gain_sums[1],
        gain_sums[2],
        gain_sums[3],
        projected_owned[:, :query_width],
        projected_owned[:, query_width : query_width + key_width],
        projected_owned[:, query_width + key_width :],
        out_owned,
        owned(0),
        owned(1),
        owned(2),
    )


def solution(mesh):
    placed = (
        P(("fsdp", "tp"), None),
        P(("fsdp", "tp"), None),
        P("fsdp"),
        P("fsdp", None),
        P("fsdp", None),
        P(),
        P(),
        P(),
        P(),
        P("fsdp", "tp"),
        P("fsdp", "tp"),
        P("fsdp", "tp"),
        P("fsdp", "tp"),
        P("fsdp", None, "tp"),
        P("fsdp", None, "tp"),
        P("fsdp", None, "tp"),
    )
    return jax.shard_map(
        partial(per_device, mesh.shape["fsdp"], mesh.shape["tp"]),
        mesh=mesh,
        in_specs=placed,
        out_specs=(
            P(("fsdp", "tp"), None),
            P(("fsdp", "tp"), None),
            P(),
            P(),
            P(),
            P(),
            P("fsdp", "tp"),
            P("fsdp", "tp"),
            P("fsdp", "tp"),
            P("fsdp", "tp"),
            P("fsdp", None, "tp"),
            P("fsdp", None, "tp"),
            P("fsdp", None, "tp"),
        ),
        check_vma=False,
    )
```

```python
from functools import partial

import jax
import jax.numpy as jnp
from jax import lax
from jax.experimental import pallas as pl
from jax.experimental.pallas import tpu as pltpu
from jax.sharding import PartitionSpec as P

SEQ = 1024
TILE = 256
PARTS = 4
VMEM_BYTES = 48 * 1024 * 1024


eps_norm = 1e-06
rope_base = 1000000.0


def matmul(left_side, right_side):
    return jnp.dot(left_side, right_side, preferred_element_type=jnp.float32)


def times_transposed(left_side, right_side):
    return lax.dot_general(
        left_side, right_side, (((1,), (1,)), ((), ())), preferred_element_type=jnp.float32
    )


def inner_rows(left_side, right_side):
    return lax.dot_general(
        left_side, right_side, (((0,), (0,)), ((), ())), preferred_element_type=jnp.float32
    )


def norm_rows(values, scale_gain):
    inverse = lax.rsqrt(jnp.mean(values * values, axis=-1, keepdims=True) + eps_norm)
    return (values * inverse * scale_gain, inverse)


def norm_back(values, inverse, scale_gain, incoming):
    normed = values * inverse
    scaled_grad = incoming * scale_gain
    gain_grad = jnp.sum(incoming * normed, axis=tuple(range(values.ndim - 1)))
    result = inverse * (
        scaled_grad - normed * jnp.mean(scaled_grad * normed, axis=-1, keepdims=True)
    )
    return (result, gain_grad)


def rope_tables(row_count, head_size):
    positions = jnp.arange(row_count, dtype=jnp.float32)
    frequencies = rope_base ** (-jnp.arange(0, head_size, 2, dtype=jnp.float32) / head_size)
    angles = positions[:, None] * frequencies[None, :]
    angles = jnp.concatenate([angles, angles], axis=-1)
    return (jnp.cos(angles), jnp.sin(angles))


def head_norm(values):
    inverse = lax.rsqrt(jnp.mean(values * values, axis=-1, keepdims=True) + eps_norm)
    return (values * inverse, inverse)


def turn(values, cosine, signed_sine):
    half_size = values.shape[-1] // 2
    return values * cosine + pltpu.roll(values, half_size, 1) * signed_sine


def turn_back(incoming, cosine, signed_sine):
    half_size = incoming.shape[-1] // 2
    return incoming * cosine + pltpu.roll(incoming * signed_sine, half_size, 1)


def masked_probs(query_tile, key_rows, row_ids, column_ids, offset, scaling):
    scores = times_transposed(query_tile, key_rows) * scaling
    row_place = lax.broadcasted_iota(jnp.int32, scores.shape, 0) + offset
    column_place = lax.broadcasted_iota(jnp.int32, scores.shape, 1)
    allowed = (column_place <= row_place) & (row_ids == column_ids)
    scores = jnp.where(allowed, scores, -jnp.inf)
    weights = jnp.exp(scores - jnp.max(scores, axis=-1, keepdims=True))
    return weights * (1.0 / jnp.sum(weights, axis=-1, keepdims=True))


def attend_kernel(
    group_size,
    query_ref,
    key_ref,
    value_ref,
    cosine_ref,
    sine_ref,
    row_ids_ref,
    column_ids_ref,
    query_gain_ref,
    key_gain_ref,
    heads_ref,
    key_low,
    value_low,
):
    head_size = query_ref.shape[1]
    scaling = head_size ** (-0.5)

    @pl.when(lax.rem(pl.program_id(1), group_size) == 0)
    def prepare():
        normed, unused = head_norm(key_ref[...])
        key_low[...] = turn(normed * key_gain_ref[...], cosine_ref[...], sine_ref[...]).astype(
            jnp.bfloat16
        )
        value_low[...] = value_ref[...].astype(jnp.bfloat16)

    for offset in range(0, SEQ, TILE):
        finish = offset + TILE
        rows = pl.ds(offset, TILE)
        normed, unused = head_norm(query_ref[rows, :])
        query_tile = turn(
            normed * query_gain_ref[...], cosine_ref[rows, :], sine_ref[rows, :]
        ).astype(jnp.bfloat16)
        probs = masked_probs(
            query_tile,
            key_low[:finish, :],
            row_ids_ref[rows, :],
            column_ids_ref[:, :finish],
            offset,
            scaling,
        )
        heads_ref[rows, :] = matmul(probs.astype(jnp.bfloat16), value_low[:finish, :]).astype(
            jnp.bfloat16
        )


def attend_back_kernel(
    query_count,
    kv_count,
    query_ref,
    key_ref,
    value_ref,
    grad_ref,
    cosine_ref,
    sine_ref,
    row_ids_ref,
    column_ids_ref,
    query_gain_ref,
    key_gain_ref,
    projected_ref,
    query_gain_grad_ref,
    key_gain_grad_ref,
    key_low,
    value_low,
    key_sum,
    value_sum,
):
    head_size = query_ref.shape[1]
    scaling = head_size ** (-0.5)
    group_size = query_count // kv_count
    head = pl.program_id(1)
    place = lax.rem(head, group_size)

    @pl.when((pl.program_id(0) == 0) & (head == 0))
    def clear():
        query_gain_grad_ref[...] = jnp.zeros_like(query_gain_grad_ref)
        key_gain_grad_ref[...] = jnp.zeros_like(key_gain_grad_ref)

    @pl.when(place == 0)
    def prepare():
        normed, unused = head_norm(key_ref[...])
        key_low[...] = turn(normed * key_gain_ref[...], cosine_ref[...], sine_ref[...]).astype(
            jnp.bfloat16
        )
        value_low[...] = value_ref[...].astype(jnp.bfloat16)
        key_sum[...] = jnp.zeros_like(key_sum)
        value_sum[...] = jnp.zeros_like(value_sum)

    def through_norm(turned_grad, cosine, signed_sine, normed, inverse, gain):
        incoming = turn_back(turned_grad, cosine, signed_sine)
        scaled_grad = incoming * gain
        result = inverse * (
            scaled_grad - normed * jnp.mean(scaled_grad * normed, axis=-1, keepdims=True)
        )
        return (result, jnp.sum(incoming * normed, axis=0, keepdims=True))

    columns = pl.ds(pl.multiple_of(head * head_size, head_size), head_size)
    for offset in range(0, SEQ, TILE):
        finish = offset + TILE
        rows = pl.ds(offset, TILE)
        cosine, signed_sine = cosine_ref[rows, :], sine_ref[rows, :]
        normed, inverse = head_norm(query_ref[rows, :])
        query_tile = turn(normed * query_gain_ref[...], cosine, signed_sine).astype(jnp.bfloat16)
        grad_tile = grad_ref[rows, :]
        key_rows = key_low[:finish, :]
        probs = masked_probs(
            query_tile,
            key_rows,
            row_ids_ref[rows, :],
            column_ids_ref[:, :finish],
            offset,
            scaling,
        )
        prob_grad = times_transposed(grad_tile, value_low[:finish, :])
        score_grad = (
            probs * (prob_grad - jnp.sum(probs * prob_grad, axis=-1, keepdims=True))
        ).astype(jnp.bfloat16)
        value_sum[:finish, :] += inner_rows(probs.astype(jnp.bfloat16), grad_tile)
        key_sum[:finish, :] += inner_rows(score_grad, query_tile)
        result, gain_grad = through_norm(
            matmul(score_grad, key_rows) * scaling,
            cosine,
            signed_sine,
            normed,
            inverse,
            query_gain_ref[...],
        )
        projected_ref[rows, columns] = result.astype(jnp.bfloat16)
        query_gain_grad_ref[...] += gain_grad

    @pl.when(place == group_size - 1)
    def finish_group():
        group = lax.div(head, group_size)
        normed, inverse = head_norm(key_ref[...])
        result, gain_grad = through_norm(
            key_sum[...] * scaling,
            cosine_ref[...],
            sine_ref[...],
            normed,
            inverse,
            key_gain_ref[...],
        )
        key_columns = pl.ds(
            pl.multiple_of((query_count + group) * head_size, head_size), head_size
        )
        value_columns = pl.ds(
            pl.multiple_of((query_count + kv_count + group) * head_size, head_size), head_size
        )
        projected_ref[:, key_columns] = result.astype(jnp.bfloat16)
        projected_ref[:, value_columns] = value_sum[...].astype(jnp.bfloat16)
        key_gain_grad_ref[...] += gain_grad


def attention_specs(query_count, kv_count, head_size):
    group_size = query_count // kv_count
    block = (SEQ, head_size)
    fixed = lambda shape: pl.BlockSpec(shape, lambda s, h: (0, 0))
    operands = [
        pl.BlockSpec(block, lambda s, h: (s, h)),
        pl.BlockSpec(block, lambda s, h: (s, query_count + h // group_size)),
        pl.BlockSpec(block, lambda s, h: (s, query_count + kv_count + h // group_size)),
    ]
    tables = [
        fixed(block),
        fixed(block),
        pl.BlockSpec((SEQ, 1), lambda s, h: (s, 0)),
        pl.BlockSpec((1, SEQ), lambda s, h: (0, s)),
        fixed((1, head_size)),
        fixed((1, head_size)),
    ]
    return (operands, tables)


def attend(projected, tables, query_count, kv_count, head_size):
    rows = projected.shape[0]
    operands, table_specs = attention_specs(query_count, kv_count, head_size)
    pairs = rows * SEQ * query_count * 5 // 8
    return pl.pallas_call(
        partial(attend_kernel, query_count // kv_count),
        grid=(rows // SEQ, query_count),
        in_specs=operands + table_specs,
        out_specs=pl.BlockSpec((SEQ, head_size), lambda s, h: (s, h)),
        out_shape=jax.ShapeDtypeStruct((rows, query_count * head_size), jnp.bfloat16),
        scratch_shapes=[
            pltpu.VMEM((SEQ, head_size), jnp.bfloat16),
            pltpu.VMEM((SEQ, head_size), jnp.bfloat16),
        ],
        compiler_params=pltpu.CompilerParams(vmem_limit_bytes=VMEM_BYTES),
        cost_estimate=pl.CostEstimate(
            flops=4 * pairs * head_size,
            bytes_accessed=6 * rows * query_count * head_size,
            transcendentals=pairs,
        ),
        name="attend",
    )(projected, projected, projected, *tables)


def attend_back(projected, heads_grad, tables, query_count, kv_count, head_size):
    rows = projected.shape[0]
    width = projected.shape[1]
    operands, table_specs = attention_specs(query_count, kv_count, head_size)
    pairs = rows * SEQ * query_count * 5 // 8
    return pl.pallas_call(
        partial(attend_back_kernel, query_count, kv_count),
        grid=(rows // SEQ, query_count),
        in_specs=operands + [pl.BlockSpec((SEQ, head_size), lambda s, h: (s, h))] + table_specs,
        out_specs=[
            pl.BlockSpec((SEQ, width), lambda s, h: (s, 0)),
            pl.BlockSpec((1, head_size), lambda s, h: (0, 0)),
            pl.BlockSpec((1, head_size), lambda s, h: (0, 0)),
        ],
        out_shape=[
            jax.ShapeDtypeStruct((rows, width), jnp.bfloat16),
            jax.ShapeDtypeStruct((1, head_size), jnp.float32),
            jax.ShapeDtypeStruct((1, head_size), jnp.float32),
        ],
        scratch_shapes=[
            pltpu.VMEM((SEQ, head_size), jnp.bfloat16),
            pltpu.VMEM((SEQ, head_size), jnp.bfloat16),
            pltpu.VMEM((SEQ, head_size), jnp.float32),
            pltpu.VMEM((SEQ, head_size), jnp.float32),
        ],
        compiler_params=pltpu.CompilerParams(vmem_limit_bytes=VMEM_BYTES),
        cost_estimate=pl.CostEstimate(
            flops=10 * pairs * head_size,
            bytes_accessed=10 * rows * query_count * head_size,
            transcendentals=pairs,
        ),
        name="attend_back",
    )(projected, projected, projected, heads_grad, *tables)


def joined(own, other, bit):
    first_half = jnp.where(bit == 0, own, other)
    last_half = jnp.where(bit == 0, other, own)
    return jnp.concatenate([first_half, last_half], axis=0)


def halves(values, bit):
    rows = values.shape[0] // 2
    kept = lax.dynamic_slice_in_dim(values, bit * rows, rows, 0)
    sent = lax.dynamic_slice_in_dim(values, (1 - bit) * rows, rows, 0)
    return (kept, sent)


def make_moves(fsdp_size, tp_size):
    swap_core = [(i, i ^ 1) for i in range(tp_size)]
    swap_chip = [(i, (i + 2) % tp_size) for i in range(tp_size)]
    swap_pair = [(i, i ^ 1) for i in range(fsdp_size)]
    columns = [list(range(b, fsdp_size, 2)) for b in range(2)]

    def to_core(values):
        return lax.ppermute(values, "tp", swap_core)

    def to_chip(values):
        return lax.ppermute(values, "tp", swap_chip)

    def to_pair(values):
        return lax.ppermute(values, "fsdp", swap_pair)

    def tp_both(own, received):
        return joined(own, received, lax.axis_index("tp") // 2)

    def tp_join(both, others):
        place = lax.axis_index("tp")
        rows, width = both.shape[0] // 2, both.shape[1]
        both = both.reshape(2, 1, rows, width)
        others = others.reshape(2, 1, rows, width)
        first_core = jnp.where(place % 2 == 0, both, others)
        last_core = jnp.where(place % 2 == 0, others, both)
        return jnp.concatenate([first_core, last_core], axis=1).reshape(4 * rows, width)

    def tp_gather(own):
        both = tp_both(own, to_chip(own))
        return tp_join(both, to_core(both))

    def tp_split(full):
        place = lax.axis_index("tp")
        rows, width = full.shape[0] // 4, full.shape[1]
        split = full.reshape(2, 2, rows, width)
        kept = lax.dynamic_index_in_dim(split, place % 2, 1, False)
        sent = lax.dynamic_index_in_dim(split, 1 - place % 2, 1, False).astype(jnp.bfloat16)
        return (kept, to_core(sent))

    def tp_halve(split):
        kept, received = split
        kept, sent = halves(kept + received.astype(jnp.float32), lax.axis_index("tp") // 2)
        return (kept, to_chip(sent.astype(jnp.bfloat16)))

    def tp_sum(halved):
        kept, received = halved
        return (kept + received.astype(jnp.float32)).reshape(kept.shape[1:])

    def tp_scatter(full):
        return tp_sum(tp_halve(tp_split(full)))

    def plane_open(own):
        return (to_chip(own), to_pair(own))

    def plane_cross(opened):
        across, beside = opened
        cut = across.shape[0] // 2
        return (to_chip(beside[:cut]), to_pair(across[cut:]))

    def plane_core(own, opened, crossed):
        mine = jnp.concatenate([own, *opened, *crossed], axis=0)
        return (mine, to_core(mine))

    def plane_join(cored):
        return jnp.concatenate(cored, axis=0)

    def plane_gather(own):
        opened = plane_open(own)
        return plane_join(plane_core(own, opened, plane_cross(opened)))

    def fold_core(kept, sent):
        return (kept, to_core(sent.astype(jnp.bfloat16)))

    def fold_cross(cored):
        kept, received = cored
        rows = kept.shape[0] // 4
        cut = rows // 2
        far = (kept[3 * rows :] + received[3 * rows :].astype(jnp.float32)).astype(jnp.bfloat16)
        return (kept, received, to_chip(far[:cut]), to_pair(far[cut:]))

    def fold_open(crossed):
        kept, received, from_chip, from_pair = crossed
        rows = kept.shape[0] // 4
        cut = rows // 2
        own, across, beside = [
            kept[i * rows : (i + 1) * rows]
            + received[i * rows : (i + 1) * rows].astype(jnp.float32)
            for i in range(3)
        ]
        across = jnp.concatenate([across[:cut], across[cut:] + from_pair.astype(jnp.float32)])
        beside = jnp.concatenate([beside[:cut] + from_chip.astype(jnp.float32), beside[cut:]])
        return (
            own,
            to_chip(across.astype(jnp.bfloat16)),
            to_pair(beside.astype(jnp.bfloat16)),
        )

    def fold_sum(opened):
        own, from_chip, from_pair = opened
        return own + from_chip.astype(jnp.float32) + from_pair.astype(jnp.float32)

    def plane_share(share):
        place = lax.axis_index("tp")
        rows, count = share.shape[0] // 4, share.shape[1]
        split = share.reshape(2, 2, rows, count)
        split = jnp.where(place // 2 == 0, split, split[::-1])
        split = jnp.where(place % 2 == 0, split, split[:, ::-1]).swapaxes(0, 1)
        return jnp.stack([split, to_pair(split)], axis=1).reshape(8 * rows, count)

    def column_gather(own):
        return lax.all_gather(own, "fsdp", axis=0, tiled=True, axis_index_groups=columns)

    def column_scatter(full):
        return lax.psum_scatter(
            full, "fsdp", scatter_dimension=0, tiled=True, axis_index_groups=columns
        )

    def weight_gather(own):
        pair_bit = lax.axis_index("fsdp") % 2
        rows, width = own.shape
        mine = column_gather(own)
        theirs = to_pair(mine)
        mine = mine.reshape(fsdp_size // 2, 1, rows, width)
        theirs = theirs.reshape(fsdp_size // 2, 1, rows, width)
        return jnp.concatenate(
            [jnp.where(pair_bit == 0, mine, theirs), jnp.where(pair_bit == 0, theirs, mine)],
            axis=1,
        ).reshape(fsdp_size * rows, width)

    def pair_columns(values):
        pair_bit = lax.axis_index("fsdp") % 2
        width = values.shape[1] // fsdp_size
        return [
            jnp.concatenate(
                [
                    lax.dynamic_slice_in_dim(values, (2 * place + bit) * width, width, 1)
                    for place in range(fsdp_size // 2)
                ],
                axis=1,
            )
            for bit in (pair_bit, 1 - pair_bit)
        ]

    def weight_reduce(kept, received):
        summed = kept + received.astype(jnp.float32)
        return column_scatter(summed.astype(jnp.bfloat16)).astype(jnp.float32)

    def sum_all(values):
        for step in range(tp_size.bit_length() - 1):
            swap = [(i, i ^ (1 << step)) for i in range(tp_size)]
            values = values + lax.ppermute(values, "tp", swap)
        for step in range(fsdp_size.bit_length() - 1):
            swap = [(i, i ^ (1 << step)) for i in range(fsdp_size)]
            values = values + lax.ppermute(values, "fsdp", swap)
        return values

    return (
        to_pair,
        to_core,
        to_chip,
        tp_both,
        tp_join,
        tp_gather,
        tp_split,
        tp_halve,
        tp_sum,
        tp_scatter,
        plane_gather,
        fold_core,
        fold_cross,
        fold_open,
        fold_sum,
        plane_share,
        column_gather,
        column_scatter,
        weight_gather,
        pair_columns,
        weight_reduce,
        sum_all,
    )


def per_device(
    fsdp_size,
    tp_size,
    tokens,
    cotangent,
    segments,
    routes,
    gate_logits,
    attention_gain,
    feedforward_gain,
    query_gain,
    key_gain,
    query_weight,
    key_weight,
    value_weight,
    out_weight,
    gate_weight,
    up_weight,
    down_weight,
):
    (
        to_pair,
        to_core,
        to_chip,
        tp_both,
        tp_join,
        tp_gather,
        tp_split,
        tp_halve,
        tp_sum,
        tp_scatter,
        plane_gather,
        fold_core,
        fold_cross,
        fold_open,
        fold_sum,
        plane_share,
        column_gather,
        column_scatter,
        weight_gather,
        pair_columns,
        weight_reduce,
        sum_all,
    ) = make_moves(fsdp_size, tp_size)
    pair_bit = lax.axis_index("fsdp") % 2
    head_size = query_gain.shape[0]
    kv_count = key_weight.shape[1] // head_size
    query_count = query_weight.shape[1] // head_size
    weight_rows, expert_count, expert_width = gate_weight.shape
    half_experts = expert_count // 2
    half_width = half_experts * expert_width
    part_width = half_width // PARTS
    rows_all = segments.shape[0]
    cosine, sine_table = rope_tables(SEQ, head_size)
    turn_sign = jnp.where(jnp.arange(head_size) < head_size // 2, -1.0, 1.0)
    tables = (
        cosine,
        sine_table * turn_sign,
        segments.reshape(rows_all, 1),
        segments.reshape(1, rows_all),
        query_gain.reshape(1, head_size),
        key_gain.reshape(1, head_size),
    )
    token_rows = tokens.astype(jnp.float32)
    first_norm, first_inverse = norm_rows(token_rows, attention_gain)
    first_full = tp_gather(first_norm.astype(jnp.bfloat16))
    query_key_value = weight_gather(
        jnp.concatenate([query_weight, key_weight, value_weight], axis=1)
    )
    full_out = weight_gather(out_weight)
    model_width = tokens.shape[1]
    query_width = query_count * head_size
    key_width = kv_count * head_size

    def flat(weight):
        return weight.reshape(weight_rows, 2, PARTS, part_width)

    flats = (flat(gate_weight), flat(up_weight), flat(down_weight))

    def fetch(part):
        def side(bit):
            return jnp.concatenate(
                [lax.dynamic_index_in_dim(w[:, :, part], bit, 1, False) for w in flats], axis=1
            )

        return column_gather(joined(side(pair_bit), to_pair(side(1 - pair_bit)), pair_bit))

    expert_weights = [fetch(part) for part in range(PARTS)]

    grad_group = plane_gather(cotangent)
    projected = matmul(first_full, query_key_value)
    heads_low = attend(projected, tables, query_count, kv_count, head_size)
    heads_low, grad_group = lax.optimization_barrier((heads_low, grad_group))
    attn_local = tp_scatter(times_transposed(heads_low, full_out))
    middle = token_rows + attn_local
    second_norm, second_inverse = norm_rows(middle, feedforward_gain)

    second_group = plane_gather(second_norm.astype(jnp.bfloat16))
    gate_probs = jax.nn.softmax(gate_logits, axis=-1)
    expert_ids = jnp.arange(expert_count, dtype=jnp.int32)
    share_own = jnp.sum(
        jnp.where(routes[:, :, None] == expert_ids[None, None, :], gate_probs[:, :, None], 0.0),
        axis=1,
    )
    share_group = plane_share(share_own)
    share_half = lax.dynamic_slice_in_dim(share_group, pair_bit * half_experts, half_experts, 1)

    weight_terms = []
    last = []

    def step(value):
        if last:
            value = lax.optimization_barrier((value, last[0]))[0]
        last[:] = [value]
        return value

    def after(value, *earlier):
        return lax.optimization_barrier((value, earlier))[0]

    def exchange(reduced):
        kept, sent = halves(reduced, pair_bit)
        return (kept, to_pair(sent))

    for part in range(PARTS):
        weights = expert_weights[part]
        weight_in = weights[:, : 2 * part_width]
        weight_down = weights[:, 2 * part_width :]
        span = half_experts // PARTS
        share = jnp.repeat(share_half[:, part * span : (part + 1) * span], expert_width, axis=1)
        both_pre = matmul(second_group, weight_in)
        gate_pre, up_pre = both_pre[:, :part_width], both_pre[:, part_width:]
        sigmoid_gate = jax.nn.sigmoid(gate_pre)
        silu_gate = gate_pre * sigmoid_gate
        hidden = (silu_gate * up_pre * share).astype(jnp.bfloat16)
        hidden_grad = matmul(grad_group, weight_down) * share
        up_grad = (hidden_grad * silu_gate).astype(jnp.bfloat16)
        gate_grad = (
            hidden_grad * up_pre * sigmoid_gate * (1.0 + gate_pre * (1.0 - sigmoid_gate))
        ).astype(jnp.bfloat16)
        both_grad = jnp.concatenate([gate_grad, up_grad], axis=1)
        if part < PARTS - 1:
            moe_part = times_transposed(hidden, weight_down)
            second_part = times_transposed(both_grad, weight_in)
            moe_sum = moe_part if part == 0 else moe_sum + moe_part
            second_sum = second_part if part == 0 else second_sum + second_part
            moe_sum, second_sum = lax.optimization_barrier((moe_sum, second_sum))
        else:
            second_sent = second_sum[rows_all:] + times_transposed(
                both_grad[rows_all:], weight_in
            )
            second_sent = step(second_sent.astype(jnp.bfloat16))
            second_kept = second_sum[:rows_all] + times_transposed(
                after(both_grad, second_sent)[:rows_all], weight_in
            )
            hidden, both_grad = after((hidden, both_grad), second_kept)
            moe_sent = moe_sum[rows_all:] + times_transposed(hidden[rows_all:], weight_down)
            moe_kept = moe_sum[:rows_all] + times_transposed(hidden[:rows_all], weight_down)
            moe_sent = moe_sent.astype(jnp.bfloat16)
        weight_term = jnp.concatenate(
            [
                inner_rows(second_group, both_grad).astype(jnp.bfloat16),
                inner_rows(grad_group, hidden).astype(jnp.bfloat16),
            ],
            axis=1,
        )
        weight_terms.append(weight_term)

    reduced = [column_scatter(term) for term in weight_terms]
    second_fold = fold_cross(step(fold_core(second_kept, second_sent)))
    second_fold = fold_open(step(second_fold))
    owned_parts = [exchange(after(reduced[0], second_fold[0]))]
    second_grad = fold_sum(step(second_fold))
    middle_back, feedforward_gain_grad = norm_back(
        middle, second_inverse, feedforward_gain, second_grad
    )
    middle_grad = cotangent.astype(jnp.float32) + middle_back
    grad_low = middle_grad.astype(jnp.bfloat16)
    grad_chip = to_chip(grad_low)
    owned_parts[0] = step(owned_parts[0])
    owned_parts.append(exchange(after(reduced[1], grad_low)))
    first_kept, first_sent = pair_columns(after(first_full, grad_low))
    grad_chip, first_sent = step((grad_chip, first_sent))
    grad_both = tp_both(grad_low, grad_chip)
    attn_grad_full = tp_join(grad_both, step(to_core(grad_both)))
    moe_fold = fold_core(*after((moe_kept, moe_sent), attn_grad_full))
    heads_grad = matmul(attn_grad_full, full_out).astype(jnp.bfloat16)
    grad_kept, grad_sent = pair_columns(attn_grad_full)
    out_sent = inner_rows(grad_sent, heads_low).astype(jnp.bfloat16)
    heads_grad, out_sent = step((heads_grad, out_sent))
    out_received = to_pair(out_sent)
    owned_parts[1] = step(owned_parts[1])
    projected_grad, query_gain_grad, key_gain_grad = step(
        attend_back(projected, heads_grad, tables, query_count, kv_count, head_size)
    )
    projected_sent = step(inner_rows(first_sent, projected_grad).astype(jnp.bfloat16))
    projected_received = to_pair(projected_sent)
    out_kept = inner_rows(after(grad_kept, projected_sent), heads_low)
    out_owned = weight_reduce(out_kept, step(out_received))
    projected_kept = step(inner_rows(first_kept, projected_grad))
    first_split = tp_split(
        times_transposed(after(projected_grad, projected_kept), query_key_value)
    )
    first_halved = tp_halve(step(first_split))
    projected_received = step(projected_received)
    projected_owned = weight_reduce(projected_kept, projected_received)
    moe_fold = fold_cross(after(moe_fold, projected_received))
    owned_parts.append(exchange(after(reduced[2], projected_received)))
    moe_fold = fold_open(step(moe_fold))
    first_grad = tp_sum(step(first_halved))
    owned_parts.append(exchange(after(reduced[3], first_grad)))
    output = (middle + fold_sum(step(moe_fold))).astype(jnp.bfloat16)

    def owned(index):
        place = slice(index * part_width, (index + 1) * part_width)
        mine = jnp.concatenate([kept[:, place] for kept, sent in owned_parts], axis=1)
        theirs = jnp.concatenate([sent[:, place] for kept, sent in owned_parts], axis=1)
        return (
            jnp.concatenate(
                [
                    jnp.where(pair_bit == 0, mine, theirs),
                    jnp.where(pair_bit == 0, theirs, mine),
                ],
                axis=1,
            )
            .astype(jnp.float32)
            .reshape(weight_rows, expert_count, expert_width)
        )

    rows_back, attention_gain_grad = norm_back(
        token_rows, first_inverse, attention_gain, first_grad
    )
    tokens_grad = middle_grad + rows_back
    gain_sums = sum_all(
        jnp.concatenate(
            [
                attention_gain_grad,
                feedforward_gain_grad,
                query_gain_grad.reshape(head_size),
                key_gain_grad.reshape(head_size),
            ]
        )
    )
    gain_sums = jnp.split(
        gain_sums,
        [model_width, 2 * model_width, 2 * model_width + head_size],
    )
    return (
        output,
        tokens_grad,
        gain_sums[0],
        gain_sums[1],
        gain_sums[2],
        gain_sums[3],
        projected_owned[:, :query_width],
        projected_owned[:, query_width : query_width + key_width],
        projected_owned[:, query_width + key_width :],
        out_owned,
        owned(0),
        owned(1),
        owned(2),
    )


def solution(mesh):
    placed = (
        P(("fsdp", "tp"), None),
        P(("fsdp", "tp"), None),
        P("fsdp"),
        P("fsdp", None),
        P("fsdp", None),
        P(),
        P(),
        P(),
        P(),
        P("fsdp", "tp"),
        P("fsdp", "tp"),
        P("fsdp", "tp"),
        P("fsdp", "tp"),
        P("fsdp", None, "tp"),
        P("fsdp", None, "tp"),
        P("fsdp", None, "tp"),
    )
    return jax.shard_map(
        partial(per_device, mesh.shape["fsdp"], mesh.shape["tp"]),
        mesh=mesh,
        in_specs=placed,
        out_specs=(
            P(("fsdp", "tp"), None),
            P(("fsdp", "tp"), None),
            P(),
            P(),
            P(),
            P(),
            P("fsdp", "tp"),
            P("fsdp", "tp"),
            P("fsdp", "tp"),
            P("fsdp", "tp"),
            P("fsdp", None, "tp"),
            P("fsdp", None, "tp"),
            P("fsdp", None, "tp"),
        ),
        check_vma=False,
    )
```

```python
from functools import partial

import jax
import jax.numpy as jnp
from jax import lax
from jax.experimental import pallas as pl
from jax.experimental.pallas import tpu as pltpu
from jax.sharding import PartitionSpec as P

SEQ = 1024
TILE = 256
PARTS = 2
VMEM_BYTES = 48 * 1024 * 1024


eps_norm = 1e-06
rope_base = 1000000.0


def matmul(left_side, right_side):
    return jnp.dot(left_side, right_side, preferred_element_type=jnp.float32)


def times_transposed(left_side, right_side):
    return lax.dot_general(
        left_side, right_side, (((1,), (1,)), ((), ())), preferred_element_type=jnp.float32
    )


def inner_rows(left_side, right_side):
    return lax.dot_general(
        left_side, right_side, (((0,), (0,)), ((), ())), preferred_element_type=jnp.float32
    )


def norm_rows(values, scale_gain):
    inverse = lax.rsqrt(jnp.mean(values * values, axis=-1, keepdims=True) + eps_norm)
    return (values * inverse * scale_gain, inverse)


def norm_back(values, inverse, scale_gain, incoming):
    normed = values * inverse
    scaled_grad = incoming * scale_gain
    gain_grad = jnp.sum(incoming * normed, axis=tuple(range(values.ndim - 1)))
    result = inverse * (
        scaled_grad - normed * jnp.mean(scaled_grad * normed, axis=-1, keepdims=True)
    )
    return (result, gain_grad)


def rope_tables(row_count, head_size):
    positions = jnp.arange(row_count, dtype=jnp.float32)
    frequencies = rope_base ** (-jnp.arange(0, head_size, 2, dtype=jnp.float32) / head_size)
    angles = positions[:, None] * frequencies[None, :]
    angles = jnp.concatenate([angles, angles], axis=-1)
    return (jnp.cos(angles), jnp.sin(angles))


def head_norm(values):
    inverse = lax.rsqrt(jnp.mean(values * values, axis=-1, keepdims=True) + eps_norm)
    return (values * inverse, inverse)


def turn(values, cosine, signed_sine):
    half_size = values.shape[-1] // 2
    return values * cosine + pltpu.roll(values, half_size, 1) * signed_sine


def turn_back(incoming, cosine, signed_sine):
    half_size = incoming.shape[-1] // 2
    return incoming * cosine + pltpu.roll(incoming * signed_sine, half_size, 1)


def masked_probs(query_tile, key_rows, row_ids, column_ids, offset, scaling):
    scores = times_transposed(query_tile, key_rows) * scaling
    row_place = lax.broadcasted_iota(jnp.int32, scores.shape, 0) + offset
    column_place = lax.broadcasted_iota(jnp.int32, scores.shape, 1)
    allowed = (column_place <= row_place) & (row_ids == column_ids)
    scores = jnp.where(allowed, scores, -jnp.inf)
    weights = jnp.exp(scores - jnp.max(scores, axis=-1, keepdims=True))
    return weights * (1.0 / jnp.sum(weights, axis=-1, keepdims=True))


def attend_kernel(
    group_size,
    query_ref,
    key_ref,
    value_ref,
    cosine_ref,
    sine_ref,
    row_ids_ref,
    column_ids_ref,
    query_gain_ref,
    key_gain_ref,
    heads_ref,
    key_low,
    value_low,
):
    head_size = query_ref.shape[1]
    scaling = head_size ** (-0.5)

    @pl.when(lax.rem(pl.program_id(1), group_size) == 0)
    def prepare():
        normed, unused = head_norm(key_ref[...])
        key_low[...] = turn(normed * key_gain_ref[...], cosine_ref[...], sine_ref[...]).astype(
            jnp.bfloat16
        )
        value_low[...] = value_ref[...].astype(jnp.bfloat16)

    for offset in range(0, SEQ, TILE):
        finish = offset + TILE
        rows = pl.ds(offset, TILE)
        normed, unused = head_norm(query_ref[rows, :])
        query_tile = turn(
            normed * query_gain_ref[...], cosine_ref[rows, :], sine_ref[rows, :]
        ).astype(jnp.bfloat16)
        probs = masked_probs(
            query_tile,
            key_low[:finish, :],
            row_ids_ref[rows, :],
            column_ids_ref[:, :finish],
            offset,
            scaling,
        )
        heads_ref[rows, :] = matmul(probs.astype(jnp.bfloat16), value_low[:finish, :]).astype(
            jnp.bfloat16
        )


def attend_back_kernel(
    query_count,
    kv_count,
    query_ref,
    key_ref,
    value_ref,
    grad_ref,
    cosine_ref,
    sine_ref,
    row_ids_ref,
    column_ids_ref,
    query_gain_ref,
    key_gain_ref,
    projected_ref,
    query_gain_grad_ref,
    key_gain_grad_ref,
    key_low,
    value_low,
    key_sum,
    value_sum,
):
    head_size = query_ref.shape[1]
    scaling = head_size ** (-0.5)
    group_size = query_count // kv_count
    head = pl.program_id(1)
    place = lax.rem(head, group_size)

    @pl.when((pl.program_id(0) == 0) & (head == 0))
    def clear():
        query_gain_grad_ref[...] = jnp.zeros_like(query_gain_grad_ref)
        key_gain_grad_ref[...] = jnp.zeros_like(key_gain_grad_ref)

    @pl.when(place == 0)
    def prepare():
        normed, unused = head_norm(key_ref[...])
        key_low[...] = turn(normed * key_gain_ref[...], cosine_ref[...], sine_ref[...]).astype(
            jnp.bfloat16
        )
        value_low[...] = value_ref[...].astype(jnp.bfloat16)
        key_sum[...] = jnp.zeros_like(key_sum)
        value_sum[...] = jnp.zeros_like(value_sum)

    def through_norm(turned_grad, cosine, signed_sine, normed, inverse, gain):
        incoming = turn_back(turned_grad, cosine, signed_sine)
        scaled_grad = incoming * gain
        result = inverse * (
            scaled_grad - normed * jnp.mean(scaled_grad * normed, axis=-1, keepdims=True)
        )
        return (result, jnp.sum(incoming * normed, axis=0, keepdims=True))

    columns = pl.ds(pl.multiple_of(head * head_size, head_size), head_size)
    for offset in range(0, SEQ, TILE):
        finish = offset + TILE
        rows = pl.ds(offset, TILE)
        cosine, signed_sine = cosine_ref[rows, :], sine_ref[rows, :]
        normed, inverse = head_norm(query_ref[rows, :])
        query_tile = turn(normed * query_gain_ref[...], cosine, signed_sine).astype(jnp.bfloat16)
        grad_tile = grad_ref[rows, :]
        key_rows = key_low[:finish, :]
        probs = masked_probs(
            query_tile,
            key_rows,
            row_ids_ref[rows, :],
            column_ids_ref[:, :finish],
            offset,
            scaling,
        )
        prob_grad = times_transposed(grad_tile, value_low[:finish, :])
        score_grad = (
            probs * (prob_grad - jnp.sum(probs * prob_grad, axis=-1, keepdims=True))
        ).astype(jnp.bfloat16)
        value_sum[:finish, :] += inner_rows(probs.astype(jnp.bfloat16), grad_tile)
        key_sum[:finish, :] += inner_rows(score_grad, query_tile)
        result, gain_grad = through_norm(
            matmul(score_grad, key_rows) * scaling,
            cosine,
            signed_sine,
            normed,
            inverse,
            query_gain_ref[...],
        )
        projected_ref[rows, columns] = result.astype(jnp.bfloat16)
        query_gain_grad_ref[...] += gain_grad

    @pl.when(place == group_size - 1)
    def finish_group():
        group = lax.div(head, group_size)
        normed, inverse = head_norm(key_ref[...])
        result, gain_grad = through_norm(
            key_sum[...] * scaling,
            cosine_ref[...],
            sine_ref[...],
            normed,
            inverse,
            key_gain_ref[...],
        )
        key_columns = pl.ds(
            pl.multiple_of((query_count + group) * head_size, head_size), head_size
        )
        value_columns = pl.ds(
            pl.multiple_of((query_count + kv_count + group) * head_size, head_size), head_size
        )
        projected_ref[:, key_columns] = result.astype(jnp.bfloat16)
        projected_ref[:, value_columns] = value_sum[...].astype(jnp.bfloat16)
        key_gain_grad_ref[...] += gain_grad


def attention_specs(query_count, kv_count, head_size):
    group_size = query_count // kv_count
    block = (SEQ, head_size)
    fixed = lambda shape: pl.BlockSpec(shape, lambda s, h: (0, 0))
    operands = [
        pl.BlockSpec(block, lambda s, h: (s, h)),
        pl.BlockSpec(block, lambda s, h: (s, query_count + h // group_size)),
        pl.BlockSpec(block, lambda s, h: (s, query_count + kv_count + h // group_size)),
    ]
    tables = [
        fixed(block),
        fixed(block),
        pl.BlockSpec((SEQ, 1), lambda s, h: (s, 0)),
        pl.BlockSpec((1, SEQ), lambda s, h: (0, s)),
        fixed((1, head_size)),
        fixed((1, head_size)),
    ]
    return (operands, tables)


def attend(projected, tables, query_count, kv_count, head_size):
    rows = projected.shape[0]
    operands, table_specs = attention_specs(query_count, kv_count, head_size)
    pairs = rows * SEQ * query_count * 5 // 8
    return pl.pallas_call(
        partial(attend_kernel, query_count // kv_count),
        grid=(rows // SEQ, query_count),
        in_specs=operands + table_specs,
        out_specs=pl.BlockSpec((SEQ, head_size), lambda s, h: (s, h)),
        out_shape=jax.ShapeDtypeStruct((rows, query_count * head_size), jnp.bfloat16),
        scratch_shapes=[
            pltpu.VMEM((SEQ, head_size), jnp.bfloat16),
            pltpu.VMEM((SEQ, head_size), jnp.bfloat16),
        ],
        compiler_params=pltpu.CompilerParams(vmem_limit_bytes=VMEM_BYTES),
        cost_estimate=pl.CostEstimate(
            flops=60 * pairs * head_size,
            bytes_accessed=6 * rows * query_count * head_size,
            transcendentals=pairs,
        ),
        name="attend",
    )(projected, projected, projected, *tables)


def attend_back(projected, heads_grad, tables, query_count, kv_count, head_size):
    rows = projected.shape[0]
    width = projected.shape[1]
    operands, table_specs = attention_specs(query_count, kv_count, head_size)
    pairs = rows * SEQ * query_count * 5 // 8
    return pl.pallas_call(
        partial(attend_back_kernel, query_count, kv_count),
        grid=(rows // SEQ, query_count),
        in_specs=operands + [pl.BlockSpec((SEQ, head_size), lambda s, h: (s, h))] + table_specs,
        out_specs=[
            pl.BlockSpec((SEQ, width), lambda s, h: (s, 0)),
            pl.BlockSpec((1, head_size), lambda s, h: (0, 0)),
            pl.BlockSpec((1, head_size), lambda s, h: (0, 0)),
        ],
        out_shape=[
            jax.ShapeDtypeStruct((rows, width), jnp.bfloat16),
            jax.ShapeDtypeStruct((1, head_size), jnp.float32),
            jax.ShapeDtypeStruct((1, head_size), jnp.float32),
        ],
        scratch_shapes=[
            pltpu.VMEM((SEQ, head_size), jnp.bfloat16),
            pltpu.VMEM((SEQ, head_size), jnp.bfloat16),
            pltpu.VMEM((SEQ, head_size), jnp.float32),
            pltpu.VMEM((SEQ, head_size), jnp.float32),
        ],
        compiler_params=pltpu.CompilerParams(vmem_limit_bytes=VMEM_BYTES),
        cost_estimate=pl.CostEstimate(
            flops=90 * pairs * head_size,
            bytes_accessed=10 * rows * query_count * head_size,
            transcendentals=pairs,
        ),
        name="attend_back",
    )(projected, projected, projected, heads_grad, *tables)


def joined(own, other, bit):
    first_half = jnp.where(bit == 0, own, other)
    last_half = jnp.where(bit == 0, other, own)
    return jnp.concatenate([first_half, last_half], axis=0)


def halves(values, bit):
    rows = values.shape[0] // 2
    kept = lax.dynamic_slice_in_dim(values, bit * rows, rows, 0)
    sent = lax.dynamic_slice_in_dim(values, (1 - bit) * rows, rows, 0)
    return (kept, sent)


def make_moves(fsdp_size, tp_size):
    swap_core = [(i, i ^ 1) for i in range(tp_size)]
    swap_chip = [(i, (i + 2) % tp_size) for i in range(tp_size)]
    swap_pair = [(i, i ^ 1) for i in range(fsdp_size)]
    columns = [list(range(b, fsdp_size, 2)) for b in range(2)]

    def to_core(values):
        return lax.ppermute(values, "tp", swap_core)

    def to_chip(values):
        return lax.ppermute(values, "tp", swap_chip)

    def to_pair(values):
        return lax.ppermute(values, "fsdp", swap_pair)

    def tp_both(own, received):
        return joined(own, received, lax.axis_index("tp") // 2)

    def tp_join(both, others):
        place = lax.axis_index("tp")
        rows, width = both.shape[0] // 2, both.shape[1]
        both = both.reshape(2, 1, rows, width)
        others = others.reshape(2, 1, rows, width)
        first_core = jnp.where(place % 2 == 0, both, others)
        last_core = jnp.where(place % 2 == 0, others, both)
        return jnp.concatenate([first_core, last_core], axis=1).reshape(4 * rows, width)

    def tp_gather(own):
        both = tp_both(own, to_chip(own))
        return tp_join(both, to_core(both))

    def tp_split(full):
        place = lax.axis_index("tp")
        rows, width = full.shape[0] // 4, full.shape[1]
        split = full.reshape(2, 2, rows, width)
        kept = lax.dynamic_index_in_dim(split, place % 2, 1, False)
        sent = lax.dynamic_index_in_dim(split, 1 - place % 2, 1, False).astype(jnp.bfloat16)
        return (kept, to_core(sent))

    def tp_halve(split):
        kept, received = split
        kept, sent = halves(kept + received.astype(jnp.float32), lax.axis_index("tp") // 2)
        return (kept, to_chip(sent.astype(jnp.bfloat16)))

    def tp_sum(halved):
        kept, received = halved
        return (kept + received.astype(jnp.float32)).reshape(kept.shape[1:])

    def tp_scatter(full):
        return tp_sum(tp_halve(tp_split(full)))

    def plane_open(own):
        return (to_chip(own), to_pair(own))

    def plane_cross(opened):
        across, beside = opened
        cut = across.shape[0] // 2
        return (to_chip(beside[:cut]), to_pair(across[cut:]))

    def plane_core(own, opened, crossed):
        mine = jnp.concatenate([own, *opened, *crossed], axis=0)
        return (mine, to_core(mine))

    def plane_join(cored):
        return jnp.concatenate(cored, axis=0)

    def plane_gather(own):
        opened = plane_open(own)
        return plane_join(plane_core(own, opened, plane_cross(opened)))

    def fold_core(kept, sent):
        return (kept, to_core(sent))

    def fold_cross(cored):
        kept, received = cored
        rows = kept.shape[0] // 4
        cut = rows // 2
        far = (kept[3 * rows :] + received[3 * rows :].astype(jnp.float32)).astype(jnp.bfloat16)
        return (kept, received, to_chip(far[:cut]), to_pair(far[cut:]))

    def fold_open(crossed):
        kept, received, from_chip, from_pair = crossed
        rows = kept.shape[0] // 4
        cut = rows // 2
        own, across, beside = [
            kept[i * rows : (i + 1) * rows]
            + received[i * rows : (i + 1) * rows].astype(jnp.float32)
            for i in range(3)
        ]
        across = jnp.concatenate([across[:cut], across[cut:] + from_pair.astype(jnp.float32)])
        beside = jnp.concatenate([beside[:cut] + from_chip.astype(jnp.float32), beside[cut:]])
        return (
            own,
            to_chip(across.astype(jnp.bfloat16)),
            to_pair(beside.astype(jnp.bfloat16)),
        )

    def fold_sum(opened):
        own, from_chip, from_pair = opened
        return own + from_chip.astype(jnp.float32) + from_pair.astype(jnp.float32)

    def plane_share(share):
        place = lax.axis_index("tp")
        rows, count = share.shape[0] // 4, share.shape[1]
        split = share.reshape(2, 2, rows, count)
        split = jnp.where(place // 2 == 0, split, split[::-1])
        split = jnp.where(place % 2 == 0, split, split[:, ::-1]).swapaxes(0, 1)
        return jnp.stack([split, to_pair(split)], axis=1).reshape(8 * rows, count)

    def column_gather(own):
        return lax.all_gather(own, "fsdp", axis=0, tiled=True, axis_index_groups=columns)

    def column_scatter(full):
        return lax.psum_scatter(
            full, "fsdp", scatter_dimension=0, tiled=True, axis_index_groups=columns
        )

    def weight_join(mine, theirs):
        pair_bit = lax.axis_index("fsdp") % 2
        rows, width = mine.shape[0] // (fsdp_size // 2), mine.shape[1]
        mine = mine.reshape(fsdp_size // 2, 1, rows, width)
        theirs = theirs.reshape(fsdp_size // 2, 1, rows, width)
        return jnp.concatenate(
            [jnp.where(pair_bit == 0, mine, theirs), jnp.where(pair_bit == 0, theirs, mine)],
            axis=1,
        ).reshape(fsdp_size * rows, width)

    def pair_columns(values):
        pair_bit = lax.axis_index("fsdp") % 2
        width = values.shape[1] // fsdp_size
        return [
            jnp.concatenate(
                [
                    lax.dynamic_slice_in_dim(values, (2 * place + bit) * width, width, 1)
                    for place in range(fsdp_size // 2)
                ],
                axis=1,
            )
            for bit in (pair_bit, 1 - pair_bit)
        ]

    def weight_reduce(pairs):
        summed = [
            (kept + received.astype(jnp.float32)).astype(jnp.bfloat16) for kept, received in pairs
        ]
        return column_scatter(jnp.concatenate(summed, axis=1)).astype(jnp.float32)

    def sum_all(values):
        for step in range(tp_size.bit_length() - 1):
            swap = [(i, i ^ (1 << step)) for i in range(tp_size)]
            values = values + lax.ppermute(values, "tp", swap)
        for step in range(fsdp_size.bit_length() - 1):
            swap = [(i, i ^ (1 << step)) for i in range(fsdp_size)]
            values = values + lax.ppermute(values, "fsdp", swap)
        return values

    return (
        to_pair,
        to_core,
        to_chip,
        tp_both,
        tp_join,
        tp_gather,
        tp_split,
        tp_halve,
        tp_sum,
        tp_scatter,
        plane_open,
        plane_cross,
        plane_core,
        plane_join,
        fold_core,
        fold_cross,
        fold_open,
        fold_sum,
        plane_share,
        column_gather,
        column_scatter,
        weight_join,
        pair_columns,
        weight_reduce,
        sum_all,
    )


def per_device(
    fsdp_size,
    tp_size,
    tokens,
    cotangent,
    segments,
    routes,
    gate_logits,
    attention_gain,
    feedforward_gain,
    query_gain,
    key_gain,
    query_weight,
    key_weight,
    value_weight,
    out_weight,
    gate_weight,
    up_weight,
    down_weight,
):
    (
        to_pair,
        to_core,
        to_chip,
        tp_both,
        tp_join,
        tp_gather,
        tp_split,
        tp_halve,
        tp_sum,
        tp_scatter,
        plane_open,
        plane_cross,
        plane_core,
        plane_join,
        fold_core,
        fold_cross,
        fold_open,
        fold_sum,
        plane_share,
        column_gather,
        column_scatter,
        weight_join,
        pair_columns,
        weight_reduce,
        sum_all,
    ) = make_moves(fsdp_size, tp_size)
    pair_bit = lax.axis_index("fsdp") % 2
    head_size = query_gain.shape[0]
    kv_count = key_weight.shape[1] // head_size
    query_count = query_weight.shape[1] // head_size
    weight_rows, expert_count, expert_width = gate_weight.shape
    half_experts = expert_count // 2
    half_width = half_experts * expert_width
    part_width = half_width // PARTS
    rows_all = segments.shape[0]
    cosine, sine_table = rope_tables(SEQ, head_size)
    turn_sign = jnp.where(jnp.arange(head_size) < head_size // 2, -1.0, 1.0)
    tables = (
        cosine,
        sine_table * turn_sign,
        segments.reshape(rows_all, 1),
        segments.reshape(1, rows_all),
        query_gain.reshape(1, head_size),
        key_gain.reshape(1, head_size),
    )
    token_rows = tokens.astype(jnp.float32)
    first_norm, first_inverse = norm_rows(token_rows, attention_gain)
    last = []

    def step(value):
        if last:
            value = lax.optimization_barrier((value, last[0]))[0]
        last[:] = [value]
        return value

    def after(value, *earlier):
        return lax.optimization_barrier((value, earlier))[0]

    def exchange(reduced):
        kept, sent = halves(reduced, pair_bit)
        return (kept, to_pair(sent))

    gate_probs = jax.nn.softmax(gate_logits, axis=-1)
    expert_ids = jnp.arange(expert_count, dtype=jnp.int32)
    share_own = jnp.sum(
        jnp.where(routes[:, :, None] == expert_ids[None, None, :], gate_probs[:, :, None], 0.0),
        axis=1,
    )
    share_group = plane_share(share_own)
    share_half = lax.dynamic_slice_in_dim(share_group, pair_bit * half_experts, half_experts, 1)
    span = half_experts // PARTS
    share_wide = [
        jnp.repeat(share_half[:, part * span : (part + 1) * span], expert_width, axis=1)
        for part in range(PARTS)
    ]
    query_width = query_count * head_size
    key_width = kv_count * head_size
    model_width = tokens.shape[1]
    three_width = query_width + 2 * key_width
    attention_mine = column_gather(
        jnp.concatenate([query_weight, key_weight, value_weight, out_weight], axis=1)
    )

    def flat(weight):
        return weight.reshape(weight_rows, 2, PARTS, part_width)

    flats = (flat(gate_weight), flat(up_weight), flat(down_weight))

    def side(part, bit):
        return jnp.concatenate(
            [lax.dynamic_index_in_dim(w[:, :, part], bit, 1, False) for w in flats], axis=1
        )

    def fetched(part, received):
        whole = joined(side(part, pair_bit), received, pair_bit)
        if part == 0:
            whole = column_gather(whole)
            return [whole[:, : 2 * part_width], whole[:, 2 * part_width :]]
        return [
            column_gather(whole[:, : 2 * part_width]),
            column_gather(whole[:, 2 * part_width :]),
        ]

    first_low = first_norm.astype(jnp.bfloat16)
    first_chip = to_chip(first_low)
    swapped = to_pair(after(side(0, 1 - pair_bit), share_group))
    share_wide = step(share_wide)
    first_both = tp_both(first_low, step(first_chip))
    first_full = tp_join(first_both, step(to_core(first_both)))
    expert_weights = [fetched(0, step(swapped))]
    cotangent_open = step(plane_open(after(cotangent, first_both)))
    attention_mine = step(attention_mine)
    three_mine = attention_mine[:, :three_width]
    out_mine = attention_mine[:, three_width:]
    three_theirs = to_pair(three_mine)
    three_theirs = step(three_theirs)
    out_theirs = to_pair(after(out_mine, three_theirs))
    query_key_value = weight_join(three_mine, three_theirs)
    projected = matmul(first_full, query_key_value)
    heads_low = step(attend(projected, tables, query_count, kv_count, head_size))
    out_theirs = step(out_theirs)
    cotangent_cross = plane_cross(after(cotangent_open, out_theirs))
    full_out = weight_join(out_mine, out_theirs)
    attn_split = step(tp_split(times_transposed(heads_low, full_out)))
    received = to_pair(after(side(1, 1 - pair_bit), out_theirs))
    attn_halved = step(tp_halve(attn_split))
    middle = token_rows + tp_sum(attn_halved)
    second_norm, second_inverse = norm_rows(middle, feedforward_gain)
    second_low = second_norm.astype(jnp.bfloat16)
    second_open = plane_open(second_low)
    for part in range(1, PARTS):
        received = step(received)
        expert_weights.append(fetched(part, received))
        if part + 1 < PARTS:
            received = to_pair(after(side(part + 1, 1 - pair_bit), received))
    cotangent_core = plane_core(cotangent, cotangent_open, step(cotangent_cross))
    expert_weights[0][0] = step(expert_weights[0][0])
    second_cross = step(plane_cross(step(second_open)))
    second_core = plane_core(second_low, second_open, second_cross)
    grad_group = plane_join(step(cotangent_core))
    second_group = plane_join(step(second_core))
    weight_terms = []
    for part in range(PARTS):
        weight_in, weight_down = expert_weights[part]
        share = share_wide[part]
        both_pre = matmul(second_group, weight_in)
        gate_pre, up_pre = both_pre[:, :part_width], both_pre[:, part_width:]
        sigmoid_gate = jax.nn.sigmoid(gate_pre)
        silu_gate = gate_pre * sigmoid_gate
        hidden = (silu_gate * up_pre * share).astype(jnp.bfloat16)
        hidden_grad = matmul(grad_group, weight_down) * share
        up_grad = (hidden_grad * silu_gate).astype(jnp.bfloat16)
        gate_grad = (
            hidden_grad * up_pre * sigmoid_gate * (1.0 + gate_pre * (1.0 - sigmoid_gate))
        ).astype(jnp.bfloat16)
        both_grad = jnp.concatenate([gate_grad, up_grad], axis=1)
        if part < PARTS - 1:
            down_term = step(inner_rows(grad_group, hidden).astype(jnp.bfloat16))
            expert_weights[part + 1][0] = step(expert_weights[part + 1][0])
            both_late = after(both_grad, down_term)
            weight_term = jnp.concatenate(
                [inner_rows(second_group, both_late).astype(jnp.bfloat16), down_term], axis=1
            )
            hidden_late, both_late = after((hidden, both_grad), weight_term)
            second_part = step(times_transposed(both_late, weight_in))
            expert_weights[part + 1][1] = step(expert_weights[part + 1][1])
            moe_part = times_transposed(hidden_late, weight_down)
            moe_sum = moe_part if part == 0 else moe_sum + moe_part
            second_sum = second_part if part == 0 else second_sum + second_part
            moe_sum, second_sum = lax.optimization_barrier((moe_sum, second_sum))
        else:
            second_sent = second_sum[rows_all:] + times_transposed(
                both_grad[rows_all:], weight_in
            )
            second_sent = step(second_sent.astype(jnp.bfloat16))
            second_kept = second_sum[:rows_all] + times_transposed(
                after(both_grad, second_sent)[:rows_all], weight_in
            )
            hidden, both_grad = after((hidden, both_grad), second_kept)
            moe_hidden = hidden
            moe_sent = moe_sum[rows_all:] + times_transposed(hidden[rows_all:], weight_down)
            moe_sent = moe_sent.astype(jnp.bfloat16)
            weight_term = jnp.concatenate(
                [
                    inner_rows(second_group, both_grad).astype(jnp.bfloat16),
                    inner_rows(grad_group, hidden).astype(jnp.bfloat16),
                ],
                axis=1,
            )
        weight_terms.append(weight_term)

    second_fold = fold_cross(step(fold_core(second_kept, second_sent)))
    second_fold = fold_open(step(second_fold))
    second_fold, weight_terms[-1] = step((second_fold, weight_terms[-1]))
    reduced = [column_scatter(term) for term in weight_terms]
    second_grad = fold_sum(second_fold)
    middle_back, feedforward_gain_grad = norm_back(
        middle, second_inverse, feedforward_gain, second_grad
    )
    middle_grad = cotangent.astype(jnp.float32) + middle_back
    grad_low = middle_grad.astype(jnp.bfloat16)
    grad_chip = to_chip(grad_low)
    first_kept, first_sent = pair_columns(after(first_full, grad_low))
    grad_chip, first_sent, moe_sent = step((grad_chip, first_sent, moe_sent))
    grad_both = tp_both(grad_low, grad_chip)
    owned_parts = [step(exchange(after(reduced[0], grad_low)))]
    attn_grad_full = tp_join(grad_both, step(to_core(grad_both)))
    moe_received = to_core(after(moe_sent, attn_grad_full))
    heads_grad = matmul(attn_grad_full, full_out).astype(jnp.bfloat16)
    grad_kept, grad_sent = pair_columns(attn_grad_full)
    out_sent = inner_rows(grad_sent, heads_low).astype(jnp.bfloat16)
    heads_grad, out_sent = step((heads_grad, out_sent))
    out_received = to_pair(out_sent)
    projected_grad, query_gain_grad, key_gain_grad = step(
        attend_back(projected, heads_grad, tables, query_count, kv_count, head_size)
    )
    projected_sent = step(inner_rows(first_sent, projected_grad).astype(jnp.bfloat16))
    projected_received = to_pair(projected_sent)
    out_kept = inner_rows(after(grad_kept, projected_sent), heads_low)
    out_received = step(out_received)
    projected_kept = step(inner_rows(first_kept, projected_grad))
    first_split = tp_split(
        times_transposed(after(projected_grad, projected_kept), query_key_value)
    )
    first_halved = tp_halve(step(first_split))
    projected_received = step(projected_received)
    attention_owned = weight_reduce(
        [(projected_kept, projected_received), (out_kept, out_received)]
    )
    moe_hidden = after(moe_hidden, projected_kept)
    moe_kept = moe_sum[:rows_all] + times_transposed(moe_hidden[:rows_all], weight_down)
    owned_parts.append(step(exchange(after(reduced[1], projected_received))))
    moe_fold = fold_cross((moe_kept, after(moe_received, projected_received)))
    moe_fold = fold_open(step(moe_fold))
    first_grad = tp_sum(step(first_halved))
    output = (middle + fold_sum(step(moe_fold))).astype(jnp.bfloat16)

    def owned(index):
        place = slice(index * part_width, (index + 1) * part_width)
        mine = jnp.concatenate([kept[:, place] for kept, sent in owned_parts], axis=1)
        theirs = jnp.concatenate([sent[:, place] for kept, sent in owned_parts], axis=1)
        return (
            jnp.concatenate(
                [
                    jnp.where(pair_bit == 0, mine, theirs),
                    jnp.where(pair_bit == 0, theirs, mine),
                ],
                axis=1,
            )
            .astype(jnp.float32)
            .reshape(weight_rows, expert_count, expert_width)
        )

    rows_back, attention_gain_grad = norm_back(
        token_rows, first_inverse, attention_gain, first_grad
    )
    tokens_grad = middle_grad + rows_back
    gain_sums = sum_all(
        jnp.concatenate(
            [
                attention_gain_grad,
                feedforward_gain_grad,
                query_gain_grad.reshape(head_size),
                key_gain_grad.reshape(head_size),
            ]
        )
    )
    gain_sums = jnp.split(
        gain_sums,
        [model_width, 2 * model_width, 2 * model_width + head_size],
    )
    return (
        output,
        tokens_grad,
        gain_sums[0],
        gain_sums[1],
        gain_sums[2],
        gain_sums[3],
        attention_owned[:, :query_width],
        attention_owned[:, query_width : query_width + key_width],
        attention_owned[:, query_width + key_width : three_width],
        attention_owned[:, three_width:],
        owned(0),
        owned(1),
        owned(2),
    )


def solution(mesh):
    placed = (
        P(("fsdp", "tp"), None),
        P(("fsdp", "tp"), None),
        P("fsdp"),
        P("fsdp", None),
        P("fsdp", None),
        P(),
        P(),
        P(),
        P(),
        P("fsdp", "tp"),
        P("fsdp", "tp"),
        P("fsdp", "tp"),
        P("fsdp", "tp"),
        P("fsdp", None, "tp"),
        P("fsdp", None, "tp"),
        P("fsdp", None, "tp"),
    )
    return jax.shard_map(
        partial(per_device, mesh.shape["fsdp"], mesh.shape["tp"]),
        mesh=mesh,
        in_specs=placed,
        out_specs=(
            P(("fsdp", "tp"), None),
            P(("fsdp", "tp"), None),
            P(),
            P(),
            P(),
            P(),
            P("fsdp", "tp"),
            P("fsdp", "tp"),
            P("fsdp", "tp"),
            P("fsdp", "tp"),
            P("fsdp", None, "tp"),
            P("fsdp", None, "tp"),
            P("fsdp", None, "tp"),
        ),
        check_vma=False,
    )
```

```python
from functools import partial

import jax
import jax.numpy as jnp
from jax import lax
from jax.experimental import pallas as pl
from jax.experimental.pallas import tpu as pltpu
from jax.sharding import PartitionSpec as P

SEQ = 1024
TILE = 256
PARTS = 2
VMEM_BYTES = 48 * 1024 * 1024


eps_norm = 1e-06
rope_base = 1000000.0


def matmul(left_side, right_side):
    return jnp.dot(left_side, right_side, preferred_element_type=jnp.float32)


def times_transposed(left_side, right_side):
    return lax.dot_general(
        left_side, right_side, (((1,), (1,)), ((), ())), preferred_element_type=jnp.float32
    )


def inner_rows(left_side, right_side):
    return lax.dot_general(
        left_side, right_side, (((0,), (0,)), ((), ())), preferred_element_type=jnp.float32
    )


def norm_rows(values, scale_gain):
    inverse = lax.rsqrt(jnp.mean(values * values, axis=-1, keepdims=True) + eps_norm)
    return (values * inverse * scale_gain, inverse)


def norm_back(values, inverse, scale_gain, incoming):
    normed = values * inverse
    scaled_grad = incoming * scale_gain
    gain_grad = jnp.sum(incoming * normed, axis=tuple(range(values.ndim - 1)))
    result = inverse * (
        scaled_grad - normed * jnp.mean(scaled_grad * normed, axis=-1, keepdims=True)
    )
    return (result, gain_grad)


def rope_tables(row_count, head_size):
    positions = jnp.arange(row_count, dtype=jnp.float32)
    frequencies = rope_base ** (-jnp.arange(0, head_size, 2, dtype=jnp.float32) / head_size)
    angles = positions[:, None] * frequencies[None, :]
    angles = jnp.concatenate([angles, angles], axis=-1)
    return (jnp.cos(angles), jnp.sin(angles))


def head_norm(values):
    inverse = lax.rsqrt(jnp.mean(values * values, axis=-1, keepdims=True) + eps_norm)
    return (values * inverse, inverse)


def turn(values, cosine, signed_sine):
    half_size = values.shape[-1] // 2
    return values * cosine + pltpu.roll(values, half_size, 1) * signed_sine


def turn_back(incoming, cosine, signed_sine):
    half_size = incoming.shape[-1] // 2
    return incoming * cosine + pltpu.roll(incoming * signed_sine, half_size, 1)


def masked_probs(query_tile, key_rows, row_ids, column_ids, offset, scaling):
    scores = times_transposed(query_tile, key_rows) * scaling
    row_place = lax.broadcasted_iota(jnp.int32, scores.shape, 0) + offset
    column_place = lax.broadcasted_iota(jnp.int32, scores.shape, 1)
    allowed = (column_place <= row_place) & (row_ids == column_ids)
    scores = jnp.where(allowed, scores, -jnp.inf)
    weights = jnp.exp(scores - jnp.max(scores, axis=-1, keepdims=True))
    return weights * (1.0 / jnp.sum(weights, axis=-1, keepdims=True))


def attend_kernel(
    group_size,
    query_ref,
    key_ref,
    value_ref,
    cosine_ref,
    sine_ref,
    row_ids_ref,
    column_ids_ref,
    query_gain_ref,
    key_gain_ref,
    heads_ref,
    key_low,
    value_low,
):
    head_size = query_ref.shape[1]
    scaling = head_size ** (-0.5)

    @pl.when(lax.rem(pl.program_id(1), group_size) == 0)
    def prepare():
        normed, unused = head_norm(key_ref[...])
        key_low[...] = turn(normed * key_gain_ref[...], cosine_ref[...], sine_ref[...]).astype(
            jnp.bfloat16
        )
        value_low[...] = value_ref[...].astype(jnp.bfloat16)

    for offset in range(0, SEQ, TILE):
        finish = offset + TILE
        rows = pl.ds(offset, TILE)
        normed, unused = head_norm(query_ref[rows, :])
        query_tile = turn(
            normed * query_gain_ref[...], cosine_ref[rows, :], sine_ref[rows, :]
        ).astype(jnp.bfloat16)
        probs = masked_probs(
            query_tile,
            key_low[:finish, :],
            row_ids_ref[rows, :],
            column_ids_ref[:, :finish],
            offset,
            scaling,
        )
        heads_ref[rows, :] = matmul(probs.astype(jnp.bfloat16), value_low[:finish, :]).astype(
            jnp.bfloat16
        )


def attend_back_kernel(
    query_count,
    kv_count,
    query_ref,
    key_ref,
    value_ref,
    grad_ref,
    cosine_ref,
    sine_ref,
    row_ids_ref,
    column_ids_ref,
    query_gain_ref,
    key_gain_ref,
    projected_ref,
    query_gain_grad_ref,
    key_gain_grad_ref,
    key_low,
    value_low,
    key_sum,
    value_sum,
):
    head_size = query_ref.shape[1]
    scaling = head_size ** (-0.5)
    group_size = query_count // kv_count
    head = pl.program_id(1)
    place = lax.rem(head, group_size)

    @pl.when((pl.program_id(0) == 0) & (head == 0))
    def clear():
        query_gain_grad_ref[...] = jnp.zeros_like(query_gain_grad_ref)
        key_gain_grad_ref[...] = jnp.zeros_like(key_gain_grad_ref)

    @pl.when(place == 0)
    def prepare():
        normed, unused = head_norm(key_ref[...])
        key_low[...] = turn(normed * key_gain_ref[...], cosine_ref[...], sine_ref[...]).astype(
            jnp.bfloat16
        )
        value_low[...] = value_ref[...].astype(jnp.bfloat16)
        key_sum[...] = jnp.zeros_like(key_sum)
        value_sum[...] = jnp.zeros_like(value_sum)

    def through_norm(turned_grad, cosine, signed_sine, normed, inverse, gain):
        incoming = turn_back(turned_grad, cosine, signed_sine)
        scaled_grad = incoming * gain
        result = inverse * (
            scaled_grad - normed * jnp.mean(scaled_grad * normed, axis=-1, keepdims=True)
        )
        return (result, jnp.sum(incoming * normed, axis=0, keepdims=True))

    columns = pl.ds(pl.multiple_of(head * head_size, head_size), head_size)
    for offset in range(0, SEQ, TILE):
        finish = offset + TILE
        rows = pl.ds(offset, TILE)
        cosine, signed_sine = cosine_ref[rows, :], sine_ref[rows, :]
        normed, inverse = head_norm(query_ref[rows, :])
        query_tile = turn(normed * query_gain_ref[...], cosine, signed_sine).astype(jnp.bfloat16)
        grad_tile = grad_ref[rows, :]
        key_rows = key_low[:finish, :]
        probs = masked_probs(
            query_tile,
            key_rows,
            row_ids_ref[rows, :],
            column_ids_ref[:, :finish],
            offset,
            scaling,
        )
        prob_grad = times_transposed(grad_tile, value_low[:finish, :])
        score_grad = (
            probs * (prob_grad - jnp.sum(probs * prob_grad, axis=-1, keepdims=True))
        ).astype(jnp.bfloat16)
        value_sum[:finish, :] += inner_rows(probs.astype(jnp.bfloat16), grad_tile)
        key_sum[:finish, :] += inner_rows(score_grad, query_tile)
        result, gain_grad = through_norm(
            matmul(score_grad, key_rows) * scaling,
            cosine,
            signed_sine,
            normed,
            inverse,
            query_gain_ref[...],
        )
        projected_ref[rows, columns] = result.astype(jnp.bfloat16)
        query_gain_grad_ref[...] += gain_grad

    @pl.when(place == group_size - 1)
    def finish_group():
        group = lax.div(head, group_size)
        normed, inverse = head_norm(key_ref[...])
        result, gain_grad = through_norm(
            key_sum[...] * scaling,
            cosine_ref[...],
            sine_ref[...],
            normed,
            inverse,
            key_gain_ref[...],
        )
        key_columns = pl.ds(
            pl.multiple_of((query_count + group) * head_size, head_size), head_size
        )
        value_columns = pl.ds(
            pl.multiple_of((query_count + kv_count + group) * head_size, head_size), head_size
        )
        projected_ref[:, key_columns] = result.astype(jnp.bfloat16)
        projected_ref[:, value_columns] = value_sum[...].astype(jnp.bfloat16)
        key_gain_grad_ref[...] += gain_grad


def attention_specs(query_count, kv_count, head_size):
    group_size = query_count // kv_count
    block = (SEQ, head_size)
    fixed = lambda shape: pl.BlockSpec(shape, lambda s, h: (0, 0))
    operands = [
        pl.BlockSpec(block, lambda s, h: (s, h)),
        pl.BlockSpec(block, lambda s, h: (s, query_count + h // group_size)),
        pl.BlockSpec(block, lambda s, h: (s, query_count + kv_count + h // group_size)),
    ]
    tables = [
        fixed(block),
        fixed(block),
        pl.BlockSpec((SEQ, 1), lambda s, h: (s, 0)),
        pl.BlockSpec((1, SEQ), lambda s, h: (0, s)),
        fixed((1, head_size)),
        fixed((1, head_size)),
    ]
    return (operands, tables)


def attend(projected, tables, query_count, kv_count, head_size):
    rows = projected.shape[0]
    operands, table_specs = attention_specs(query_count, kv_count, head_size)
    pairs = rows * SEQ * query_count * 5 // 8
    return pl.pallas_call(
        partial(attend_kernel, query_count // kv_count),
        grid=(rows // SEQ, query_count),
        in_specs=operands + table_specs,
        out_specs=pl.BlockSpec((SEQ, head_size), lambda s, h: (s, h)),
        out_shape=jax.ShapeDtypeStruct((rows, query_count * head_size), jnp.bfloat16),
        scratch_shapes=[
            pltpu.VMEM((SEQ, head_size), jnp.bfloat16),
            pltpu.VMEM((SEQ, head_size), jnp.bfloat16),
        ],
        compiler_params=pltpu.CompilerParams(vmem_limit_bytes=VMEM_BYTES),
        cost_estimate=pl.CostEstimate(
            flops=60 * pairs * head_size,
            bytes_accessed=6 * rows * query_count * head_size,
            transcendentals=pairs,
        ),
        name="attend",
    )(projected, projected, projected, *tables)


def attend_back(projected, heads_grad, tables, query_count, kv_count, head_size):
    rows = projected.shape[0]
    width = projected.shape[1]
    operands, table_specs = attention_specs(query_count, kv_count, head_size)
    pairs = rows * SEQ * query_count * 5 // 8
    return pl.pallas_call(
        partial(attend_back_kernel, query_count, kv_count),
        grid=(rows // SEQ, query_count),
        in_specs=operands + [pl.BlockSpec((SEQ, head_size), lambda s, h: (s, h))] + table_specs,
        out_specs=[
            pl.BlockSpec((SEQ, width), lambda s, h: (s, 0)),
            pl.BlockSpec((1, head_size), lambda s, h: (0, 0)),
            pl.BlockSpec((1, head_size), lambda s, h: (0, 0)),
        ],
        out_shape=[
            jax.ShapeDtypeStruct((rows, width), jnp.bfloat16),
            jax.ShapeDtypeStruct((1, head_size), jnp.float32),
            jax.ShapeDtypeStruct((1, head_size), jnp.float32),
        ],
        scratch_shapes=[
            pltpu.VMEM((SEQ, head_size), jnp.bfloat16),
            pltpu.VMEM((SEQ, head_size), jnp.bfloat16),
            pltpu.VMEM((SEQ, head_size), jnp.float32),
            pltpu.VMEM((SEQ, head_size), jnp.float32),
        ],
        compiler_params=pltpu.CompilerParams(vmem_limit_bytes=VMEM_BYTES),
        cost_estimate=pl.CostEstimate(
            flops=90 * pairs * head_size,
            bytes_accessed=10 * rows * query_count * head_size,
            transcendentals=pairs,
        ),
        name="attend_back",
    )(projected, projected, projected, heads_grad, *tables)


def joined(own, other, bit):
    first_half = jnp.where(bit == 0, own, other)
    last_half = jnp.where(bit == 0, other, own)
    return jnp.concatenate([first_half, last_half], axis=0)


def halves(values, bit):
    rows = values.shape[0] // 2
    kept = lax.dynamic_slice_in_dim(values, bit * rows, rows, 0)
    sent = lax.dynamic_slice_in_dim(values, (1 - bit) * rows, rows, 0)
    return (kept, sent)


def make_moves(fsdp_size, tp_size):
    swap_core = [(i, i ^ 1) for i in range(tp_size)]
    swap_chip = [(i, (i + 2) % tp_size) for i in range(tp_size)]
    swap_pair = [(i, i ^ 1) for i in range(fsdp_size)]
    columns = [list(range(b, fsdp_size, 2)) for b in range(2)]

    def to_core(values):
        return lax.ppermute(values, "tp", swap_core)

    def to_chip(values):
        return lax.ppermute(values, "tp", swap_chip)

    def to_pair(values):
        return lax.ppermute(values, "fsdp", swap_pair)

    def tp_both(own, received):
        return joined(own, received, lax.axis_index("tp") // 2)

    def tp_join(both, others):
        place = lax.axis_index("tp")
        rows, width = both.shape[0] // 2, both.shape[1]
        both = both.reshape(2, 1, rows, width)
        others = others.reshape(2, 1, rows, width)
        first_core = jnp.where(place % 2 == 0, both, others)
        last_core = jnp.where(place % 2 == 0, others, both)
        return jnp.concatenate([first_core, last_core], axis=1).reshape(4 * rows, width)

    def tp_gather(own):
        both = tp_both(own, to_chip(own))
        return tp_join(both, to_core(both))

    def tp_split(full):
        place = lax.axis_index("tp")
        rows, width = full.shape[0] // 4, full.shape[1]
        split = full.reshape(2, 2, rows, width)
        kept = lax.dynamic_index_in_dim(split, place % 2, 1, False)
        sent = lax.dynamic_index_in_dim(split, 1 - place % 2, 1, False).astype(jnp.bfloat16)
        return (kept, to_core(sent))

    def tp_halve(split):
        kept, received = split
        kept, sent = halves(kept + received.astype(jnp.float32), lax.axis_index("tp") // 2)
        return (kept, to_chip(sent.astype(jnp.bfloat16)))

    def tp_sum(halved):
        kept, received = halved
        return (kept + received.astype(jnp.float32)).reshape(kept.shape[1:])

    def tp_scatter(full):
        return tp_sum(tp_halve(tp_split(full)))

    def plane_open(own):
        return (to_chip(own), to_pair(own))

    def plane_cross(opened):
        across, beside = opened
        cut = across.shape[0] // 2
        return (to_chip(beside[:cut]), to_pair(across[cut:]))

    def plane_core(own, opened, crossed):
        mine = jnp.concatenate([own, *opened, *crossed], axis=0)
        return (mine, to_core(mine))

    def plane_join(cored):
        return jnp.concatenate(cored, axis=0)

    def plane_gather(own):
        opened = plane_open(own)
        return plane_join(plane_core(own, opened, plane_cross(opened)))

    def fold_core(kept, sent):
        return (kept, to_core(sent))

    def fold_cross(cored):
        kept, received = cored
        rows = kept.shape[0] // 4
        cut = rows // 2
        far = (kept[3 * rows :] + received[3 * rows :].astype(jnp.float32)).astype(jnp.bfloat16)
        return (kept, received, to_chip(far[:cut]), to_pair(far[cut:]))

    def fold_open(crossed):
        kept, received, from_chip, from_pair = crossed
        rows = kept.shape[0] // 4
        cut = rows // 2
        own, across, beside = [
            kept[i * rows : (i + 1) * rows]
            + received[i * rows : (i + 1) * rows].astype(jnp.float32)
            for i in range(3)
        ]
        across = jnp.concatenate([across[:cut], across[cut:] + from_pair.astype(jnp.float32)])
        beside = jnp.concatenate([beside[:cut] + from_chip.astype(jnp.float32), beside[cut:]])
        return (
            own,
            to_chip(across.astype(jnp.bfloat16)),
            to_pair(beside.astype(jnp.bfloat16)),
        )

    def fold_sum(opened):
        own, from_chip, from_pair = opened
        return own + from_chip.astype(jnp.float32) + from_pair.astype(jnp.float32)

    def plane_share(share):
        place = lax.axis_index("tp")
        rows, count = share.shape[0] // 4, share.shape[1]
        split = share.reshape(2, 2, rows, count)
        split = jnp.where(place // 2 == 0, split, split[::-1])
        split = jnp.where(place % 2 == 0, split, split[:, ::-1]).swapaxes(0, 1)
        return jnp.stack([split, to_pair(split)], axis=1).reshape(8 * rows, count)

    def column_gather(own):
        return lax.all_gather(own, "fsdp", axis=0, tiled=True, axis_index_groups=columns)

    def column_scatter(full):
        return lax.psum_scatter(
            full, "fsdp", scatter_dimension=0, tiled=True, axis_index_groups=columns
        )

    def weight_join(mine, theirs):
        pair_bit = lax.axis_index("fsdp") % 2
        rows, width = mine.shape[0] // (fsdp_size // 2), mine.shape[1]
        mine = mine.reshape(fsdp_size // 2, 1, rows, width)
        theirs = theirs.reshape(fsdp_size // 2, 1, rows, width)
        return jnp.concatenate(
            [jnp.where(pair_bit == 0, mine, theirs), jnp.where(pair_bit == 0, theirs, mine)],
            axis=1,
        ).reshape(fsdp_size * rows, width)

    def column_shift(values):
        pairs = [(i, (i + 2) % fsdp_size) for i in range(fsdp_size)]
        return lax.ppermute(values, "fsdp", pairs)

    def column_place(whole, piece, offset):
        count = fsdp_size // 2
        place = (lax.axis_index("fsdp") // 2 - offset) % count
        return lax.dynamic_update_index_in_dim(whole, piece, place, 0)

    def pair_columns(values):
        pair_bit = lax.axis_index("fsdp") % 2
        width = values.shape[1] // fsdp_size
        return [
            jnp.concatenate(
                [
                    lax.dynamic_slice_in_dim(values, (2 * place + bit) * width, width, 1)
                    for place in range(fsdp_size // 2)
                ],
                axis=1,
            )
            for bit in (pair_bit, 1 - pair_bit)
        ]

    def weight_reduce(pairs):
        summed = [
            (kept + received.astype(jnp.float32)).astype(jnp.bfloat16) for kept, received in pairs
        ]
        return column_scatter(jnp.concatenate(summed, axis=1))

    def sum_all(values):
        for step in range(tp_size.bit_length() - 1):
            swap = [(i, i ^ (1 << step)) for i in range(tp_size)]
            values = values + lax.ppermute(values, "tp", swap)
        for step in range(fsdp_size.bit_length() - 1):
            swap = [(i, i ^ (1 << step)) for i in range(fsdp_size)]
            values = values + lax.ppermute(values, "fsdp", swap)
        return values

    return (
        to_pair,
        to_core,
        to_chip,
        tp_both,
        tp_join,
        tp_gather,
        tp_split,
        tp_halve,
        tp_sum,
        tp_scatter,
        plane_open,
        plane_cross,
        plane_core,
        plane_join,
        fold_core,
        fold_cross,
        fold_open,
        fold_sum,
        plane_share,
        column_gather,
        column_scatter,
        weight_join,
        column_shift,
        column_place,
        pair_columns,
        weight_reduce,
        sum_all,
    )


def per_device(
    fsdp_size,
    tp_size,
    tokens,
    cotangent,
    segments,
    routes,
    gate_logits,
    attention_gain,
    feedforward_gain,
    query_gain,
    key_gain,
    query_weight,
    key_weight,
    value_weight,
    out_weight,
    gate_weight,
    up_weight,
    down_weight,
):
    (
        to_pair,
        to_core,
        to_chip,
        tp_both,
        tp_join,
        tp_gather,
        tp_split,
        tp_halve,
        tp_sum,
        tp_scatter,
        plane_open,
        plane_cross,
        plane_core,
        plane_join,
        fold_core,
        fold_cross,
        fold_open,
        fold_sum,
        plane_share,
        column_gather,
        column_scatter,
        weight_join,
        column_shift,
        column_place,
        pair_columns,
        weight_reduce,
        sum_all,
    ) = make_moves(fsdp_size, tp_size)
    pair_bit = lax.axis_index("fsdp") % 2
    head_size = query_gain.shape[0]
    kv_count = key_weight.shape[1] // head_size
    query_count = query_weight.shape[1] // head_size
    weight_rows, expert_count, expert_width = gate_weight.shape
    half_experts = expert_count // 2
    half_width = half_experts * expert_width
    part_width = half_width // PARTS
    rows_all = segments.shape[0]
    cosine, sine_table = rope_tables(SEQ, head_size)
    turn_sign = jnp.where(jnp.arange(head_size) < head_size // 2, -1.0, 1.0)
    tables = (
        cosine,
        sine_table * turn_sign,
        segments.reshape(rows_all, 1),
        segments.reshape(1, rows_all),
        query_gain.reshape(1, head_size),
        key_gain.reshape(1, head_size),
    )
    token_rows = tokens.astype(jnp.float32)
    first_norm, first_inverse = norm_rows(token_rows, attention_gain)
    last = []

    def step(value):
        if last:
            value = lax.optimization_barrier((value, last[0]))[0]
        last[:] = [value]
        return value

    def after(value, *earlier):
        return lax.optimization_barrier((value, earlier))[0]

    def exchange(reduced):
        kept, sent = halves(reduced, pair_bit)
        return (kept, to_pair(sent))

    gate_probs = jax.nn.softmax(gate_logits, axis=-1)
    expert_ids = jnp.arange(expert_count, dtype=jnp.int32)
    share_own = jnp.sum(
        jnp.where(routes[:, :, None] == expert_ids[None, None, :], gate_probs[:, :, None], 0.0),
        axis=1,
    )
    share_group = plane_share(share_own)
    share_half = lax.dynamic_slice_in_dim(share_group, pair_bit * half_experts, half_experts, 1)
    span = half_experts // PARTS
    share_wide = [
        jnp.repeat(share_half[:, part * span : (part + 1) * span], expert_width, axis=1)
        for part in range(PARTS)
    ]
    query_width = query_count * head_size
    key_width = kv_count * head_size
    model_width = tokens.shape[1]
    three_width = query_width + 2 * key_width
    column_count = fsdp_size // 2
    three_own = jnp.concatenate([query_weight, key_weight, value_weight], axis=1)

    def flat(weight):
        return weight.reshape(weight_rows, 2, PARTS, part_width)

    flats = (flat(gate_weight), flat(up_weight), flat(down_weight))

    def side(part, bit):
        return jnp.concatenate(
            [lax.dynamic_index_in_dim(w[:, :, part], bit, 1, False) for w in flats], axis=1
        )

    def fetched(part, received):
        whole = joined(side(part, pair_bit), received, pair_bit)
        if part == 0:
            whole = column_gather(whole)
            return [whole[:, : 2 * part_width], whole[:, 2 * part_width :]]
        return [
            column_gather(whole[:, : 2 * part_width]),
            column_gather(whole[:, 2 * part_width :]),
        ]

    def start_whole(own, beside):
        shape = (column_count, fsdp_size // column_count * weight_rows, own.shape[1])
        whole = jnp.zeros(shape, own.dtype)
        return column_place(whole, joined(own, beside, pair_bit), 0)

    first_low = first_norm.astype(jnp.bfloat16)
    first_chip = to_chip(first_low)
    out_mine = column_gather(out_weight)
    swapped = to_pair(after(side(0, 1 - pair_bit), share_group))
    three_pieces = [three_own, column_shift(three_own)]
    three_pieces[-1] = step(three_pieces[-1])
    three_pieces.append(column_shift(three_pieces[-1]))
    first_both = tp_both(first_low, step(first_chip))
    first_core = to_core(first_both)
    swapped = step(swapped)
    three_besides = [to_pair(after(three_own, swapped)), to_pair(after(three_pieces[1], swapped))]
    for offset in range(2, column_count):
        three_pieces[offset] = step(three_pieces[offset])
        three_besides.append(to_pair(three_pieces[offset]))
        if offset + 1 < column_count:
            three_pieces.append(column_shift(three_pieces[offset]))
    expert_weights = [fetched(0, swapped)]
    first_full = tp_join(first_both, step(first_core))
    share_wide = step(share_wide)
    three_whole = start_whole(three_own, step(three_besides[0]))
    out_mine = step(out_mine)
    for offset in range(1, column_count):
        three_besides[offset] = step(three_besides[offset])
        three_whole = column_place(
            three_whole, joined(three_pieces[offset], three_besides[offset], pair_bit), offset
        )
    out_theirs = to_pair(after(out_mine, three_besides[-1]))
    query_key_value = three_whole.reshape(fsdp_size * weight_rows, three_width)
    projected = matmul(first_full, query_key_value)
    heads_low = step(attend(projected, tables, query_count, kv_count, head_size))
    out_theirs = step(out_theirs)
    cotangent_open = plane_open(after(cotangent, out_theirs))
    full_out = weight_join(out_mine, out_theirs)
    attn_split = step(tp_split(times_transposed(heads_low, full_out)))
    received = to_pair(after(side(1, 1 - pair_bit), out_theirs))
    attn_halved = step(tp_halve(attn_split))
    middle = token_rows + tp_sum(attn_halved)
    second_norm, second_inverse = norm_rows(middle, feedforward_gain)
    second_low = second_norm.astype(jnp.bfloat16)
    second_open = plane_open(second_low)
    for part in range(1, PARTS):
        received = step(received)
        expert_weights.append(fetched(part, received))
        if part + 1 < PARTS:
            received = to_pair(after(side(part + 1, 1 - pair_bit), received))
    second_open = step(second_open)
    second_cross = plane_cross(second_open)
    cotangent_open = step(cotangent_open)
    second_cross = step(second_cross)
    second_core = plane_core(second_low, second_open, second_cross)
    cotangent_cross = plane_cross(after(cotangent_open, second_cross))
    expert_weights[0][0] = step(expert_weights[0][0])
    second_group = plane_join(step(second_core))
    cotangent_core = plane_core(cotangent, cotangent_open, step(cotangent_cross))
    grad_group = plane_join(step(cotangent_core))
    weight_terms = []
    hiddens = []
    for part in range(PARTS):
        weight_in, weight_down = expert_weights[part]
        share = share_wide[part]
        both_pre = matmul(second_group, weight_in)
        gate_pre, up_pre = both_pre[:, :part_width], both_pre[:, part_width:]
        sigmoid_gate = jax.nn.sigmoid(gate_pre)
        silu_gate = gate_pre * sigmoid_gate
        hidden = (silu_gate * up_pre * share).astype(jnp.bfloat16)
        hidden_grad = matmul(grad_group, weight_down) * share
        up_grad = (hidden_grad * silu_gate).astype(jnp.bfloat16)
        gate_grad = (
            hidden_grad * up_pre * sigmoid_gate * (1.0 + gate_pre * (1.0 - sigmoid_gate))
        ).astype(jnp.bfloat16)
        both_grad = jnp.concatenate([gate_grad, up_grad], axis=1)
        if part < PARTS - 1:
            down_term = step(inner_rows(grad_group, hidden).astype(jnp.bfloat16))
            expert_weights[part + 1][0] = step(expert_weights[part + 1][0])
            both_late = after(both_grad, down_term)
            weight_term = jnp.concatenate(
                [inner_rows(second_group, both_late).astype(jnp.bfloat16), down_term], axis=1
            )
            both_late = after(both_grad, weight_term)
            second_part = times_transposed(both_late, weight_in)
            hiddens.append(hidden)
            expert_weights[part + 1][1] = step(expert_weights[part + 1][1])
            second_sum = second_part if part == 0 else second_sum + second_part
            second_sum = step(second_sum)
        else:
            second_sent = second_sum[rows_all:] + times_transposed(
                both_grad[rows_all:], weight_in
            )
            second_sent = step(second_sent.astype(jnp.bfloat16))
            second_kept = second_sum[:rows_all] + times_transposed(
                after(both_grad, second_sent)[:rows_all], weight_in
            )
            hidden, both_grad = after((hidden, both_grad), second_kept)
            hiddens.append(hidden)
            weight_term = jnp.concatenate(
                [
                    inner_rows(second_group, both_grad).astype(jnp.bfloat16),
                    inner_rows(grad_group, hidden).astype(jnp.bfloat16),
                ],
                axis=1,
            )
        weight_terms.append(weight_term)

    second_fold = fold_cross(step(fold_core(second_kept, second_sent)))
    second_fold = fold_open(step(second_fold))
    second_fold, weight_terms[-1] = step((second_fold, weight_terms[-1]))
    reduced = [column_scatter(term) for term in weight_terms]
    second_grad = fold_sum(second_fold)
    middle_back, feedforward_gain_grad = norm_back(
        middle, second_inverse, feedforward_gain, second_grad
    )
    middle_grad = cotangent.astype(jnp.float32) + middle_back
    grad_low = middle_grad.astype(jnp.bfloat16)
    grad_chip = to_chip(grad_low)
    first_kept, first_sent = pair_columns(after(first_full, grad_low))
    def moe_rows(rows, *earlier):
        kept = after(hiddens, *earlier)
        return sum(
            times_transposed(piece[rows], weights[1])
            for piece, weights in zip(kept, expert_weights, strict=True)
        )

    moe_sent = moe_rows(slice(rows_all, None), grad_low).astype(jnp.bfloat16)
    grad_chip, first_sent, moe_sent = step((grad_chip, first_sent, moe_sent))
    grad_both = tp_both(grad_low, grad_chip)
    attn_grad_full = tp_join(grad_both, step(to_core(grad_both)))
    moe_received = to_core(after(moe_sent, attn_grad_full))
    heads_grad = matmul(attn_grad_full, full_out).astype(jnp.bfloat16)
    grad_kept, grad_sent = pair_columns(attn_grad_full)
    out_sent = inner_rows(grad_sent, heads_low).astype(jnp.bfloat16)
    heads_grad, out_sent = step((heads_grad, out_sent))
    out_received = to_pair(out_sent)
    projected_grad, query_gain_grad, key_gain_grad = step(
        attend_back(projected, heads_grad, tables, query_count, kv_count, head_size)
    )
    projected_sent = step(inner_rows(first_sent, projected_grad).astype(jnp.bfloat16))
    projected_received = to_pair(projected_sent)
    out_kept = inner_rows(after(grad_kept, projected_sent), heads_low)
    out_received = step(out_received)
    projected_kept = step(inner_rows(first_kept, projected_grad))
    first_split = tp_split(
        times_transposed(after(projected_grad, projected_kept), query_key_value)
    )
    first_halved = tp_halve(step(first_split))
    projected_received = step(projected_received)
    attention_owned = weight_reduce(
        [(projected_kept, projected_received), (out_kept, out_received)]
    )
    owned_parts = [exchange(after(reduced[0], projected_received))]
    first_grad = tp_sum(step(first_halved))
    moe_kept = moe_rows(slice(0, rows_all), projected_kept)
    moe_fold = fold_cross((moe_kept, after(moe_received, projected_received)))
    owned_parts[0] = step(owned_parts[0])
    moe_fold = step(moe_fold)
    owned_parts.append(exchange(step(reduced[1])))
    moe_fold = fold_open(moe_fold)
    owned_parts[1] = step(owned_parts[1])
    output = (middle + fold_sum(step(moe_fold))).astype(jnp.bfloat16)

    def owned(index):
        place = slice(index * part_width, (index + 1) * part_width)
        mine = jnp.concatenate([kept[:, place] for kept, sent in owned_parts], axis=1)
        theirs = jnp.concatenate([sent[:, place] for kept, sent in owned_parts], axis=1)
        return (
            jnp.concatenate(
                [
                    jnp.where(pair_bit == 0, mine, theirs),
                    jnp.where(pair_bit == 0, theirs, mine),
                ],
                axis=1,
            )
            .astype(jnp.float32)
            .reshape(weight_rows, expert_count, expert_width)
        )

    rows_back, attention_gain_grad = norm_back(
        token_rows, first_inverse, attention_gain, first_grad
    )
    tokens_grad = middle_grad + rows_back
    gain_sums = sum_all(
        jnp.concatenate(
            [
                attention_gain_grad,
                feedforward_gain_grad,
                query_gain_grad.reshape(head_size),
                key_gain_grad.reshape(head_size),
            ]
        )
    )
    attention_owned = after(attention_owned, gain_sums, output).astype(jnp.float32)
    gain_sums = jnp.split(
        gain_sums,
        [model_width, 2 * model_width, 2 * model_width + head_size],
    )
    return (
        output,
        tokens_grad,
        gain_sums[0],
        gain_sums[1],
        gain_sums[2],
        gain_sums[3],
        attention_owned[:, :query_width],
        attention_owned[:, query_width : query_width + key_width],
        attention_owned[:, query_width + key_width : three_width],
        attention_owned[:, three_width:],
        owned(0),
        owned(1),
        owned(2),
    )


def solution(mesh):
    placed = (
        P(("fsdp", "tp"), None),
        P(("fsdp", "tp"), None),
        P("fsdp"),
        P("fsdp", None),
        P("fsdp", None),
        P(),
        P(),
        P(),
        P(),
        P("fsdp", "tp"),
        P("fsdp", "tp"),
        P("fsdp", "tp"),
        P("fsdp", "tp"),
        P("fsdp", None, "tp"),
        P("fsdp", None, "tp"),
        P("fsdp", None, "tp"),
    )
    return jax.shard_map(
        partial(per_device, mesh.shape["fsdp"], mesh.shape["tp"]),
        mesh=mesh,
        in_specs=placed,
        out_specs=(
            P(("fsdp", "tp"), None),
            P(("fsdp", "tp"), None),
            P(),
            P(),
            P(),
            P(),
            P("fsdp", "tp"),
            P("fsdp", "tp"),
            P("fsdp", "tp"),
            P("fsdp", "tp"),
            P("fsdp", None, "tp"),
            P("fsdp", None, "tp"),
            P("fsdp", None, "tp"),
        ),
        check_vma=False,
    )
```

```python
from functools import partial

import jax
import jax.numpy as jnp
from jax import lax
from jax.experimental import pallas as pl
from jax.experimental.pallas import tpu as pltpu
from jax.sharding import PartitionSpec as P

SEQ = 1024
TILE = 256
PARTS = 2
VMEM_BYTES = 48 * 1024 * 1024


eps_norm = 1e-06
rope_base = 1000000.0


def matmul(left_side, right_side):
    return jnp.dot(left_side, right_side, preferred_element_type=jnp.float32)


def times_transposed(left_side, right_side):
    return lax.dot_general(
        left_side, right_side, (((1,), (1,)), ((), ())), preferred_element_type=jnp.float32
    )


def inner_rows(left_side, right_side):
    return lax.dot_general(
        left_side, right_side, (((0,), (0,)), ((), ())), preferred_element_type=jnp.float32
    )


def norm_rows(values, scale_gain):
    inverse = lax.rsqrt(jnp.mean(values * values, axis=-1, keepdims=True) + eps_norm)
    return (values * inverse * scale_gain, inverse)


def norm_back(values, inverse, scale_gain, incoming):
    normed = values * inverse
    scaled_grad = incoming * scale_gain
    gain_grad = jnp.sum(incoming * normed, axis=tuple(range(values.ndim - 1)))
    result = inverse * (
        scaled_grad - normed * jnp.mean(scaled_grad * normed, axis=-1, keepdims=True)
    )
    return (result, gain_grad)


def rope_tables(row_count, head_size):
    positions = jnp.arange(row_count, dtype=jnp.float32)
    frequencies = rope_base ** (-jnp.arange(0, head_size, 2, dtype=jnp.float32) / head_size)
    angles = positions[:, None] * frequencies[None, :]
    angles = jnp.concatenate([angles, angles], axis=-1)
    return (jnp.cos(angles), jnp.sin(angles))


def head_norm(values):
    inverse = lax.rsqrt(jnp.mean(values * values, axis=-1, keepdims=True) + eps_norm)
    return (values * inverse, inverse)


def turn(values, cosine, signed_sine):
    half_size = values.shape[-1] // 2
    return values * cosine + pltpu.roll(values, half_size, 1) * signed_sine


def turn_back(incoming, cosine, signed_sine):
    half_size = incoming.shape[-1] // 2
    return incoming * cosine + pltpu.roll(incoming * signed_sine, half_size, 1)


def masked_probs(query_tile, key_rows, row_ids, column_ids, offset, scaling):
    scores = times_transposed(query_tile, key_rows) * scaling
    row_place = lax.broadcasted_iota(jnp.int32, scores.shape, 0) + offset
    column_place = lax.broadcasted_iota(jnp.int32, scores.shape, 1)
    allowed = (column_place <= row_place) & (row_ids == column_ids)
    scores = jnp.where(allowed, scores, -jnp.inf)
    weights = jnp.exp(scores - jnp.max(scores, axis=-1, keepdims=True))
    return weights * (1.0 / jnp.sum(weights, axis=-1, keepdims=True))


def attend_kernel(
    group_size,
    query_ref,
    key_ref,
    value_ref,
    cosine_ref,
    sine_ref,
    row_ids_ref,
    column_ids_ref,
    query_gain_ref,
    key_gain_ref,
    heads_ref,
    key_low,
    value_low,
):
    head_size = query_ref.shape[1]
    scaling = head_size ** (-0.5)

    @pl.when(lax.rem(pl.program_id(1), group_size) == 0)
    def prepare():
        normed, unused = head_norm(key_ref[...])
        key_low[...] = turn(normed * key_gain_ref[...], cosine_ref[...], sine_ref[...]).astype(
            jnp.bfloat16
        )
        value_low[...] = value_ref[...].astype(jnp.bfloat16)

    for offset in range(0, SEQ, TILE):
        finish = offset + TILE
        rows = pl.ds(offset, TILE)
        normed, unused = head_norm(query_ref[rows, :])
        query_tile = turn(
            normed * query_gain_ref[...], cosine_ref[rows, :], sine_ref[rows, :]
        ).astype(jnp.bfloat16)
        probs = masked_probs(
            query_tile,
            key_low[:finish, :],
            row_ids_ref[rows, :],
            column_ids_ref[:, :finish],
            offset,
            scaling,
        )
        heads_ref[rows, :] = matmul(probs.astype(jnp.bfloat16), value_low[:finish, :]).astype(
            jnp.bfloat16
        )


def attend_back_kernel(
    query_count,
    kv_count,
    query_ref,
    key_ref,
    value_ref,
    grad_ref,
    cosine_ref,
    sine_ref,
    row_ids_ref,
    column_ids_ref,
    query_gain_ref,
    key_gain_ref,
    projected_ref,
    query_gain_grad_ref,
    key_gain_grad_ref,
    key_low,
    value_low,
    key_sum,
    value_sum,
):
    head_size = query_ref.shape[1]
    scaling = head_size ** (-0.5)
    group_size = query_count // kv_count
    head = pl.program_id(1)
    place = lax.rem(head, group_size)

    @pl.when((pl.program_id(0) == 0) & (head == 0))
    def clear():
        query_gain_grad_ref[...] = jnp.zeros_like(query_gain_grad_ref)
        key_gain_grad_ref[...] = jnp.zeros_like(key_gain_grad_ref)

    @pl.when(place == 0)
    def prepare():
        normed, unused = head_norm(key_ref[...])
        key_low[...] = turn(normed * key_gain_ref[...], cosine_ref[...], sine_ref[...]).astype(
            jnp.bfloat16
        )
        value_low[...] = value_ref[...].astype(jnp.bfloat16)
        key_sum[...] = jnp.zeros_like(key_sum)
        value_sum[...] = jnp.zeros_like(value_sum)

    def through_norm(turned_grad, cosine, signed_sine, normed, inverse, gain):
        incoming = turn_back(turned_grad, cosine, signed_sine)
        scaled_grad = incoming * gain
        result = inverse * (
            scaled_grad - normed * jnp.mean(scaled_grad * normed, axis=-1, keepdims=True)
        )
        return (result, jnp.sum(incoming * normed, axis=0, keepdims=True))

    columns = pl.ds(pl.multiple_of(head * head_size, head_size), head_size)
    for offset in range(0, SEQ, TILE):
        finish = offset + TILE
        rows = pl.ds(offset, TILE)
        cosine, signed_sine = cosine_ref[rows, :], sine_ref[rows, :]
        normed, inverse = head_norm(query_ref[rows, :])
        query_tile = turn(normed * query_gain_ref[...], cosine, signed_sine).astype(jnp.bfloat16)
        grad_tile = grad_ref[rows, :]
        key_rows = key_low[:finish, :]
        probs = masked_probs(
            query_tile,
            key_rows,
            row_ids_ref[rows, :],
            column_ids_ref[:, :finish],
            offset,
            scaling,
        )
        prob_grad = times_transposed(grad_tile, value_low[:finish, :])
        score_grad = (
            probs * (prob_grad - jnp.sum(probs * prob_grad, axis=-1, keepdims=True))
        ).astype(jnp.bfloat16)
        value_sum[:finish, :] += inner_rows(probs.astype(jnp.bfloat16), grad_tile)
        key_sum[:finish, :] += inner_rows(score_grad, query_tile)
        result, gain_grad = through_norm(
            matmul(score_grad, key_rows) * scaling,
            cosine,
            signed_sine,
            normed,
            inverse,
            query_gain_ref[...],
        )
        projected_ref[rows, columns] = result.astype(jnp.bfloat16)
        query_gain_grad_ref[...] += gain_grad

    @pl.when(place == group_size - 1)
    def finish_group():
        group = lax.div(head, group_size)
        normed, inverse = head_norm(key_ref[...])
        result, gain_grad = through_norm(
            key_sum[...] * scaling,
            cosine_ref[...],
            sine_ref[...],
            normed,
            inverse,
            key_gain_ref[...],
        )
        key_columns = pl.ds(
            pl.multiple_of((query_count + group) * head_size, head_size), head_size
        )
        value_columns = pl.ds(
            pl.multiple_of((query_count + kv_count + group) * head_size, head_size), head_size
        )
        projected_ref[:, key_columns] = result.astype(jnp.bfloat16)
        projected_ref[:, value_columns] = value_sum[...].astype(jnp.bfloat16)
        key_gain_grad_ref[...] += gain_grad


def attention_specs(query_count, kv_count, head_size):
    group_size = query_count // kv_count
    block = (SEQ, head_size)
    fixed = lambda shape: pl.BlockSpec(shape, lambda s, h: (0, 0))
    operands = [
        pl.BlockSpec(block, lambda s, h: (s, h)),
        pl.BlockSpec(block, lambda s, h: (s, query_count + h // group_size)),
        pl.BlockSpec(block, lambda s, h: (s, query_count + kv_count + h // group_size)),
    ]
    tables = [
        fixed(block),
        fixed(block),
        pl.BlockSpec((SEQ, 1), lambda s, h: (s, 0)),
        pl.BlockSpec((1, SEQ), lambda s, h: (0, s)),
        fixed((1, head_size)),
        fixed((1, head_size)),
    ]
    return (operands, tables)


def attend(projected, tables, query_count, kv_count, head_size):
    rows = projected.shape[0]
    operands, table_specs = attention_specs(query_count, kv_count, head_size)
    pairs = rows * SEQ * query_count * 5 // 8
    return pl.pallas_call(
        partial(attend_kernel, query_count // kv_count),
        grid=(rows // SEQ, query_count),
        in_specs=operands + table_specs,
        out_specs=pl.BlockSpec((SEQ, head_size), lambda s, h: (s, h)),
        out_shape=jax.ShapeDtypeStruct((rows, query_count * head_size), jnp.bfloat16),
        scratch_shapes=[
            pltpu.VMEM((SEQ, head_size), jnp.bfloat16),
            pltpu.VMEM((SEQ, head_size), jnp.bfloat16),
        ],
        compiler_params=pltpu.CompilerParams(vmem_limit_bytes=VMEM_BYTES),
        cost_estimate=pl.CostEstimate(
            flops=60 * pairs * head_size,
            bytes_accessed=6 * rows * query_count * head_size,
            transcendentals=pairs,
        ),
        name="attend",
    )(projected, projected, projected, *tables)


def attend_back(projected, heads_grad, tables, query_count, kv_count, head_size):
    rows = projected.shape[0]
    width = projected.shape[1]
    operands, table_specs = attention_specs(query_count, kv_count, head_size)
    pairs = rows * SEQ * query_count * 5 // 8
    return pl.pallas_call(
        partial(attend_back_kernel, query_count, kv_count),
        grid=(rows // SEQ, query_count),
        in_specs=operands + [pl.BlockSpec((SEQ, head_size), lambda s, h: (s, h))] + table_specs,
        out_specs=[
            pl.BlockSpec((SEQ, width), lambda s, h: (s, 0)),
            pl.BlockSpec((1, head_size), lambda s, h: (0, 0)),
            pl.BlockSpec((1, head_size), lambda s, h: (0, 0)),
        ],
        out_shape=[
            jax.ShapeDtypeStruct((rows, width), jnp.bfloat16),
            jax.ShapeDtypeStruct((1, head_size), jnp.float32),
            jax.ShapeDtypeStruct((1, head_size), jnp.float32),
        ],
        scratch_shapes=[
            pltpu.VMEM((SEQ, head_size), jnp.bfloat16),
            pltpu.VMEM((SEQ, head_size), jnp.bfloat16),
            pltpu.VMEM((SEQ, head_size), jnp.float32),
            pltpu.VMEM((SEQ, head_size), jnp.float32),
        ],
        compiler_params=pltpu.CompilerParams(vmem_limit_bytes=VMEM_BYTES),
        cost_estimate=pl.CostEstimate(
            flops=90 * pairs * head_size,
            bytes_accessed=10 * rows * query_count * head_size,
            transcendentals=pairs,
        ),
        name="attend_back",
    )(projected, projected, projected, heads_grad, *tables)


def joined(own, other, bit):
    first_half = jnp.where(bit == 0, own, other)
    last_half = jnp.where(bit == 0, other, own)
    return jnp.concatenate([first_half, last_half], axis=0)


def halves(values, bit):
    rows = values.shape[0] // 2
    kept = lax.dynamic_slice_in_dim(values, bit * rows, rows, 0)
    sent = lax.dynamic_slice_in_dim(values, (1 - bit) * rows, rows, 0)
    return (kept, sent)


def make_moves(fsdp_size, tp_size):
    swap_core = [(i, i ^ 1) for i in range(tp_size)]
    swap_chip = [(i, (i + 2) % tp_size) for i in range(tp_size)]
    swap_pair = [(i, i ^ 1) for i in range(fsdp_size)]
    columns = [list(range(b, fsdp_size, 2)) for b in range(2)]

    def to_core(values):
        return lax.ppermute(values, "tp", swap_core)

    def to_chip(values):
        return lax.ppermute(values, "tp", swap_chip)

    def to_pair(values):
        return lax.ppermute(values, "fsdp", swap_pair)

    def tp_both(own, received):
        return joined(own, received, lax.axis_index("tp") // 2)

    def tp_join(both, others):
        place = lax.axis_index("tp")
        rows, width = both.shape[0] // 2, both.shape[1]
        both = both.reshape(2, 1, rows, width)
        others = others.reshape(2, 1, rows, width)
        first_core = jnp.where(place % 2 == 0, both, others)
        last_core = jnp.where(place % 2 == 0, others, both)
        return jnp.concatenate([first_core, last_core], axis=1).reshape(4 * rows, width)

    def tp_gather(own):
        both = tp_both(own, to_chip(own))
        return tp_join(both, to_core(both))

    def tp_split(full):
        place = lax.axis_index("tp")
        rows, width = full.shape[0] // 4, full.shape[1]
        split = full.reshape(2, 2, rows, width)
        kept = lax.dynamic_index_in_dim(split, place % 2, 1, False)
        sent = lax.dynamic_index_in_dim(split, 1 - place % 2, 1, False).astype(jnp.bfloat16)
        return (kept, to_core(sent))

    def tp_halve(split):
        kept, received = split
        kept, sent = halves(kept + received.astype(jnp.float32), lax.axis_index("tp") // 2)
        return (kept, to_chip(sent.astype(jnp.bfloat16)))

    def tp_sum(halved):
        kept, received = halved
        return (kept + received.astype(jnp.float32)).reshape(kept.shape[1:])

    def tp_scatter(full):
        return tp_sum(tp_halve(tp_split(full)))

    def plane_open(own):
        return (to_chip(own), to_pair(own))

    def plane_cross(opened):
        across, beside = opened
        cut = across.shape[0] // 2
        return (to_chip(beside[:cut]), to_pair(across[cut:]))

    def plane_core(own, opened, crossed):
        mine = jnp.concatenate([own, *opened, *crossed], axis=0)
        return (mine, to_core(mine))

    def plane_join(cored):
        return jnp.concatenate(cored, axis=0)

    def plane_gather(own):
        opened = plane_open(own)
        return plane_join(plane_core(own, opened, plane_cross(opened)))

    def fold_core(kept, sent):
        return (kept, to_core(sent))

    def fold_cross(cored):
        kept, received = cored
        rows = kept.shape[0] // 4
        cut = rows // 2
        far = (kept[3 * rows :] + received[3 * rows :].astype(jnp.float32)).astype(jnp.bfloat16)
        return (kept, received, to_chip(far[:cut]), to_pair(far[cut:]))

    def fold_open(crossed):
        kept, received, from_chip, from_pair = crossed
        rows = kept.shape[0] // 4
        cut = rows // 2
        own, across, beside = [
            kept[i * rows : (i + 1) * rows]
            + received[i * rows : (i + 1) * rows].astype(jnp.float32)
            for i in range(3)
        ]
        across = jnp.concatenate([across[:cut], across[cut:] + from_pair.astype(jnp.float32)])
        beside = jnp.concatenate([beside[:cut] + from_chip.astype(jnp.float32), beside[cut:]])
        return (
            own,
            to_chip(across.astype(jnp.bfloat16)),
            to_pair(beside.astype(jnp.bfloat16)),
        )

    def fold_sum(opened):
        own, from_chip, from_pair = opened
        return own + from_chip.astype(jnp.float32) + from_pair.astype(jnp.float32)

    def plane_share(share):
        place = lax.axis_index("tp")
        rows, count = share.shape[0] // 4, share.shape[1]
        split = share.reshape(2, 2, rows, count)
        split = jnp.where(place // 2 == 0, split, split[::-1])
        split = jnp.where(place % 2 == 0, split, split[:, ::-1]).swapaxes(0, 1)
        return jnp.stack([split, to_pair(split)], axis=1).reshape(8 * rows, count)

    def column_gather(own):
        return lax.all_gather(own, "fsdp", axis=0, tiled=True, axis_index_groups=columns)

    def column_scatter(full):
        return lax.psum_scatter(
            full, "fsdp", scatter_dimension=0, tiled=True, axis_index_groups=columns
        )

    def weight_join(mine, theirs):
        pair_bit = lax.axis_index("fsdp") % 2
        rows, width = mine.shape[0] // (fsdp_size // 2), mine.shape[1]
        mine = mine.reshape(fsdp_size // 2, 1, rows, width)
        theirs = theirs.reshape(fsdp_size // 2, 1, rows, width)
        return jnp.concatenate(
            [jnp.where(pair_bit == 0, mine, theirs), jnp.where(pair_bit == 0, theirs, mine)],
            axis=1,
        ).reshape(fsdp_size * rows, width)

    def column_shift(values):
        pairs = [(i, (i + 2) % fsdp_size) for i in range(fsdp_size)]
        return lax.ppermute(values, "fsdp", pairs)

    def column_place(whole, piece, offset):
        count = fsdp_size // 2
        place = (lax.axis_index("fsdp") // 2 - offset) % count
        return lax.dynamic_update_index_in_dim(whole, piece, place, 0)

    def pair_columns(values):
        pair_bit = lax.axis_index("fsdp") % 2
        width = values.shape[1] // fsdp_size
        return [
            jnp.concatenate(
                [
                    lax.dynamic_slice_in_dim(values, (2 * place + bit) * width, width, 1)
                    for place in range(fsdp_size // 2)
                ],
                axis=1,
            )
            for bit in (pair_bit, 1 - pair_bit)
        ]

    def weight_reduce(pairs):
        summed = [
            (kept + received.astype(jnp.float32)).astype(jnp.bfloat16) for kept, received in pairs
        ]
        return column_scatter(jnp.concatenate(summed, axis=1))

    def sum_all(values):
        for step in range(tp_size.bit_length() - 1):
            swap = [(i, i ^ (1 << step)) for i in range(tp_size)]
            values = values + lax.ppermute(values, "tp", swap)
        for step in range(fsdp_size.bit_length() - 1):
            swap = [(i, i ^ (1 << step)) for i in range(fsdp_size)]
            values = values + lax.ppermute(values, "fsdp", swap)
        return values

    return (
        to_pair,
        to_core,
        to_chip,
        tp_both,
        tp_join,
        tp_gather,
        tp_split,
        tp_halve,
        tp_sum,
        tp_scatter,
        plane_open,
        plane_cross,
        plane_core,
        plane_join,
        fold_core,
        fold_cross,
        fold_open,
        fold_sum,
        plane_share,
        column_gather,
        column_scatter,
        weight_join,
        column_shift,
        column_place,
        pair_columns,
        weight_reduce,
        sum_all,
    )


def per_device(
    fsdp_size,
    tp_size,
    tokens,
    cotangent,
    segments,
    routes,
    gate_logits,
    attention_gain,
    feedforward_gain,
    query_gain,
    key_gain,
    query_weight,
    key_weight,
    value_weight,
    out_weight,
    gate_weight,
    up_weight,
    down_weight,
):
    (
        to_pair,
        to_core,
        to_chip,
        tp_both,
        tp_join,
        tp_gather,
        tp_split,
        tp_halve,
        tp_sum,
        tp_scatter,
        plane_open,
        plane_cross,
        plane_core,
        plane_join,
        fold_core,
        fold_cross,
        fold_open,
        fold_sum,
        plane_share,
        column_gather,
        column_scatter,
        weight_join,
        column_shift,
        column_place,
        pair_columns,
        weight_reduce,
        sum_all,
    ) = make_moves(fsdp_size, tp_size)
    pair_bit = lax.axis_index("fsdp") % 2
    head_size = query_gain.shape[0]
    kv_count = key_weight.shape[1] // head_size
    query_count = query_weight.shape[1] // head_size
    weight_rows, expert_count, expert_width = gate_weight.shape
    half_experts = expert_count // 2
    half_width = half_experts * expert_width
    part_width = half_width // PARTS
    rows_all = segments.shape[0]
    cosine, sine_table = rope_tables(SEQ, head_size)
    turn_sign = jnp.where(jnp.arange(head_size) < head_size // 2, -1.0, 1.0)
    tables = (
        cosine,
        sine_table * turn_sign,
        segments.reshape(rows_all, 1),
        segments.reshape(1, rows_all),
        query_gain.reshape(1, head_size),
        key_gain.reshape(1, head_size),
    )
    token_rows = tokens.astype(jnp.float32)
    first_norm, first_inverse = norm_rows(token_rows, attention_gain)
    last = []

    def step(value):
        if last:
            value = lax.optimization_barrier((value, last[0]))[0]
        last[:] = [value]
        return value

    def after(value, *earlier):
        return lax.optimization_barrier((value, earlier))[0]

    def exchange(reduced):
        kept, sent = halves(reduced, pair_bit)
        return (kept, to_pair(sent))

    gate_probs = jax.nn.softmax(gate_logits, axis=-1)
    expert_ids = jnp.arange(expert_count, dtype=jnp.int32)
    share_own = jnp.sum(
        jnp.where(routes[:, :, None] == expert_ids[None, None, :], gate_probs[:, :, None], 0.0),
        axis=1,
    )
    share_group = plane_share(share_own)
    share_half = lax.dynamic_slice_in_dim(share_group, pair_bit * half_experts, half_experts, 1)
    span = half_experts // PARTS
    share_wide = [
        jnp.repeat(share_half[:, part * span : (part + 1) * span], expert_width, axis=1)
        for part in range(PARTS)
    ]
    query_width = query_count * head_size
    key_width = kv_count * head_size
    model_width = tokens.shape[1]
    three_width = query_width + 2 * key_width
    column_count = fsdp_size // 2
    three_own = jnp.concatenate([query_weight, key_weight, value_weight], axis=1)

    def flat(weight):
        return weight.reshape(weight_rows, 2, PARTS, part_width)

    flats = (flat(gate_weight), flat(up_weight), flat(down_weight))

    def side(part, bit):
        return jnp.concatenate(
            [lax.dynamic_index_in_dim(w[:, :, part], bit, 1, False) for w in flats], axis=1
        )

    def fetched(part, received):
        whole = joined(side(part, pair_bit), received, pair_bit)
        if part == 0:
            whole = column_gather(whole)
            return [whole[:, : 2 * part_width], whole[:, 2 * part_width :]]
        return [
            column_gather(whole[:, : 2 * part_width]),
            column_gather(whole[:, 2 * part_width :]),
        ]

    def start_whole(own, beside):
        shape = (column_count, fsdp_size // column_count * weight_rows, own.shape[1])
        whole = jnp.zeros(shape, own.dtype)
        return column_place(whole, joined(own, beside, pair_bit), 0)

    first_low = first_norm.astype(jnp.bfloat16)
    first_chip = to_chip(first_low)
    out_mine = column_gather(out_weight)
    swapped = to_pair(after(side(0, 1 - pair_bit), share_group))
    three_pieces = [three_own, column_shift(three_own)]
    three_pieces[-1] = step(three_pieces[-1])
    three_pieces.append(column_shift(three_pieces[-1]))
    first_both = tp_both(first_low, step(first_chip))
    first_core = to_core(first_both)
    swapped = step(swapped)
    three_besides = [to_pair(after(three_own, swapped)), to_pair(after(three_pieces[1], swapped))]
    for offset in range(2, column_count):
        three_pieces[offset] = step(three_pieces[offset])
        three_besides.append(to_pair(three_pieces[offset]))
        if offset + 1 < column_count:
            three_pieces.append(column_shift(three_pieces[offset]))
    expert_weights = [fetched(0, swapped)]
    first_full = tp_join(first_both, step(first_core))
    share_wide = step(share_wide)
    three_whole = start_whole(three_own, step(three_besides[0]))
    out_mine = step(out_mine)
    for offset in range(1, column_count):
        three_besides[offset] = step(three_besides[offset])
        three_whole = column_place(
            three_whole, joined(three_pieces[offset], three_besides[offset], pair_bit), offset
        )
    out_theirs = to_pair(after(out_mine, three_besides[-1]))
    query_key_value = three_whole.reshape(fsdp_size * weight_rows, three_width)
    projected = matmul(first_full, query_key_value)
    heads_low = step(attend(projected, tables, query_count, kv_count, head_size))
    out_theirs = step(out_theirs)
    cotangent_open = plane_open(after(cotangent, out_theirs))
    full_out = weight_join(out_mine, out_theirs)
    attn_split = step(tp_split(times_transposed(heads_low, full_out)))
    received = to_pair(after(side(1, 1 - pair_bit), out_theirs))
    attn_halved = step(tp_halve(attn_split))
    middle = token_rows + tp_sum(attn_halved)
    second_norm, second_inverse = norm_rows(middle, feedforward_gain)
    second_low = second_norm.astype(jnp.bfloat16)
    second_open = plane_open(second_low)
    for part in range(1, PARTS):
        received = step(received)
        expert_weights.append(fetched(part, received))
        if part + 1 < PARTS:
            received = to_pair(after(side(part + 1, 1 - pair_bit), received))
    second_open = step(second_open)
    second_cross = plane_cross(second_open)
    cotangent_open = step(cotangent_open)
    second_cross = step(second_cross)
    second_core = plane_core(second_low, second_open, second_cross)
    cotangent_cross = plane_cross(after(cotangent_open, second_cross))
    expert_weights[0][0] = step(expert_weights[0][0])
    second_group = plane_join(step(second_core))
    cotangent_core = plane_core(cotangent, cotangent_open, step(cotangent_cross))
    grad_group = plane_join(step(cotangent_core))
    weight_terms = []
    hiddens = []
    for part in range(PARTS):
        weight_in, weight_down = expert_weights[part]
        share = share_wide[part]
        both_pre = matmul(second_group, weight_in)
        gate_pre, up_pre = both_pre[:, :part_width], both_pre[:, part_width:]
        sigmoid_gate = jax.nn.sigmoid(gate_pre)
        silu_gate = gate_pre * sigmoid_gate
        hidden = (silu_gate * up_pre * share).astype(jnp.bfloat16)
        hidden_grad = matmul(grad_group, weight_down) * share
        up_grad = (hidden_grad * silu_gate).astype(jnp.bfloat16)
        gate_grad = (
            hidden_grad * up_pre * sigmoid_gate * (1.0 + gate_pre * (1.0 - sigmoid_gate))
        ).astype(jnp.bfloat16)
        both_grad = jnp.concatenate([gate_grad, up_grad], axis=1)
        if part < PARTS - 1:
            down_term = step(inner_rows(grad_group, hidden).astype(jnp.bfloat16))
            expert_weights[part + 1][0] = step(expert_weights[part + 1][0])
            both_late = after(both_grad, down_term)
            weight_term = jnp.concatenate(
                [inner_rows(second_group, both_late).astype(jnp.bfloat16), down_term], axis=1
            )
            both_late = after(both_grad, weight_term)
            second_part = times_transposed(both_late, weight_in)
            hiddens.append(hidden)
            expert_weights[part + 1][1] = step(expert_weights[part + 1][1])
            second_sum = second_part if part == 0 else second_sum + second_part
            second_sum = step(second_sum)
        else:
            second_sent = second_sum[rows_all:] + times_transposed(
                both_grad[rows_all:], weight_in
            )
            second_sent = step(second_sent.astype(jnp.bfloat16))
            second_kept = second_sum[:rows_all] + times_transposed(
                after(both_grad, second_sent)[:rows_all], weight_in
            )
            hidden, both_grad = after((hidden, both_grad), second_kept)
            hiddens.append(hidden)
            weight_term = jnp.concatenate(
                [
                    inner_rows(second_group, both_grad).astype(jnp.bfloat16),
                    inner_rows(grad_group, hidden).astype(jnp.bfloat16),
                ],
                axis=1,
            )
        weight_terms.append(weight_term)

    second_fold = fold_cross(step(fold_core(second_kept, second_sent)))
    second_fold = fold_open(step(second_fold))
    second_fold, weight_terms[-1] = step((second_fold, weight_terms[-1]))
    reduced = [column_scatter(term) for term in weight_terms]
    second_grad = fold_sum(second_fold)
    middle_back, feedforward_gain_grad = norm_back(
        middle, second_inverse, feedforward_gain, second_grad
    )
    middle_grad = cotangent.astype(jnp.float32) + middle_back
    grad_low = middle_grad.astype(jnp.bfloat16)
    grad_chip = to_chip(grad_low)
    first_kept, first_sent = pair_columns(after(first_full, grad_low))
    def moe_rows(rows, *earlier):
        kept = after(hiddens, *earlier)
        return sum(
            times_transposed(piece[rows], weights[1])
            for piece, weights in zip(kept, expert_weights, strict=True)
        )

    moe_sent = moe_rows(slice(rows_all, None), grad_low).astype(jnp.bfloat16)
    grad_chip, first_sent, moe_sent = step((grad_chip, first_sent, moe_sent))
    grad_both = tp_both(grad_low, grad_chip)
    attn_grad_full = tp_join(grad_both, step(to_core(grad_both)))
    moe_received = to_core(after(moe_sent, attn_grad_full))
    heads_grad = matmul(attn_grad_full, full_out).astype(jnp.bfloat16)
    grad_kept, grad_sent = pair_columns(attn_grad_full)
    out_sent = inner_rows(grad_sent, heads_low).astype(jnp.bfloat16)
    heads_grad, out_sent = step((heads_grad, out_sent))
    out_received = to_pair(out_sent)
    projected_grad, query_gain_grad, key_gain_grad = step(
        attend_back(projected, heads_grad, tables, query_count, kv_count, head_size)
    )
    projected_sent = step(inner_rows(first_sent, projected_grad).astype(jnp.bfloat16))
    projected_received = to_pair(projected_sent)
    out_kept = inner_rows(after(grad_kept, projected_sent), heads_low)
    out_received = step(out_received)
    projected_kept = step(inner_rows(first_kept, projected_grad))
    first_split = tp_split(
        times_transposed(after(projected_grad, projected_kept), query_key_value)
    )
    first_halved = tp_halve(step(first_split))
    projected_received = step(projected_received)
    attention_owned = weight_reduce(
        [(projected_kept, projected_received), (out_kept, out_received)]
    )
    owned_parts = [exchange(after(reduced[0], projected_received))]
    first_grad = tp_sum(step(first_halved))
    moe_kept = moe_rows(slice(0, rows_all), projected_kept)
    moe_fold = fold_cross((moe_kept, after(moe_received, projected_received)))
    owned_parts[0] = step(owned_parts[0])
    moe_fold = step(moe_fold)
    owned_parts.append(step(exchange(step(reduced[1]))))
    moe_fold = fold_open(after(moe_fold, owned_parts[1]))
    output = (middle + fold_sum(step(moe_fold))).astype(jnp.bfloat16)

    def owned(index):
        place = slice(index * part_width, (index + 1) * part_width)
        mine = jnp.concatenate([kept[:, place] for kept, sent in owned_parts], axis=1)
        theirs = jnp.concatenate([sent[:, place] for kept, sent in owned_parts], axis=1)
        return (
            jnp.concatenate(
                [
                    jnp.where(pair_bit == 0, mine, theirs),
                    jnp.where(pair_bit == 0, theirs, mine),
                ],
                axis=1,
            )
            .astype(jnp.float32)
            .reshape(weight_rows, expert_count, expert_width)
        )

    rows_back, attention_gain_grad = norm_back(
        token_rows, first_inverse, attention_gain, first_grad
    )
    tokens_grad = middle_grad + rows_back
    gain_sums = sum_all(
        jnp.concatenate(
            [
                attention_gain_grad,
                feedforward_gain_grad,
                query_gain_grad.reshape(head_size),
                key_gain_grad.reshape(head_size),
            ]
        )
    )
    owned_all = [owned(index) for index in range(3)]
    attention_owned = after(attention_owned, gain_sums, output, owned_all).astype(jnp.float32)
    gain_sums = jnp.split(
        gain_sums,
        [model_width, 2 * model_width, 2 * model_width + head_size],
    )
    return (
        output,
        tokens_grad,
        gain_sums[0],
        gain_sums[1],
        gain_sums[2],
        gain_sums[3],
        attention_owned[:, :query_width],
        attention_owned[:, query_width : query_width + key_width],
        attention_owned[:, query_width + key_width : three_width],
        attention_owned[:, three_width:],
        *owned_all,
    )


def solution(mesh):
    placed = (
        P(("fsdp", "tp"), None),
        P(("fsdp", "tp"), None),
        P("fsdp"),
        P("fsdp", None),
        P("fsdp", None),
        P(),
        P(),
        P(),
        P(),
        P("fsdp", "tp"),
        P("fsdp", "tp"),
        P("fsdp", "tp"),
        P("fsdp", "tp"),
        P("fsdp", None, "tp"),
        P("fsdp", None, "tp"),
        P("fsdp", None, "tp"),
    )
    return jax.shard_map(
        partial(per_device, mesh.shape["fsdp"], mesh.shape["tp"]),
        mesh=mesh,
        in_specs=placed,
        out_specs=(
            P(("fsdp", "tp"), None),
            P(("fsdp", "tp"), None),
            P(),
            P(),
            P(),
            P(),
            P("fsdp", "tp"),
            P("fsdp", "tp"),
            P("fsdp", "tp"),
            P("fsdp", "tp"),
            P("fsdp", None, "tp"),
            P("fsdp", None, "tp"),
            P("fsdp", None, "tp"),
        ),
        check_vma=False,
    )
```

```python
from functools import partial

import jax
import jax.numpy as jnp
from jax import lax
from jax.experimental import pallas as pl
from jax.experimental.pallas import tpu as pltpu
from jax.sharding import PartitionSpec as P

SEQ = 1024
TILE = 256
PARTS = 2
VMEM_BYTES = 48 * 1024 * 1024


eps_norm = 1e-06
rope_base = 1000000.0


def matmul(left_side, right_side):
    return jnp.dot(left_side, right_side, preferred_element_type=jnp.float32)


def times_transposed(left_side, right_side):
    return lax.dot_general(
        left_side, right_side, (((1,), (1,)), ((), ())), preferred_element_type=jnp.float32
    )


def inner_rows(left_side, right_side):
    return lax.dot_general(
        left_side, right_side, (((0,), (0,)), ((), ())), preferred_element_type=jnp.float32
    )


def norm_rows(values, scale_gain):
    inverse = lax.rsqrt(jnp.mean(values * values, axis=-1, keepdims=True) + eps_norm)
    return (values * inverse * scale_gain, inverse)


def norm_back(values, inverse, scale_gain, incoming):
    normed = values * inverse
    scaled_grad = incoming * scale_gain
    gain_grad = jnp.sum(incoming * normed, axis=tuple(range(values.ndim - 1)))
    result = inverse * (
        scaled_grad - normed * jnp.mean(scaled_grad * normed, axis=-1, keepdims=True)
    )
    return (result, gain_grad)


def rope_tables(row_count, head_size):
    positions = jnp.arange(row_count, dtype=jnp.float32)
    frequencies = rope_base ** (-jnp.arange(0, head_size, 2, dtype=jnp.float32) / head_size)
    angles = positions[:, None] * frequencies[None, :]
    angles = jnp.concatenate([angles, angles], axis=-1)
    return (jnp.cos(angles), jnp.sin(angles))


def head_norm(values):
    inverse = lax.rsqrt(jnp.mean(values * values, axis=-1, keepdims=True) + eps_norm)
    return (values * inverse, inverse)


def turn(values, cosine, signed_sine):
    half_size = values.shape[-1] // 2
    return values * cosine + pltpu.roll(values, half_size, 1) * signed_sine


def turn_back(incoming, cosine, signed_sine):
    half_size = incoming.shape[-1] // 2
    return incoming * cosine + pltpu.roll(incoming * signed_sine, half_size, 1)


def masked_probs(query_tile, key_rows, row_ids, column_ids, offset, scaling):
    scores = times_transposed(query_tile, key_rows) * scaling
    row_place = lax.broadcasted_iota(jnp.int32, scores.shape, 0) + offset
    column_place = lax.broadcasted_iota(jnp.int32, scores.shape, 1)
    allowed = (column_place <= row_place) & (row_ids == column_ids)
    scores = jnp.where(allowed, scores, -jnp.inf)
    weights = jnp.exp(scores - jnp.max(scores, axis=-1, keepdims=True))
    return weights * (1.0 / jnp.sum(weights, axis=-1, keepdims=True))


def attend_kernel(
    group_size,
    query_ref,
    key_ref,
    value_ref,
    cosine_ref,
    sine_ref,
    row_ids_ref,
    column_ids_ref,
    query_gain_ref,
    key_gain_ref,
    heads_ref,
    key_low,
    value_low,
):
    head_size = query_ref.shape[1]
    scaling = head_size ** (-0.5)

    @pl.when(lax.rem(pl.program_id(1), group_size) == 0)
    def prepare():
        normed, unused = head_norm(key_ref[...])
        key_low[...] = turn(normed * key_gain_ref[...], cosine_ref[...], sine_ref[...]).astype(
            jnp.bfloat16
        )
        value_low[...] = value_ref[...].astype(jnp.bfloat16)

    for offset in range(0, SEQ, TILE):
        finish = offset + TILE
        rows = pl.ds(offset, TILE)
        normed, unused = head_norm(query_ref[rows, :])
        query_tile = turn(
            normed * query_gain_ref[...], cosine_ref[rows, :], sine_ref[rows, :]
        ).astype(jnp.bfloat16)
        probs = masked_probs(
            query_tile,
            key_low[:finish, :],
            row_ids_ref[rows, :],
            column_ids_ref[:, :finish],
            offset,
            scaling,
        )
        heads_ref[rows, :] = matmul(probs.astype(jnp.bfloat16), value_low[:finish, :]).astype(
            jnp.bfloat16
        )


def attend_back_kernel(
    query_count,
    kv_count,
    query_ref,
    key_ref,
    value_ref,
    grad_ref,
    cosine_ref,
    sine_ref,
    row_ids_ref,
    column_ids_ref,
    query_gain_ref,
    key_gain_ref,
    projected_ref,
    query_gain_grad_ref,
    key_gain_grad_ref,
    key_low,
    value_low,
    key_sum,
    value_sum,
):
    head_size = query_ref.shape[1]
    scaling = head_size ** (-0.5)
    group_size = query_count // kv_count
    head = pl.program_id(1)
    place = lax.rem(head, group_size)

    @pl.when((pl.program_id(0) == 0) & (head == 0))
    def clear():
        query_gain_grad_ref[...] = jnp.zeros_like(query_gain_grad_ref)
        key_gain_grad_ref[...] = jnp.zeros_like(key_gain_grad_ref)

    @pl.when(place == 0)
    def prepare():
        normed, unused = head_norm(key_ref[...])
        key_low[...] = turn(normed * key_gain_ref[...], cosine_ref[...], sine_ref[...]).astype(
            jnp.bfloat16
        )
        value_low[...] = value_ref[...].astype(jnp.bfloat16)
        key_sum[...] = jnp.zeros_like(key_sum)
        value_sum[...] = jnp.zeros_like(value_sum)

    def through_norm(turned_grad, cosine, signed_sine, normed, inverse, gain):
        incoming = turn_back(turned_grad, cosine, signed_sine)
        scaled_grad = incoming * gain
        result = inverse * (
            scaled_grad - normed * jnp.mean(scaled_grad * normed, axis=-1, keepdims=True)
        )
        return (result, jnp.sum(incoming * normed, axis=0, keepdims=True))

    columns = pl.ds(pl.multiple_of(head * head_size, head_size), head_size)
    for offset in range(0, SEQ, TILE):
        finish = offset + TILE
        rows = pl.ds(offset, TILE)
        cosine, signed_sine = cosine_ref[rows, :], sine_ref[rows, :]
        normed, inverse = head_norm(query_ref[rows, :])
        query_tile = turn(normed * query_gain_ref[...], cosine, signed_sine).astype(jnp.bfloat16)
        grad_tile = grad_ref[rows, :]
        key_rows = key_low[:finish, :]
        probs = masked_probs(
            query_tile,
            key_rows,
            row_ids_ref[rows, :],
            column_ids_ref[:, :finish],
            offset,
            scaling,
        )
        prob_grad = times_transposed(grad_tile, value_low[:finish, :])
        score_grad = (
            probs * (prob_grad - jnp.sum(probs * prob_grad, axis=-1, keepdims=True))
        ).astype(jnp.bfloat16)
        value_sum[:finish, :] += inner_rows(probs.astype(jnp.bfloat16), grad_tile)
        key_sum[:finish, :] += inner_rows(score_grad, query_tile)
        result, gain_grad = through_norm(
            matmul(score_grad, key_rows) * scaling,
            cosine,
            signed_sine,
            normed,
            inverse,
            query_gain_ref[...],
        )
        projected_ref[rows, columns] = result.astype(jnp.bfloat16)
        query_gain_grad_ref[...] += gain_grad

    @pl.when(place == group_size - 1)
    def finish_group():
        group = lax.div(head, group_size)
        normed, inverse = head_norm(key_ref[...])
        result, gain_grad = through_norm(
            key_sum[...] * scaling,
            cosine_ref[...],
            sine_ref[...],
            normed,
            inverse,
            key_gain_ref[...],
        )
        key_columns = pl.ds(
            pl.multiple_of((query_count + group) * head_size, head_size), head_size
        )
        value_columns = pl.ds(
            pl.multiple_of((query_count + kv_count + group) * head_size, head_size), head_size
        )
        projected_ref[:, key_columns] = result.astype(jnp.bfloat16)
        projected_ref[:, value_columns] = value_sum[...].astype(jnp.bfloat16)
        key_gain_grad_ref[...] += gain_grad


def attention_specs(query_count, kv_count, head_size):
    group_size = query_count // kv_count
    block = (SEQ, head_size)
    fixed = lambda shape: pl.BlockSpec(shape, lambda s, h: (0, 0))
    operands = [
        pl.BlockSpec(block, lambda s, h: (s, h)),
        pl.BlockSpec(block, lambda s, h: (s, query_count + h // group_size)),
        pl.BlockSpec(block, lambda s, h: (s, query_count + kv_count + h // group_size)),
    ]
    tables = [
        fixed(block),
        fixed(block),
        pl.BlockSpec((SEQ, 1), lambda s, h: (s, 0)),
        pl.BlockSpec((1, SEQ), lambda s, h: (0, s)),
        fixed((1, head_size)),
        fixed((1, head_size)),
    ]
    return (operands, tables)


def attend(projected, tables, query_count, kv_count, head_size):
    rows = projected.shape[0]
    operands, table_specs = attention_specs(query_count, kv_count, head_size)
    pairs = rows * SEQ * query_count * 5 // 8
    return pl.pallas_call(
        partial(attend_kernel, query_count // kv_count),
        grid=(rows // SEQ, query_count),
        in_specs=operands + table_specs,
        out_specs=pl.BlockSpec((SEQ, head_size), lambda s, h: (s, h)),
        out_shape=jax.ShapeDtypeStruct((rows, query_count * head_size), jnp.bfloat16),
        scratch_shapes=[
            pltpu.VMEM((SEQ, head_size), jnp.bfloat16),
            pltpu.VMEM((SEQ, head_size), jnp.bfloat16),
        ],
        compiler_params=pltpu.CompilerParams(vmem_limit_bytes=VMEM_BYTES),
        cost_estimate=pl.CostEstimate(
            flops=60 * pairs * head_size,
            bytes_accessed=6 * rows * query_count * head_size,
            transcendentals=pairs,
        ),
        name="attend",
    )(projected, projected, projected, *tables)


def attend_back(projected, heads_grad, tables, query_count, kv_count, head_size):
    rows = projected.shape[0]
    width = projected.shape[1]
    operands, table_specs = attention_specs(query_count, kv_count, head_size)
    pairs = rows * SEQ * query_count * 5 // 8
    return pl.pallas_call(
        partial(attend_back_kernel, query_count, kv_count),
        grid=(rows // SEQ, query_count),
        in_specs=operands + [pl.BlockSpec((SEQ, head_size), lambda s, h: (s, h))] + table_specs,
        out_specs=[
            pl.BlockSpec((SEQ, width), lambda s, h: (s, 0)),
            pl.BlockSpec((1, head_size), lambda s, h: (0, 0)),
            pl.BlockSpec((1, head_size), lambda s, h: (0, 0)),
        ],
        out_shape=[
            jax.ShapeDtypeStruct((rows, width), jnp.bfloat16),
            jax.ShapeDtypeStruct((1, head_size), jnp.float32),
            jax.ShapeDtypeStruct((1, head_size), jnp.float32),
        ],
        scratch_shapes=[
            pltpu.VMEM((SEQ, head_size), jnp.bfloat16),
            pltpu.VMEM((SEQ, head_size), jnp.bfloat16),
            pltpu.VMEM((SEQ, head_size), jnp.float32),
            pltpu.VMEM((SEQ, head_size), jnp.float32),
        ],
        compiler_params=pltpu.CompilerParams(vmem_limit_bytes=VMEM_BYTES),
        cost_estimate=pl.CostEstimate(
            flops=90 * pairs * head_size,
            bytes_accessed=10 * rows * query_count * head_size,
            transcendentals=pairs,
        ),
        name="attend_back",
    )(projected, projected, projected, heads_grad, *tables)


def joined(own, other, bit):
    first_half = jnp.where(bit == 0, own, other)
    last_half = jnp.where(bit == 0, other, own)
    return jnp.concatenate([first_half, last_half], axis=0)


def halves(values, bit):
    rows = values.shape[0] // 2
    kept = lax.dynamic_slice_in_dim(values, bit * rows, rows, 0)
    sent = lax.dynamic_slice_in_dim(values, (1 - bit) * rows, rows, 0)
    return (kept, sent)


def make_moves(fsdp_size, tp_size):
    swap_core = [(i, i ^ 1) for i in range(tp_size)]
    swap_chip = [(i, (i + 2) % tp_size) for i in range(tp_size)]
    swap_pair = [(i, i ^ 1) for i in range(fsdp_size)]
    columns = [list(range(b, fsdp_size, 2)) for b in range(2)]

    def to_core(values):
        return lax.ppermute(values, "tp", swap_core)

    def to_chip(values):
        return lax.ppermute(values, "tp", swap_chip)

    def to_pair(values):
        return lax.ppermute(values, "fsdp", swap_pair)

    def tp_both(own, received):
        return joined(own, received, lax.axis_index("tp") // 2)

    def tp_join(both, others):
        place = lax.axis_index("tp")
        rows, width = both.shape[0] // 2, both.shape[1]
        both = both.reshape(2, 1, rows, width)
        others = others.reshape(2, 1, rows, width)
        first_core = jnp.where(place % 2 == 0, both, others)
        last_core = jnp.where(place % 2 == 0, others, both)
        return jnp.concatenate([first_core, last_core], axis=1).reshape(4 * rows, width)

    def tp_gather(own):
        both = tp_both(own, to_chip(own))
        return tp_join(both, to_core(both))

    def tp_split(full):
        place = lax.axis_index("tp")
        rows, width = full.shape[0] // 4, full.shape[1]
        split = full.reshape(2, 2, rows, width)
        kept = lax.dynamic_index_in_dim(split, place % 2, 1, False)
        sent = lax.dynamic_index_in_dim(split, 1 - place % 2, 1, False).astype(jnp.bfloat16)
        return (kept, to_core(sent))

    def tp_halve(split):
        kept, received = split
        kept, sent = halves(kept + received.astype(jnp.float32), lax.axis_index("tp") // 2)
        return (kept, to_chip(sent.astype(jnp.bfloat16)))

    def tp_sum(halved):
        kept, received = halved
        return (kept + received.astype(jnp.float32)).reshape(kept.shape[1:])

    def tp_scatter(full):
        return tp_sum(tp_halve(tp_split(full)))

    def plane_open(own):
        return (to_chip(own), to_pair(own))

    def plane_cross(opened):
        across, beside = opened
        cut = across.shape[0] // 2
        return (to_chip(beside[:cut]), to_pair(across[cut:]))

    def plane_core(own, opened, crossed):
        mine = jnp.concatenate([own, *opened, *crossed], axis=0)
        return (mine, to_core(mine))

    def plane_join(cored):
        return jnp.concatenate(cored, axis=0)

    def plane_gather(own):
        opened = plane_open(own)
        return plane_join(plane_core(own, opened, plane_cross(opened)))

    def fold_core(kept, sent):
        return (kept, to_core(sent))

    def fold_cross(cored):
        kept, received = cored
        rows = kept.shape[0] // 4
        cut = rows // 2
        far = (kept[3 * rows :] + received[3 * rows :].astype(jnp.float32)).astype(jnp.bfloat16)
        return (kept, received, to_chip(far[:cut]), to_pair(far[cut:]))

    def fold_open(crossed):
        kept, received, from_chip, from_pair = crossed
        rows = kept.shape[0] // 4
        cut = rows // 2
        own, across, beside = [
            kept[i * rows : (i + 1) * rows]
            + received[i * rows : (i + 1) * rows].astype(jnp.float32)
            for i in range(3)
        ]
        across = jnp.concatenate([across[:cut], across[cut:] + from_pair.astype(jnp.float32)])
        beside = jnp.concatenate([beside[:cut] + from_chip.astype(jnp.float32), beside[cut:]])
        return (
            own,
            to_chip(across.astype(jnp.bfloat16)),
            to_pair(beside.astype(jnp.bfloat16)),
        )

    def fold_sum(opened):
        own, from_chip, from_pair = opened
        return own + from_chip.astype(jnp.float32) + from_pair.astype(jnp.float32)

    def plane_share(share):
        place = lax.axis_index("tp")
        rows, count = share.shape[0] // 4, share.shape[1]
        split = share.reshape(2, 2, rows, count)
        split = jnp.where(place // 2 == 0, split, split[::-1])
        split = jnp.where(place % 2 == 0, split, split[:, ::-1]).swapaxes(0, 1)
        return jnp.stack([split, to_pair(split)], axis=1).reshape(8 * rows, count)

    def column_gather(own):
        return lax.all_gather(own, "fsdp", axis=0, tiled=True, axis_index_groups=columns)

    def column_scatter(full):
        return lax.psum_scatter(
            full, "fsdp", scatter_dimension=0, tiled=True, axis_index_groups=columns
        )

    def weight_join(mine, theirs):
        pair_bit = lax.axis_index("fsdp") % 2
        rows, width = mine.shape[0] // (fsdp_size // 2), mine.shape[1]
        mine = mine.reshape(fsdp_size // 2, 1, rows, width)
        theirs = theirs.reshape(fsdp_size // 2, 1, rows, width)
        return jnp.concatenate(
            [jnp.where(pair_bit == 0, mine, theirs), jnp.where(pair_bit == 0, theirs, mine)],
            axis=1,
        ).reshape(fsdp_size * rows, width)

    def column_shift(values):
        pairs = [(i, (i + 2) % fsdp_size) for i in range(fsdp_size)]
        return lax.ppermute(values, "fsdp", pairs)

    def column_place(whole, piece, offset):
        count = fsdp_size // 2
        place = (lax.axis_index("fsdp") // 2 - offset) % count
        return lax.dynamic_update_index_in_dim(whole, piece, place, 0)

    def pair_columns(values):
        pair_bit = lax.axis_index("fsdp") % 2
        width = values.shape[1] // fsdp_size
        return [
            jnp.concatenate(
                [
                    lax.dynamic_slice_in_dim(values, (2 * place + bit) * width, width, 1)
                    for place in range(fsdp_size // 2)
                ],
                axis=1,
            )
            for bit in (pair_bit, 1 - pair_bit)
        ]

    def weight_reduce(pairs):
        summed = [
            (kept + received.astype(jnp.float32)).astype(jnp.bfloat16) for kept, received in pairs
        ]
        return column_scatter(jnp.concatenate(summed, axis=1))

    def sum_all(values):
        for step in range(tp_size.bit_length() - 1):
            swap = [(i, i ^ (1 << step)) for i in range(tp_size)]
            values = values + lax.ppermute(values, "tp", swap)
        for step in range(fsdp_size.bit_length() - 1):
            swap = [(i, i ^ (1 << step)) for i in range(fsdp_size)]
            values = values + lax.ppermute(values, "fsdp", swap)
        return values

    return (
        to_pair,
        to_core,
        to_chip,
        tp_both,
        tp_join,
        tp_gather,
        tp_split,
        tp_halve,
        tp_sum,
        tp_scatter,
        plane_open,
        plane_cross,
        plane_core,
        plane_join,
        fold_core,
        fold_cross,
        fold_open,
        fold_sum,
        plane_share,
        column_gather,
        column_scatter,
        weight_join,
        column_shift,
        column_place,
        pair_columns,
        weight_reduce,
        sum_all,
    )


def per_device(
    fsdp_size,
    tp_size,
    tokens,
    cotangent,
    segments,
    routes,
    gate_logits,
    attention_gain,
    feedforward_gain,
    query_gain,
    key_gain,
    query_weight,
    key_weight,
    value_weight,
    out_weight,
    gate_weight,
    up_weight,
    down_weight,
):
    (
        to_pair,
        to_core,
        to_chip,
        tp_both,
        tp_join,
        tp_gather,
        tp_split,
        tp_halve,
        tp_sum,
        tp_scatter,
        plane_open,
        plane_cross,
        plane_core,
        plane_join,
        fold_core,
        fold_cross,
        fold_open,
        fold_sum,
        plane_share,
        column_gather,
        column_scatter,
        weight_join,
        column_shift,
        column_place,
        pair_columns,
        weight_reduce,
        sum_all,
    ) = make_moves(fsdp_size, tp_size)
    pair_bit = lax.axis_index("fsdp") % 2
    head_size = query_gain.shape[0]
    kv_count = key_weight.shape[1] // head_size
    query_count = query_weight.shape[1] // head_size
    weight_rows, expert_count, expert_width = gate_weight.shape
    half_experts = expert_count // 2
    half_width = half_experts * expert_width
    part_width = half_width // PARTS
    rows_all = segments.shape[0]
    cosine, sine_table = rope_tables(SEQ, head_size)
    turn_sign = jnp.where(jnp.arange(head_size) < head_size // 2, -1.0, 1.0)
    tables = (
        cosine,
        sine_table * turn_sign,
        segments.reshape(rows_all, 1),
        segments.reshape(1, rows_all),
        query_gain.reshape(1, head_size),
        key_gain.reshape(1, head_size),
    )
    token_rows = tokens.astype(jnp.float32)
    first_norm, first_inverse = norm_rows(token_rows, attention_gain)
    last = []

    def step(value):
        if last:
            value = lax.optimization_barrier((value, last[0]))[0]
        last[:] = [value]
        return value

    def after(value, *earlier):
        return lax.optimization_barrier((value, earlier))[0]

    def exchange(reduced):
        kept, sent = halves(reduced, pair_bit)
        return (kept, to_pair(sent))

    gate_probs = jax.nn.softmax(gate_logits, axis=-1)
    expert_ids = jnp.arange(expert_count, dtype=jnp.int32)
    share_own = jnp.sum(
        jnp.where(routes[:, :, None] == expert_ids[None, None, :], gate_probs[:, :, None], 0.0),
        axis=1,
    )
    share_group = plane_share(share_own)
    share_half = lax.dynamic_slice_in_dim(share_group, pair_bit * half_experts, half_experts, 1)
    span = half_experts // PARTS
    share_wide = [
        jnp.repeat(share_half[:, part * span : (part + 1) * span], expert_width, axis=1)
        for part in range(PARTS)
    ]
    query_width = query_count * head_size
    key_width = kv_count * head_size
    model_width = tokens.shape[1]
    three_width = query_width + 2 * key_width
    column_count = fsdp_size // 2
    three_own = jnp.concatenate([query_weight, key_weight, value_weight], axis=1)

    def flat(weight):
        return weight.reshape(weight_rows, 2, PARTS, part_width)

    flats = (flat(gate_weight), flat(up_weight), flat(down_weight))

    def side(part, bit):
        return jnp.concatenate(
            [lax.dynamic_index_in_dim(w[:, :, part], bit, 1, False) for w in flats], axis=1
        )

    def fetched(part, received):
        whole = joined(side(part, pair_bit), received, pair_bit)
        if part == 0:
            whole = column_gather(whole)
            return [whole[:, : 2 * part_width], whole[:, 2 * part_width :]]
        return [
            column_gather(whole[:, : 2 * part_width]),
            column_gather(whole[:, 2 * part_width :]),
        ]

    def start_whole(own, beside):
        shape = (column_count, fsdp_size // column_count * weight_rows, own.shape[1])
        whole = jnp.zeros(shape, own.dtype)
        return column_place(whole, joined(own, beside, pair_bit), 0)

    first_low = first_norm.astype(jnp.bfloat16)
    first_chip = to_chip(first_low)
    out_mine = column_gather(out_weight)
    swapped = to_pair(after(side(0, 1 - pair_bit), share_group))
    three_pieces = [three_own, column_shift(three_own)]
    three_pieces[-1] = step(three_pieces[-1])
    three_pieces.append(column_shift(three_pieces[-1]))
    first_both = tp_both(first_low, step(first_chip))
    first_core = to_core(first_both)
    swapped = step(swapped)
    three_besides = [to_pair(after(three_own, swapped)), to_pair(after(three_pieces[1], swapped))]
    for offset in range(2, column_count):
        three_pieces[offset] = step(three_pieces[offset])
        three_besides.append(to_pair(three_pieces[offset]))
        if offset + 1 < column_count:
            three_pieces.append(column_shift(three_pieces[offset]))
    expert_weights = [fetched(0, swapped)]
    first_full = tp_join(first_both, step(first_core))
    share_wide = step(share_wide)
    three_whole = start_whole(three_own, step(three_besides[0]))
    out_mine = step(out_mine)
    for offset in range(1, column_count):
        three_besides[offset] = step(three_besides[offset])
        three_whole = column_place(
            three_whole, joined(three_pieces[offset], three_besides[offset], pair_bit), offset
        )
    out_theirs = to_pair(after(out_mine, three_besides[-1]))
    query_key_value = three_whole.reshape(fsdp_size * weight_rows, three_width)
    projected = matmul(first_full, query_key_value)
    heads_low = step(attend(projected, tables, query_count, kv_count, head_size))
    out_theirs = step(out_theirs)
    cotangent_open = plane_open(after(cotangent, out_theirs))
    full_out = weight_join(out_mine, out_theirs)
    attn_split = step(tp_split(times_transposed(heads_low, full_out)))
    received = to_pair(after(side(1, 1 - pair_bit), out_theirs))
    attn_halved = step(tp_halve(attn_split))
    middle = token_rows + tp_sum(attn_halved)
    second_norm, second_inverse = norm_rows(middle, feedforward_gain)
    second_low = second_norm.astype(jnp.bfloat16)
    second_open = plane_open(second_low)
    for part in range(1, PARTS):
        received = step(received)
        expert_weights.append(fetched(part, received))
        if part + 1 < PARTS:
            received = to_pair(after(side(part + 1, 1 - pair_bit), received))
    second_open = step(second_open)
    second_cross = plane_cross(second_open)
    cotangent_open = step(cotangent_open)
    second_cross = step(second_cross)
    second_core = plane_core(second_low, second_open, second_cross)
    cotangent_cross = plane_cross(after(cotangent_open, second_cross))
    expert_weights[0][0] = step(expert_weights[0][0])
    second_group = plane_join(step(second_core))
    cotangent_core = plane_core(cotangent, cotangent_open, step(cotangent_cross))
    grad_group = plane_join(step(cotangent_core))
    weight_terms = []
    hiddens = []
    for part in range(PARTS):
        weight_in, weight_down = expert_weights[part]
        share = share_wide[part]
        both_pre = matmul(second_group, weight_in)
        gate_pre, up_pre = both_pre[:, :part_width], both_pre[:, part_width:]
        sigmoid_gate = jax.nn.sigmoid(gate_pre)
        silu_gate = gate_pre * sigmoid_gate
        hidden = (silu_gate * up_pre * share).astype(jnp.bfloat16)
        hidden_grad = matmul(grad_group, weight_down) * share
        up_grad = (hidden_grad * silu_gate).astype(jnp.bfloat16)
        gate_grad = (
            hidden_grad * up_pre * sigmoid_gate * (1.0 + gate_pre * (1.0 - sigmoid_gate))
        ).astype(jnp.bfloat16)
        both_grad = jnp.concatenate([gate_grad, up_grad], axis=1)
        if part < PARTS - 1:
            down_term = step(inner_rows(grad_group, hidden).astype(jnp.bfloat16))
            expert_weights[part + 1][0] = step(expert_weights[part + 1][0])
            both_late = after(both_grad, down_term)
            weight_term = jnp.concatenate(
                [inner_rows(second_group, both_late).astype(jnp.bfloat16), down_term], axis=1
            )
            both_late = after(both_grad, weight_term)
            second_part = times_transposed(both_late, weight_in)
            hiddens.append(hidden)
            expert_weights[part + 1][1] = step(expert_weights[part + 1][1])
            second_sum = second_part if part == 0 else second_sum + second_part
            second_sum = step(second_sum)
        else:
            second_sent = second_sum[rows_all:] + times_transposed(
                both_grad[rows_all:], weight_in
            )
            second_sent = step(second_sent.astype(jnp.bfloat16))
            second_kept = second_sum[:rows_all] + times_transposed(
                after(both_grad, second_sent)[:rows_all], weight_in
            )
            hidden, both_grad = after((hidden, both_grad), second_kept)
            hiddens.append(hidden)
            weight_term = jnp.concatenate(
                [
                    inner_rows(second_group, both_grad).astype(jnp.bfloat16),
                    inner_rows(grad_group, hidden).astype(jnp.bfloat16),
                ],
                axis=1,
            )
        weight_terms.append(weight_term)

    second_fold = fold_cross(step(fold_core(second_kept, second_sent)))
    second_fold = fold_open(step(second_fold))
    second_fold, weight_terms[-1] = step((second_fold, weight_terms[-1]))
    reduced = [column_scatter(term) for term in weight_terms]
    second_grad = fold_sum(second_fold)
    middle_back, feedforward_gain_grad = norm_back(
        middle, second_inverse, feedforward_gain, second_grad
    )
    middle_grad = cotangent.astype(jnp.float32) + middle_back
    grad_low = middle_grad.astype(jnp.bfloat16)
    grad_chip = to_chip(grad_low)
    first_kept, first_sent = pair_columns(after(first_full, grad_low))
    def moe_rows(rows, *earlier):
        kept = after(hiddens, *earlier)
        return sum(
            times_transposed(piece[rows], weights[1])
            for piece, weights in zip(kept, expert_weights, strict=True)
        )

    moe_sent = moe_rows(slice(rows_all, None), grad_low).astype(jnp.bfloat16)
    grad_chip, first_sent, moe_sent = step((grad_chip, first_sent, moe_sent))
    grad_both = tp_both(grad_low, grad_chip)
    attn_grad_full = tp_join(grad_both, step(to_core(grad_both)))
    moe_received = to_core(after(moe_sent, attn_grad_full))
    heads_grad = matmul(attn_grad_full, full_out).astype(jnp.bfloat16)
    grad_kept, grad_sent = pair_columns(attn_grad_full)
    out_sent = inner_rows(grad_sent, heads_low).astype(jnp.bfloat16)
    heads_grad, out_sent = step((heads_grad, out_sent))
    out_received = to_pair(out_sent)
    projected_grad, query_gain_grad, key_gain_grad = step(
        attend_back(projected, heads_grad, tables, query_count, kv_count, head_size)
    )
    owned_parts = [exchange(after(reduced[0], heads_grad))]
    projected_sent = step(inner_rows(first_sent, projected_grad).astype(jnp.bfloat16))
    projected_received = to_pair(projected_sent)
    out_kept = inner_rows(after(grad_kept, projected_sent), heads_low)
    out_received = step(out_received)
    projected_kept = step(inner_rows(first_kept, projected_grad))
    first_split = tp_split(
        times_transposed(after(projected_grad, projected_kept), query_key_value)
    )
    first_halved = tp_halve(step(first_split))
    owned_parts[0] = step(owned_parts[0])
    projected_received = step(projected_received)
    attention_owned = weight_reduce(
        [(projected_kept, projected_received), (out_kept, out_received)]
    )
    first_grad = tp_sum(step(first_halved))
    moe_kept = moe_rows(slice(0, rows_all), projected_kept)
    moe_fold = fold_cross((moe_kept, after(moe_received, projected_received)))
    moe_fold = step(moe_fold)
    owned_parts.append(step(exchange(step(reduced[1]))))
    moe_fold = fold_open(after(moe_fold, owned_parts[1]))
    output = (middle + fold_sum(step(moe_fold))).astype(jnp.bfloat16)

    def owned(index):
        place = slice(index * part_width, (index + 1) * part_width)
        mine = jnp.concatenate([kept[:, place] for kept, sent in owned_parts], axis=1)
        theirs = jnp.concatenate([sent[:, place] for kept, sent in owned_parts], axis=1)
        return (
            jnp.concatenate(
                [
                    jnp.where(pair_bit == 0, mine, theirs),
                    jnp.where(pair_bit == 0, theirs, mine),
                ],
                axis=1,
            )
            .astype(jnp.float32)
            .reshape(weight_rows, expert_count, expert_width)
        )

    rows_back, attention_gain_grad = norm_back(
        token_rows, first_inverse, attention_gain, first_grad
    )
    tokens_grad = middle_grad + rows_back
    gain_sums = sum_all(
        jnp.concatenate(
            [
                attention_gain_grad,
                feedforward_gain_grad,
                query_gain_grad.reshape(head_size),
                key_gain_grad.reshape(head_size),
            ]
        )
    )
    owned_all = [owned(index) for index in range(3)]
    attention_owned = after(attention_owned, gain_sums, output, owned_all).astype(jnp.float32)
    gain_sums = jnp.split(
        gain_sums,
        [model_width, 2 * model_width, 2 * model_width + head_size],
    )
    return (
        output,
        tokens_grad,
        gain_sums[0],
        gain_sums[1],
        gain_sums[2],
        gain_sums[3],
        attention_owned[:, :query_width],
        attention_owned[:, query_width : query_width + key_width],
        attention_owned[:, query_width + key_width : three_width],
        attention_owned[:, three_width:],
        *owned_all,
    )


def solution(mesh):
    placed = (
        P(("fsdp", "tp"), None),
        P(("fsdp", "tp"), None),
        P("fsdp"),
        P("fsdp", None),
        P("fsdp", None),
        P(),
        P(),
        P(),
        P(),
        P("fsdp", "tp"),
        P("fsdp", "tp"),
        P("fsdp", "tp"),
        P("fsdp", "tp"),
        P("fsdp", None, "tp"),
        P("fsdp", None, "tp"),
        P("fsdp", None, "tp"),
    )
    return jax.shard_map(
        partial(per_device, mesh.shape["fsdp"], mesh.shape["tp"]),
        mesh=mesh,
        in_specs=placed,
        out_specs=(
            P(("fsdp", "tp"), None),
            P(("fsdp", "tp"), None),
            P(),
            P(),
            P(),
            P(),
            P("fsdp", "tp"),
            P("fsdp", "tp"),
            P("fsdp", "tp"),
            P("fsdp", "tp"),
            P("fsdp", None, "tp"),
            P("fsdp", None, "tp"),
            P("fsdp", None, "tp"),
        ),
        check_vma=False,
    )
```
